32 devices in a mesh: seq: 8 (over z, x), chan: 4 (over y, core).
Axes of the slice: x: 2, y: 2, z: 4, core: 2. Of those that a mesh axis runs over, the one named last changes fastest.
Arguments:
- query_rows: bfloat16 [2048, 2048], P('seq', 'chan'), may hold values from -6 to 6
- key_rows: bfloat16 [2048, 2048], P('seq', 'chan'), may hold values from -6 to 6
- value_rows: bfloat16 [2048, 2048], P('seq', 'chan'), may hold values from -6 to 6
- long_filter: float32 [2048, 2048], P('seq', 'chan'), may hold values from -2 to 2
- short_taps: float32 [3, 3, 2048], P(None, None, ('seq', 'chan')), may hold values from -3 to 3
- skip_gain: float32 [2048], P(('seq', 'chan')), may hold values from -3 to 3
- cotangent: bfloat16 [2048, 2048], P('seq', 'chan'), may hold values from -6 to 6
Outputs:
- gated_out: bfloat16 [2048, 2048], P('seq', 'chan')
- query_grad: bfloat16 [2048, 2048], P('seq', 'chan')
- key_grad: bfloat16 [2048, 2048], P('seq', 'chan')
- value_grad: bfloat16 [2048, 2048], P('seq', 'chan')
- filter_grad: float32 [2048, 2048], P('seq', 'chan')
- taps_grad: float32 [3, 3, 2048], P(None, None, 'chan')
- skip_grad: float32 [2048], P('chan')
The draws below stay inside these ranges and needn't reach their ends.
All inputs are finite; a program needn't handle non-finite values.
Results may differ from the reference program's by a relative error of at most 0.00135.
Values may be sent and summed in bfloat16 or wider, within the bound.
No kernel may reach another device: no remote copies, remote signals or barrier semaphores. Data moves between devices by JAX's collectives and lax.ppermute only.
A program may use at most 64 MiB of HBM per device.

```python
import math
import jax
import jax.numpy as jnp

C = 2048
SEQ = 2048


def draw_long_filter(key, part):
    key_rate, key_noise = jax.random.split(jax.random.fold_in(key, 7), 2)
    position = jnp.arange(SEQ, dtype=jnp.float32)[:, None]
    low_rate = math.log(30.0)
    high_rate = math.log(SEQ * 4.0)
    horizon = jnp.exp(jax.random.uniform(key_rate, (1, C), jnp.float32, low_rate, high_rate))
    envelope = jnp.exp(-position / horizon)
    scaling = 1.0 / jnp.sqrt(0.5 * horizon * (1.0 - jnp.exp(-2.0 * SEQ / horizon)) + 1.0)
    rough = jax.random.truncated_normal(key_noise, -4.0, 4.0, (SEQ, C), jnp.float32)
    return rough * envelope * scaling


def levels(rng, shape, shards, low, high):
    factor_of = 1.0
    for axis_at, shards_of in shards:
        heights = jax.random.uniform(jax.random.fold_in(jax.random.fold_in(rng, 6), axis_at), (shards_of,), jnp.float32, low / len(shards), high / len(shards))
        factor_of = factor_of * jnp.repeat(jnp.exp(heights), shape[axis_at] // shards_of).reshape((-1,) + (1,) * (len(shape) - 1 - axis_at))
    return factor_of


def centred(stream_key, shape, spread, reach, shards=(), held_as=jnp.bfloat16):
    drawn = spread * jax.random.normal(stream_key, shape, jnp.float32)
    if shards:
        drawn = drawn * levels(stream_key, shape, shards, -0.22, 0.18)
    return jnp.clip(drawn, -reach, reach).astype(held_as)


def setup_inputs(seed: int = 0) -> dict:
    streams_of = jax.random.split(jax.random.key(seed), 8)
    query_rows = centred(streams_of[0], (SEQ, C), 1.0, 6.0, ((0, 8), (1, 4)))
    key_rows = centred(streams_of[1], (SEQ, C), 1.0, 6.0, ((0, 8), (1, 4)))
    value_rows = centred(streams_of[2], (SEQ, C), 1.0, 6.0, ((0, 8), (1, 4)))
    long_filter = draw_long_filter(jax.random.fold_in(streams_of[7], 71), 0)
    short_taps = centred(streams_of[4], (3, 3, C), 0.6, 3.0, ((2, 32),), jnp.float32)
    skip_gain = centred(streams_of[5], (C,), 0.7, 3.0, ((0, 32),), jnp.float32)
    cotangent = centred(streams_of[6], (SEQ, C), 1.0, 6.0, ((0, 8), (1, 4)))
    return dict(query_rows=query_rows, key_rows=key_rows, value_rows=value_rows, long_filter=long_filter, short_taps=short_taps, skip_gain=skip_gain, cotangent=cotangent)


def delay(signal, steps):
    if steps == 0:
        return signal
    zeros_block = jnp.zeros((steps,) + signal.shape[1:], signal.dtype)
    return jnp.concatenate([zeros_block, signal[:-steps]], axis=0)


def advance(signal, steps):
    if steps == 0:
        return signal
    zeros_block = jnp.zeros((steps,) + signal.shape[1:], signal.dtype)
    return jnp.concatenate([signal[steps:], zeros_block], axis=0)


def reference(query_rows, key_rows, value_rows, long_filter, short_taps, skip_gain, cotangent):
    length = query_rows.shape[0]
    points = 2 * length
    grad_scale = length ** -0.5
    inputs = [query_rows.astype(jnp.float32), key_rows.astype(jnp.float32), value_rows.astype(jnp.float32)]
    convs = []
    for stream in range(3):
        total = short_taps[stream, 0] * inputs[stream]
        for offset in range(1, 3):
            total = total + short_taps[stream, offset] * delay(inputs[stream], offset)
        convs.append(total)
    query_conv, key_conv, value_conv = convs
    product = key_conv * value_conv
    prod_spec = jnp.fft.rfft(product, n=points, axis=0)
    filt_spec = jnp.fft.rfft(long_filter, n=points, axis=0)
    mixed_conv = jnp.fft.irfft(prod_spec * filt_spec, n=points, axis=0)[:length] + skip_gain * product
    gated_out = (query_conv * mixed_conv).astype(jnp.bfloat16)
    upstream = cotangent.astype(jnp.float32)
    gated_grad = upstream * query_conv
    query_conv_grad = upstream * mixed_conv
    grad_spec = jnp.fft.rfft(gated_grad, n=points, axis=0)
    product_grad = jnp.fft.irfft(grad_spec * jnp.conj(filt_spec), n=points, axis=0)[:length] + skip_gain * gated_grad
    filter_grad = grad_scale * jnp.fft.irfft(grad_spec * jnp.conj(prod_spec), n=points, axis=0)[:length]
    skip_grad = grad_scale * jnp.sum(gated_grad * product, axis=0)
    key_conv_grad = product_grad * value_conv
    value_conv_grad = product_grad * key_conv
    conv_grads = [query_conv_grad, key_conv_grad, value_conv_grad]
    input_grads = []
    tap_rows = []
    for stream in range(3):
        total = short_taps[stream, 0] * conv_grads[stream]
        for offset in range(1, 3):
            total = total + short_taps[stream, offset] * advance(conv_grads[stream], offset)
        input_grads.append(total.astype(jnp.bfloat16))
        tap_rows.append(jnp.stack([grad_scale * jnp.sum(conv_grads[stream] * delay(inputs[stream], offset), axis=0) for offset in range(3)]))
    taps_grad = jnp.stack(tap_rows)
    return (gated_out, input_grads[0], input_grads[1], input_grads[2], filter_grad, taps_grad, skip_grad)
```

```python
import math

import jax
import jax.numpy as jnp
import numpy as np
from jax import lax
from jax.experimental import pallas as pl
from jax.experimental.pallas import tpu as pltpu
from jax.sharding import PartitionSpec as P

HALF = 64
LANES = 2 * HALF
SUMS = 16
VMEM_BYTES = 62 * 1024 * 1024


def swap(value):
    return pltpu.roll(value, HALF, 1)


def left_lanes(shape):
    return lax.broadcasted_iota(jnp.int32, shape, 1) < HALF


def head_tail(value):
    head = value.astype(jnp.bfloat16)
    tail = (value - head.astype(jnp.float32)).astype(jnp.bfloat16)
    return head, tail


def transform_matrices(rows):
    freq = np.concatenate([np.arange(0, rows, 2), np.arange(1, rows, 2)])
    turn = (2 * freq[:, None] + 1) * np.arange(rows)[None, :] % (4 * rows)
    theta = turn * (math.pi / (2 * rows))
    forward = np.concatenate([np.cos(theta), -np.sin(theta)])
    inverse = forward.T / rows

    def split(matrix):
        single = matrix.astype(np.float32)
        head = single.astype(jnp.bfloat16)
        tail = (single - head.astype(np.float32)).astype(jnp.bfloat16)
        return np.concatenate([head, head, tail], axis=1)

    return split(forward), split(inverse)


def pack_kernel(query_ref, key_ref, value_ref, cot_ref, filter_ref, out_ref):
    rows, channels = query_ref.shape
    left = left_lanes((rows, LANES))
    for tile in range(channels // LANES):
        at = pl.ds(tile * LANES, LANES)
        for first, second, place in ((query_ref, key_ref, 0), (cot_ref, value_ref, 1)):
            one = first[:, at].astype(jnp.float32)
            two = second[:, at].astype(jnp.float32)
            here = pl.ds(place * rows, rows)
            out_ref[2 * tile, here, :] = jnp.where(left, one, swap(two)).astype(jnp.bfloat16)
            out_ref[2 * tile + 1, here, :] = jnp.where(left, swap(one), two).astype(jnp.bfloat16)
        head, tail = head_tail(filter_ref[:, at])
        head, tail = head.astype(jnp.float32), tail.astype(jnp.float32)
        here = pl.ds(2 * rows, rows)
        out_ref[2 * tile, here, :] = jnp.where(left, head, swap(tail)).astype(jnp.bfloat16)
        out_ref[2 * tile + 1, here, :] = jnp.where(left, swap(head), tail).astype(jnp.bfloat16)


def pack(query_rows, key_rows, value_rows, cotangent, long_filter, devices):
    rows, channels = query_rows.shape
    if channels == devices * HALF:
        return pl.pallas_call(
            pack_kernel,
            out_shape=jax.ShapeDtypeStruct((devices, 3 * rows, LANES), jnp.bfloat16),
            compiler_params=pltpu.CompilerParams(vmem_limit_bytes=VMEM_BYTES),
        )(query_rows, key_rows, value_rows, cotangent, long_filter)
    head, tail = head_tail(long_filter)
    share = channels // devices

    def lay(value):
        pieces = value.reshape(rows, devices, share).transpose(1, 0, 2)
        return jnp.pad(pieces, ((0, 0), (0, 0), (0, HALF - share)))

    pairs = ((query_rows, key_rows), (cotangent, value_rows), (head, tail))
    return jnp.concatenate([jnp.concatenate([lay(a), lay(b)], axis=2) for a, b in pairs], axis=1)


def unpack_kernel(in_ref, gated_ref, query_ref, key_ref, value_ref, filter_ref, sums_ref):
    rows, channels = gated_ref.shape
    left = left_lanes((rows, LANES))
    left_sums = left_lanes((SUMS // 2, LANES))
    for tile in range(channels // LANES):
        at = pl.ds(tile * LANES, LANES)
        for first, second, place in ((query_ref, key_ref, 0), (gated_ref, value_ref, 1)):
            here = pl.ds(place * rows, rows)
            one = in_ref[2 * tile, here, :].astype(jnp.float32)
            two = in_ref[2 * tile + 1, here, :].astype(jnp.float32)
            first[:, at] = jnp.where(left, one, swap(two)).astype(jnp.bfloat16)
            second[:, at] = jnp.where(left, swap(one), two).astype(jnp.bfloat16)
        here = pl.ds(2 * rows, rows)
        one = in_ref[2 * tile, here, :].astype(jnp.float32)
        two = in_ref[2 * tile + 1, here, :].astype(jnp.float32)
        filter_ref[:, at] = jnp.where(left, one + swap(one), two + swap(two))
        sums = []
        for source in (2 * tile, 2 * tile + 1):
            pair = in_ref[source, pl.ds(3 * rows, SUMS), :].astype(jnp.float32)
            sums.append(pair[: SUMS // 2] + pair[SUMS // 2 :])
        sums_ref[0, :, at] = jnp.where(left_sums, sums[0], swap(sums[1]))
        sums_ref[1, :, at] = jnp.where(left_sums, swap(sums[0]), sums[1])


def unpack(received, rows, channels):
    devices = received.shape[0]
    low = jax.ShapeDtypeStruct((rows, channels), jnp.bfloat16)
    if channels == devices * HALF:
        return pl.pallas_call(
            unpack_kernel,
            out_shape=(
                low,
                low,
                low,
                low,
                jax.ShapeDtypeStruct((rows, channels), jnp.float32),
                jax.ShapeDtypeStruct((2, SUMS // 2, channels), jnp.float32),
            ),
            compiler_params=pltpu.CompilerParams(vmem_limit_bytes=VMEM_BYTES),
        )(received)
    share = channels // devices

    def lay(start, count, side):
        piece = received[:, start : start + count, side * HALF : side * HALF + share]
        return piece.transpose(1, 0, 2).reshape(count, channels)

    def whole(start, count, side):
        return lay(start, count, side).astype(jnp.float32)

    sums = [
        whole(3 * rows, SUMS // 2, side) + whole(3 * rows + SUMS // 2, SUMS // 2, side)
        for side in (0, 1)
    ]
    return (
        lay(rows, rows, 0),
        lay(0, rows, 0),
        lay(0, rows, 1),
        lay(rows, rows, 1),
        whole(2 * rows, rows, 0) + whole(2 * rows, rows, 1),
        jnp.stack(sums),
    )


def operator_kernel(
    forward_ref, inverse_ref, taps_ref, in_ref, out_ref,
    behind, ahead, first_ref, second_ref, fields, spectra, filters, rhs, rhs_back, sums_ref,
):
    blocks = in_ref.shape[0]
    rows = in_ref.shape[1] // 3
    half = blocks // 2
    grad_scale = 1.0 / math.sqrt(blocks * rows)
    left = left_lanes((rows, LANES))
    taps = taps_ref[...]
    query_taps = [taps[i : i + 1] for i in range(3)]
    value_taps = [taps[3 + i : 4 + i] for i in range(3)]
    gain = taps[6:7]

    def short(block, carry):
        outs, ends = [], []
        for place, weights, before in ((0, query_taps, carry[0]), (1, value_taps, carry[1])):
            now = in_ref[block, pl.ds(place * rows, rows), :].astype(jnp.float32)
            behind[place, pl.ds(0, 8), :] = before
            behind[place, pl.ds(8, rows), :] = now
            total = weights[0] * now
            for offset in (1, 2):
                total = total + weights[offset] * behind[place, pl.ds(8 - offset, rows), :]
            outs.append(total)
            ends.append(now[rows - 8 :])
        first_ref[block] = outs[0]
        second_ref[block] = outs[1]
        fields[block] = outs[0] * outs[1]
        return tuple(ends)

    nothing = jnp.zeros((8, LANES), jnp.float32)
    lax.fori_loop(0, blocks, short, (nothing, nothing))

    def transform(pair, _):
        for side in range(2):
            block = 2 * pair + side
            field = jnp.where(left, fields[blocks - 1 - block], fields[block])
            head, tail = head_tail(field)
            at = pl.ds(side * LANES, LANES)
            rhs[pl.ds(0, rows), at] = head
            rhs[pl.ds(rows, rows), at] = tail
            rhs[pl.ds(2 * rows, rows), at] = head
        result = jnp.dot(forward_ref[...], rhs[...], preferred_element_type=jnp.float32)
        for side in range(2):
            spectra[2 * pair + side] = result[:, side * LANES : (side + 1) * LANES]
        for side in range(2):
            both = in_ref[2 * pair + side, pl.ds(2 * rows, rows), :]
            wide = both.astype(jnp.float32)
            turned = swap(wide)
            at = pl.ds(side * LANES, LANES)
            rhs[pl.ds(0, rows), at] = both
            rhs[pl.ds(rows, rows), at] = turned.astype(jnp.bfloat16)
            rhs[pl.ds(2 * rows, rows), at] = jnp.where(left, wide, turned).astype(jnp.bfloat16)
        result = jnp.dot(forward_ref[...], rhs[...], preferred_element_type=jnp.float32)
        for side in range(2):
            filters[2 * pair + side] = result[:, side * LANES : (side + 1) * LANES]
        return 0

    lax.fori_loop(0, half, transform, 0)

    chunk = 8
    left_chunk = left_lanes((chunk, LANES))
    conjugate = jnp.where(left_chunk, -1.0, 1.0)

    def spectral(step, sign):
        real_at = pl.ds(pl.multiple_of(step * chunk, chunk), chunk)
        imag_at = pl.ds(pl.multiple_of(rows + step * chunk, chunk), chunk)
        field_re = [spectra[block, real_at, :] for block in range(blocks)]
        field_im = [spectra[block, imag_at, :] for block in range(blocks)]

        def joined(re, im, block):
            if block == 0:
                return re[0], im[0]
            if sign > 0:
                return re[block] - im[block - 1], im[block] + re[block - 1]
            return re[block] + im[block - 1], im[block] - re[block - 1]

        filt_re = [filters[block, real_at, :] for block in range(blocks)]
        filt_im = [filters[block, imag_at, :] for block in range(blocks)]
        joins = [joined(filt_re, filt_im, block) for block in range(blocks)]
        joins = [(re, im * conjugate) for re, im in joins]
        for block in range(blocks):
            out_re = out_im = None
            for lag in range(block + 1):
                re, im = field_re[block - lag], field_im[block - lag]
                join_re, join_im = joins[lag]
                term_re = re * join_re - im * join_im
                term_im = re * join_im + im * join_re
                out_re = term_re if out_re is None else out_re + term_re
                out_im = term_im if out_im is None else out_im + term_im
            spectra[block, real_at, :] = out_re
            spectra[block, imag_at, :] = out_im
        grads = []
        for block in range(blocks):
            re, im = field_re[blocks - 1 - block], field_im[blocks - 1 - block]
            grads.append(
                (jnp.where(left_chunk, re, swap(re)), jnp.where(left_chunk, im, swap(im)))
            )
        joins = [joined(field_re, field_im, block) for block in range(blocks)]
        products = []
        for block in range(blocks):
            parts = []
            for part in range(2):
                far = joins[block - half][part] if block >= half else 0.0
                parts.append(jnp.where(left_chunk, swap(joins[block][part]), far))
            products.append(parts)
        for lag in range(half):
            out_re = out_im = None
            for block in range(lag, blocks):
                re, im = grads[block]
                join_re, join_im = products[block - lag]
                term_re = re * join_re + im * join_im
                term_im = im * join_re - re * join_im
                out_re = term_re if out_re is None else out_re + term_re
                out_im = term_im if out_im is None else out_im + term_im
            filters[lag, real_at, :] = out_re
            filters[lag, imag_at, :] = out_im

    def even(step, _):
        spectral(step, 1)
        return 0

    def odd(step, _):
        spectral(step, -1)
        return 0

    steps = rows // chunk
    lax.fori_loop(0, steps // 2, even, 0)
    lax.fori_loop(steps // 2, steps, odd, 0)

    def back(source, pair):
        for side in range(2):
            head, tail = head_tail(source[2 * pair + side])
            at = pl.ds(side * LANES, LANES)
            rhs_back[pl.ds(0, 2 * rows), at] = head
            rhs_back[pl.ds(2 * rows, 2 * rows), at] = tail
            rhs_back[pl.ds(4 * rows, 2 * rows), at] = head
        return jnp.dot(inverse_ref[...], rhs_back[...], preferred_element_type=jnp.float32)

    def mixed(pair, _):
        result = back(spectra, pair)
        for side in range(2):
            spectra[2 * pair + side, pl.ds(0, rows), :] = result[
                :, side * LANES : (side + 1) * LANES
            ]
        return 0

    lax.fori_loop(0, half, mixed, 0)

    def filter_grads(pair, _):
        result = back(filters, pair) * grad_scale
        for side in range(2):
            value = result[:, side * LANES : (side + 1) * LANES]
            head, tail = head_tail(value)
            head, tail = head.astype(jnp.float32), tail.astype(jnp.float32)
            near = 2 * pair + side
            here = pl.ds(2 * rows, rows)
            out_ref[near, here, :] = jnp.where(left, head, swap(tail)).astype(jnp.bfloat16)
            out_ref[near + half, here, :] = jnp.where(left, swap(head), tail).astype(jnp.bfloat16)
        return 0

    lax.fori_loop(0, half // 2, filter_grads, 0)

    def fold(value):
        return jnp.sum(value.reshape(rows // 8, 8, LANES), axis=0)

    def outputs(step, carry):
        block = blocks - 1 - step
        starts, totals = carry[:2], carry[2:]
        field = fields[block]
        result = jnp.where(
            left,
            spectra[blocks - 1 - block, pl.ds(0, rows), :],
            spectra[block, pl.ds(0, rows), :],
        )
        turned = swap(result + gain * field)
        grads = (second_ref[block] * turned, first_ref[block] * turned)
        new_totals = []
        for place, weights in ((0, query_taps), (1, value_taps)):
            grad = grads[place]
            ahead[place, pl.ds(0, rows), :] = grad
            ahead[place, pl.ds(rows, 8), :] = starts[place]
            here = pl.ds(place * rows, rows)
            stream = in_ref[block, here, :].astype(jnp.float32)
            total = weights[0] * grad
            new_totals.append(totals[3 * place] + fold(grad * stream))
            for offset in (1, 2):
                later = ahead[place, pl.ds(offset, rows), :]
                total = total + weights[offset] * later
                new_totals.append(totals[3 * place + offset] + fold(later * stream))
            out_ref[block, here, :] = total.astype(jnp.bfloat16)
        new_totals.append(totals[6] + fold(field * swap(field)))
        return (grads[0][:8], grads[1][:8], *new_totals)

    totals = lax.fori_loop(0, blocks, outputs, (nothing,) * 9)[2:]
    sums_ref[...] = jnp.zeros((8, LANES), jnp.float32)
    for row, total in enumerate(totals):
        sums_ref[row : row + 1, :] = grad_scale * jnp.sum(total, axis=0, keepdims=True)
    head, tail = head_tail(sums_ref[...])
    both = jnp.concatenate([head.astype(jnp.float32), tail.astype(jnp.float32)], axis=0)
    for block in range(blocks):
        out_ref[block, pl.ds(3 * rows, SUMS), :] = both.astype(jnp.bfloat16)


def operator(taps, streams):
    blocks = streams.shape[0]
    rows = streams.shape[1] // 3
    forward, inverse = transform_matrices(rows)
    wide = (blocks, rows, LANES)
    return pl.pallas_call(
        operator_kernel,
        out_shape=jax.ShapeDtypeStruct((blocks, 3 * rows + SUMS, LANES), jnp.bfloat16),
        scratch_shapes=[
            pltpu.VMEM((2, rows + 8, LANES), jnp.float32),
            pltpu.VMEM((2, rows + 8, LANES), jnp.float32),
            pltpu.VMEM(wide, jnp.float32),
            pltpu.VMEM(wide, jnp.float32),
            pltpu.VMEM(wide, jnp.float32),
            pltpu.VMEM((blocks, 2 * rows, LANES), jnp.float32),
            pltpu.VMEM((blocks, 2 * rows, LANES), jnp.float32),
            pltpu.VMEM((3 * rows, 2 * LANES), jnp.bfloat16),
            pltpu.VMEM((6 * rows, 2 * LANES), jnp.bfloat16),
            pltpu.VMEM((8, LANES), jnp.float32),
        ],
        compiler_params=pltpu.CompilerParams(vmem_limit_bytes=VMEM_BYTES),
    )(jnp.asarray(forward), jnp.asarray(inverse), taps, streams)


def own_taps(short_taps, skip_gain):
    places = lax.axis_size("seq")
    columns = lax.axis_size("chan")
    share = skip_gain.shape[0]

    def pair(one, two):
        fill = ((0, 0), (0, HALF - share))
        return jnp.concatenate([jnp.pad(one, fill), jnp.pad(two, fill)], axis=1)

    straight = jnp.concatenate([jnp.ones((1, share)), jnp.zeros((2, share))]).astype(jnp.float32)
    rows = jnp.concatenate(
        [
            pair(short_taps[0], short_taps[1]),
            pair(straight, short_taps[2]),
            pair(skip_gain[None], skip_gain[None]),
            jnp.zeros((1, LANES), jnp.float32),
        ]
    )
    route = [
        (flat, (flat % places) * columns + flat // places) for flat in range(places * columns)
    ]
    return lax.ppermute(rows, ("seq", "chan"), route)


def per_device(query_rows, key_rows, value_rows, long_filter, short_taps, skip_gain, cotangent):
    rows, channels = query_rows.shape
    devices = lax.axis_size("seq")
    taps = own_taps(short_taps, skip_gain)
    sent = pack(query_rows, key_rows, value_rows, cotangent, long_filter, devices)
    streams = lax.all_to_all(sent, "seq", 0, 0, tiled=True)
    results = lax.all_to_all(operator(taps, streams), "seq", 0, 0, tiled=True)
    gated, query_grad, key_grad, value_grad, filter_grad, sums = unpack(results, rows, channels)
    taps_grad = jnp.stack([sums[0, 0:3], sums[1, 0:3], sums[1, 3:6]])
    return gated, query_grad, key_grad, value_grad, filter_grad, taps_grad, sums[0, 6]


def solution(mesh):
    in_specs = (
        P("seq", "chan"),
        P("seq", "chan"),
        P("seq", "chan"),
        P("seq", "chan"),
        P(None, None, ("seq", "chan")),
        P(("seq", "chan")),
        P("seq", "chan"),
    )
    out_specs = (
        P("seq", "chan"),
        P("seq", "chan"),
        P("seq", "chan"),
        P("seq", "chan"),
        P("seq", "chan"),
        P(None, None, "chan"),
        P("chan"),
    )
    return jax.shard_map(
        per_device, mesh=mesh, in_specs=in_specs, out_specs=out_specs, check_vma=False
    )
```

```python
import math

import jax
import jax.numpy as jnp
import numpy as np
from jax import lax
from jax.experimental import pallas as pl
from jax.experimental.pallas import tpu as pltpu
from jax.sharding import PartitionSpec as P

HALF = 64
LANES = 2 * HALF
EDGE = 16
MISC = 24
SPAN = 252.0
FLOOR = 125.0
VMEM_BYTES = 62 * 1024 * 1024


def swap(value):
    return pltpu.roll(value, HALF, 1)


def left_lanes(shape):
    return lax.broadcasted_iota(jnp.int32, shape, 1) < HALF


def head_tail(value):
    head = value.astype(jnp.bfloat16)
    tail = (value - head.astype(jnp.float32)).astype(jnp.bfloat16)
    return head, tail


def transform_matrices(rows):
    freq = np.concatenate([np.arange(0, rows, 2), np.arange(1, rows, 2)])
    turn = (2 * freq[:, None] + 1) * np.arange(rows)[None, :] % (4 * rows)
    theta = turn * (math.pi / (2 * rows))
    forward = np.concatenate([np.cos(theta), -np.sin(theta)])
    inverse = forward.T / rows

    def split(matrix):
        single = matrix.astype(np.float32)
        head = single.astype(jnp.bfloat16)
        tail = (single - head.astype(np.float32)).astype(jnp.bfloat16)
        return np.concatenate([head, head, tail], axis=1)

    return split(forward), split(inverse)


def encode(value, scale):
    code = jnp.exp2(jnp.abs(value) * (SPAN / scale) - FLOOR)
    return jnp.where(value < 0.0, -code, code)


def decode(code, scale):
    size = (jnp.log2(jnp.abs(code)) + FLOOR) * (scale * (1.0 / SPAN))
    return jnp.where(code < 0.0, -size, size)


def scale_of(value):
    peak = jnp.max(jnp.abs(value), axis=0, keepdims=True)
    return jnp.maximum(peak * 1.0001, 1e-30)


def pack_kernel(
    query_ref, key_ref, value_ref, cot_ref, filter_ref, out_ref, last_ref, first_ref
):
    rows, channels = query_ref.shape
    half = rows // 2
    left = left_lanes((rows, LANES))
    left_half = left_lanes((half, LANES))
    for tile in range(channels // LANES):
        at = pl.ds(tile * LANES, LANES)
        for first, second, place in ((query_ref, key_ref, 0), (cot_ref, value_ref, 1)):
            one = first[:, at].astype(jnp.float32)
            two = second[:, at].astype(jnp.float32)
            here = pl.ds(place * rows, rows)
            out_ref[2 * tile, here, :] = jnp.where(left, one, swap(two)).astype(jnp.bfloat16)
            out_ref[2 * tile + 1, here, :] = jnp.where(left, swap(one), two).astype(jnp.bfloat16)
        upper = filter_ref[pl.ds(0, half), at]
        lower = filter_ref[pl.ds(half, half), at]
        for dest, pair in (
            (2 * tile, jnp.where(left_half, upper, swap(lower))),
            (2 * tile + 1, jnp.where(left_half, swap(upper), lower)),
        ):
            scale = scale_of(pair)
            out_ref[dest, pl.ds(2 * rows, half), :] = encode(pair, scale).astype(jnp.bfloat16)
            head, tail = head_tail(jnp.broadcast_to(scale, (8, LANES)))
            both = jnp.concatenate([head.astype(jnp.float32), tail.astype(jnp.float32)], axis=0)
            out_ref[dest, pl.ds(2 * rows + half, 16), :] = both.astype(jnp.bfloat16)
    for stream, source in enumerate((query_ref, key_ref, value_ref, cot_ref)):
        first_ref[stream] = source[pl.ds(0, EDGE), :]
        if stream < 3:
            last_ref[stream] = source[pl.ds(rows - EDGE, EDGE), :]


def pack(streams, cotangent, long_filter, devices):
    rows, channels = cotangent.shape
    return pl.pallas_call(
        pack_kernel,
        out_shape=(
            jax.ShapeDtypeStruct((devices, 2 * rows + rows // 2 + 16, LANES), jnp.bfloat16),
            jax.ShapeDtypeStruct((3, EDGE, channels), jnp.bfloat16),
            jax.ShapeDtypeStruct((4, EDGE, channels), jnp.bfloat16),
        ),
        compiler_params=pltpu.CompilerParams(vmem_limit_bytes=VMEM_BYTES),
    )(*streams, cotangent, long_filter)


def finish_kernel(
    in_ref, query_ref, key_ref, value_ref, cot_ref, last_ref, first_ref,
    gated_out, query_out, key_out, value_out, filter_out, taps_out, skip_out,
    before, after,
):
    rows, channels = query_ref.shape
    half = rows // 2
    left = left_lanes((rows, LANES))
    left_half = left_lanes((half, LANES))
    left_misc = left_lanes((MISC, LANES))
    for tile in range(channels // LANES):
        at = pl.ds(tile * LANES, LANES)
        miscs, results, grads = [], [], []
        for source in (2 * tile, 2 * tile + 1):
            pair = in_ref[source, pl.ds(rows + half, 2 * MISC), :].astype(jnp.float32)
            misc = pair[:MISC] + pair[MISC:]
            miscs.append(misc)
            code = in_ref[source, pl.ds(0, rows), :].astype(jnp.float32)
            results.append(decode(code, misc[0:1]))
            code = in_ref[source, pl.ds(rows, half), :].astype(jnp.float32)
            grads.append(decode(code, misc[1:2]))
        one, two = grads
        filter_out[pl.ds(0, half), at] = jnp.where(left_half, one, swap(two))
        filter_out[pl.ds(half, half), at] = jnp.where(left_half, swap(one), two)
        one, two = results
        back = jnp.where(left, one, swap(two))
        mixed = jnp.where(left, swap(one), two)
        one, two = miscs
        lefts = jnp.where(left_misc, one, swap(two))
        rights = jnp.where(left_misc, swap(one), two)
        taps = (lefts[4:7], rights[4:7], rights[7:10])
        for offset in range(3):
            taps_out[0, offset : offset + 1, at] = lefts[10 + offset : 11 + offset]
            taps_out[1, offset : offset + 1, at] = rights[10 + offset : 11 + offset]
            taps_out[2, offset : offset + 1, at] = rights[13 + offset : 14 + offset]
        skip_out[0:1, at] = lefts[16:17]
        back_edge, mixed_edge = lefts[2:4], rights[2:4]
        convs, edges = [], []
        for stream, source in enumerate((query_ref, key_ref, value_ref)):
            now = source[:, at].astype(jnp.float32)
            before[pl.ds(0, 8), :] = last_ref[stream, :, at].astype(jnp.float32)[EDGE - 8 :]
            before[pl.ds(8, rows), :] = now
            before[pl.ds(8 + rows, 8), :] = first_ref[stream, :, at].astype(jnp.float32)[:8]
            conv = taps[stream][0:1] * now
            edge = taps[stream][0:1] * before[pl.ds(8 + rows, 2), :]
            for offset in (1, 2):
                weight = taps[stream][offset : offset + 1]
                conv = conv + weight * before[pl.ds(8 - offset, rows), :]
                edge = edge + weight * before[pl.ds(8 + rows - offset, 2), :]
            convs.append(conv)
            edges.append(edge)
        cotangent = cot_ref[:, at].astype(jnp.float32)
        cot_edge = first_ref[3, :, at].astype(jnp.float32)[0:2]
        gated_out[:, at] = (convs[0] * mixed).astype(jnp.bfloat16)
        for stream, (out, grad, edge) in enumerate(
            (
                (query_out, cotangent * mixed, cot_edge * mixed_edge),
                (key_out, back * convs[2], back_edge * edges[2]),
                (value_out, back * convs[1], back_edge * edges[1]),
            )
        ):
            after[pl.ds(0, rows), :] = grad
            after[pl.ds(rows, 2), :] = edge
            total = taps[stream][0:1] * grad
            for offset in (1, 2):
                weight = taps[stream][offset : offset + 1]
                total = total + weight * after[pl.ds(offset, rows), :]
            out[:, at] = total.astype(jnp.bfloat16)


def finish(received, streams, cotangent, last_rows, next_rows):
    rows, channels = cotangent.shape
    low = jax.ShapeDtypeStruct((rows, channels), jnp.bfloat16)
    return pl.pallas_call(
        finish_kernel,
        out_shape=(
            low,
            low,
            low,
            low,
            jax.ShapeDtypeStruct((rows, channels), jnp.float32),
            jax.ShapeDtypeStruct((3, 3, channels), jnp.float32),
            jax.ShapeDtypeStruct((1, channels), jnp.float32),
        ),
        scratch_shapes=[
            pltpu.VMEM((rows + 16, LANES), jnp.float32),
            pltpu.VMEM((rows + 8, LANES), jnp.float32),
        ],
        compiler_params=pltpu.CompilerParams(vmem_limit_bytes=VMEM_BYTES),
    )(received, *streams, cotangent, last_rows, next_rows)


def operator_kernel(
    forward_ref, inverse_ref, taps_ref, in_ref, out_ref,
    behind, ahead, first_ref, second_ref, fields, spectra, filters, rhs, rhs_back, sums_ref, misc,
):
    blocks = in_ref.shape[0]
    rows = forward_ref.shape[0] // 2
    half = blocks // 2
    half_rows = rows // 2
    grad_scale = 1.0 / math.sqrt(blocks * rows)
    left = left_lanes((rows, LANES))
    left_half = left_lanes((half_rows, LANES))
    taps = taps_ref[...]
    query_taps = [taps[i : i + 1] for i in range(3)]
    value_taps = [taps[3 + i : 4 + i] for i in range(3)]
    gain = taps[6:7]

    def short(block, carry):
        outs, ends = [], []
        for place, weights, before in ((0, query_taps, carry[0]), (1, value_taps, carry[1])):
            now = in_ref[block, pl.ds(place * rows, rows), :].astype(jnp.float32)
            behind[place, pl.ds(0, 8), :] = before
            behind[place, pl.ds(8, rows), :] = now
            total = weights[0] * now
            for offset in (1, 2):
                total = total + weights[offset] * behind[place, pl.ds(8 - offset, rows), :]
            outs.append(total)
            ends.append(now[rows - 8 :])
        first_ref[block] = outs[0]
        second_ref[block] = outs[1]
        fields[block] = outs[0] * outs[1]
        return tuple(ends)

    nothing = jnp.zeros((8, LANES), jnp.float32)
    lax.fori_loop(0, blocks, short, (nothing, nothing))

    def transform(pair, _):
        for side in range(2):
            block = 2 * pair + side
            field = jnp.where(left, fields[blocks - 1 - block], fields[block])
            head, tail = head_tail(field)
            at = pl.ds(side * LANES, LANES)
            rhs[pl.ds(0, rows), at] = head
            rhs[pl.ds(rows, rows), at] = tail
            rhs[pl.ds(2 * rows, rows), at] = head
        result = jnp.dot(forward_ref[...], rhs[...], preferred_element_type=jnp.float32)
        for side in range(2):
            spectra[2 * pair + side] = result[:, side * LANES : (side + 1) * LANES]
        for side in range(2):
            block = 2 * pair + side
            ends = in_ref[block, pl.ds(2 * rows + half_rows, 16), :].astype(jnp.float32)
            code = in_ref[block, pl.ds(2 * rows, half_rows), :].astype(jnp.float32)
            taken = decode(code, ends[0:1] + ends[8:9])
            turned = swap(taken)
            at = pl.ds(side * LANES, LANES)
            for place, value in (
                (0, jnp.where(left_half, taken, turned)),
                (half_rows, jnp.where(left_half, turned, taken)),
            ):
                head, tail = head_tail(value)
                rhs[pl.ds(place, half_rows), at] = head
                rhs[pl.ds(rows + place, half_rows), at] = tail
                rhs[pl.ds(2 * rows + place, half_rows), at] = head
        result = jnp.dot(forward_ref[...], rhs[...], preferred_element_type=jnp.float32)
        for side in range(2):
            filters[2 * pair + side] = result[:, side * LANES : (side + 1) * LANES]
        return 0

    lax.fori_loop(0, half, transform, 0)

    chunk = 8
    left_chunk = left_lanes((chunk, LANES))
    conjugate = jnp.where(left_chunk, -1.0, 1.0)

    def spectral(step, sign):
        real_at = pl.ds(pl.multiple_of(step * chunk, chunk), chunk)
        imag_at = pl.ds(pl.multiple_of(rows + step * chunk, chunk), chunk)
        field_re = [spectra[block, real_at, :] for block in range(blocks)]
        field_im = [spectra[block, imag_at, :] for block in range(blocks)]

        def joined(re, im, block):
            if block == 0:
                return re[0], im[0]
            if sign > 0:
                return re[block] - im[block - 1], im[block] + re[block - 1]
            return re[block] + im[block - 1], im[block] - re[block - 1]

        filt_re = [filters[block, real_at, :] for block in range(blocks)]
        filt_im = [filters[block, imag_at, :] for block in range(blocks)]
        joins = [joined(filt_re, filt_im, block) for block in range(blocks)]
        joins = [(re, im * conjugate) for re, im in joins]
        for block in range(blocks):
            out_re = out_im = None
            for lag in range(block + 1):
                re, im = field_re[block - lag], field_im[block - lag]
                join_re, join_im = joins[lag]
                term_re = re * join_re - im * join_im
                term_im = re * join_im + im * join_re
                out_re = term_re if out_re is None else out_re + term_re
                out_im = term_im if out_im is None else out_im + term_im
            spectra[block, real_at, :] = out_re
            spectra[block, imag_at, :] = out_im
        grads = []
        for block in range(blocks):
            re, im = field_re[blocks - 1 - block], field_im[blocks - 1 - block]
            grads.append(
                (jnp.where(left_chunk, re, swap(re)), jnp.where(left_chunk, im, swap(im)))
            )
        joins = [joined(field_re, field_im, block) for block in range(blocks)]
        products = []
        for block in range(blocks):
            parts = []
            for part in range(2):
                far = joins[block - half][part] if block >= half else 0.0
                parts.append(jnp.where(left_chunk, swap(joins[block][part]), far))
            products.append(parts)
        for lag in range(half):
            out_re = out_im = None
            for block in range(lag, blocks):
                re, im = grads[block]
                join_re, join_im = products[block - lag]
                term_re = re * join_re + im * join_im
                term_im = im * join_re - re * join_im
                out_re = term_re if out_re is None else out_re + term_re
                out_im = term_im if out_im is None else out_im + term_im
            filters[lag, real_at, :] = out_re
            filters[lag, imag_at, :] = out_im

    def even(step, _):
        spectral(step, 1)
        return 0

    def odd(step, _):
        spectral(step, -1)
        return 0

    steps = rows // chunk
    lax.fori_loop(0, steps // 2, even, 0)
    lax.fori_loop(steps // 2, steps, odd, 0)

    def back(source, pair):
        for side in range(2):
            head, tail = head_tail(source[2 * pair + side])
            at = pl.ds(side * LANES, LANES)
            rhs_back[pl.ds(0, 2 * rows), at] = head
            rhs_back[pl.ds(2 * rows, 2 * rows), at] = tail
            rhs_back[pl.ds(4 * rows, 2 * rows), at] = head
        return jnp.dot(inverse_ref[...], rhs_back[...], preferred_element_type=jnp.float32)

    def mixed(pair, _):
        result = back(spectra, pair)
        for side in range(2):
            spectra[2 * pair + side, pl.ds(0, rows), :] = result[
                :, side * LANES : (side + 1) * LANES
            ]
        return 0

    lax.fori_loop(0, half, mixed, 0)

    def filter_grads(pair, _):
        result = back(filters, pair) * grad_scale
        for side in range(2):
            value = result[:, side * LANES : (side + 1) * LANES]
            upper, lower = value[:half_rows], value[half_rows:]
            near = 2 * pair + side
            for dest, halves in (
                (near, jnp.where(left_half, upper, swap(lower))),
                (near + half, jnp.where(left_half, swap(upper), lower)),
            ):
                scale = scale_of(halves)
                code = encode(halves, scale).astype(jnp.bfloat16)
                out_ref[dest, pl.ds(rows, half_rows), :] = code
                misc[dest, 1:2, :] = scale
        return 0

    lax.fori_loop(0, half // 2, filter_grads, 0)

    def fold(value):
        return jnp.sum(value.reshape(rows // 8, 8, LANES), axis=0)

    def outputs(step, carry):
        block = blocks - 1 - step
        starts, totals = carry[:3], carry[3:]
        field = fields[block]
        result = jnp.where(
            left,
            spectra[blocks - 1 - block, pl.ds(0, rows), :],
            spectra[block, pl.ds(0, rows), :],
        )
        result = result + gain * field
        scale = scale_of(result)
        out_ref[block, pl.ds(0, rows), :] = encode(result, scale).astype(jnp.bfloat16)
        misc[block, 0:1, :] = scale
        misc[block, 2:4, :] = starts[2][0:2]
        turned = swap(result)
        grads = (second_ref[block] * turned, first_ref[block] * turned)
        new_totals = []
        for place in (0, 1):
            grad = grads[place]
            ahead[place, pl.ds(0, rows), :] = grad
            ahead[place, pl.ds(rows, 8), :] = starts[place]
            stream = in_ref[block, pl.ds(place * rows, rows), :].astype(jnp.float32)
            new_totals.append(totals[3 * place] + fold(grad * stream))
            for offset in (1, 2):
                later = ahead[place, pl.ds(offset, rows), :]
                new_totals.append(totals[3 * place + offset] + fold(later * stream))
        new_totals.append(totals[6] + fold(field * swap(field)))
        return (grads[0][:8], grads[1][:8], result[:8], *new_totals)

    totals = lax.fori_loop(0, blocks, outputs, (nothing,) * 10)[3:]
    sums_ref[pl.ds(0, 6), :] = taps[0:6]
    for row, total in enumerate(totals):
        sums_ref[6 + row : 7 + row, :] = grad_scale * jnp.sum(total, axis=0, keepdims=True)

    def close(block, _):
        misc[block, pl.ds(4, 13), :] = sums_ref[pl.ds(0, 13), :]
        misc[block, pl.ds(17, 7), :] = jnp.zeros((7, LANES), jnp.float32)
        head, tail = head_tail(misc[block])
        both = jnp.concatenate([head.astype(jnp.float32), tail.astype(jnp.float32)], axis=0)
        out_ref[block, pl.ds(rows + half_rows, 2 * MISC), :] = both.astype(jnp.bfloat16)
        return 0

    lax.fori_loop(0, blocks, close, 0)


def operator(taps, streams):
    blocks = streams.shape[0]
    rows = (streams.shape[1] - 16) * 2 // 5
    forward, inverse = transform_matrices(rows)
    wide = (blocks, rows, LANES)
    return pl.pallas_call(
        operator_kernel,
        out_shape=jax.ShapeDtypeStruct((blocks, rows + rows // 2 + 2 * MISC, LANES), jnp.bfloat16),
        scratch_shapes=[
            pltpu.VMEM((2, rows + 8, LANES), jnp.float32),
            pltpu.VMEM((2, rows + 8, LANES), jnp.float32),
            pltpu.VMEM(wide, jnp.float32),
            pltpu.VMEM(wide, jnp.float32),
            pltpu.VMEM(wide, jnp.float32),
            pltpu.VMEM((blocks, 2 * rows, LANES), jnp.float32),
            pltpu.VMEM((blocks, 2 * rows, LANES), jnp.float32),
            pltpu.VMEM((3 * rows, 2 * LANES), jnp.bfloat16),
            pltpu.VMEM((6 * rows, 2 * LANES), jnp.bfloat16),
            pltpu.VMEM((16, LANES), jnp.float32),
            pltpu.VMEM((blocks, MISC, LANES), jnp.float32),
        ],
        compiler_params=pltpu.CompilerParams(vmem_limit_bytes=VMEM_BYTES),
    )(jnp.asarray(forward), jnp.asarray(inverse), taps, streams)


def own_taps(short_taps, skip_gain):
    places = lax.axis_size("seq")
    columns = lax.axis_size("chan")
    share = skip_gain.shape[0]

    def pair(one, two):
        fill = ((0, 0), (0, HALF - share))
        return jnp.concatenate([jnp.pad(one, fill), jnp.pad(two, fill)], axis=1)

    straight = jnp.concatenate([jnp.ones((1, share)), jnp.zeros((2, share))]).astype(jnp.float32)
    rows = jnp.concatenate(
        [
            pair(short_taps[0], short_taps[1]),
            pair(straight, short_taps[2]),
            pair(skip_gain[None], skip_gain[None]),
            jnp.zeros((1, LANES), jnp.float32),
        ]
    )
    route = [
        (flat, (flat % places) * columns + flat // places) for flat in range(places * columns)
    ]
    return lax.ppermute(rows, ("seq", "chan"), route)


def spread(value, devices):
    rows, channels = value.shape
    share = channels // devices
    if share == HALF:
        return value
    wide = jnp.pad(value.reshape(rows, devices, share), ((0, 0), (0, 0), (0, HALF - share)))
    return wide.reshape(rows, devices * HALF)


def gathered(value, share):
    if share == HALF:
        return value
    groups = value.reshape(*value.shape[:-1], value.shape[-1] // HALF, HALF)[..., :share]
    return groups.reshape(*value.shape[:-1], -1)


def shift(value, by):
    length = lax.axis_size("seq")
    pairs = [(i, i + by) for i in range(length) if 0 <= i + by < length]
    return lax.ppermute(value, "seq", pairs)


def per_device(query_rows, key_rows, value_rows, long_filter, short_taps, skip_gain, cotangent):
    devices = lax.axis_size("seq")
    share = query_rows.shape[1] // devices
    taps = own_taps(short_taps, skip_gain)
    streams = [spread(value, devices) for value in (query_rows, key_rows, value_rows)]
    upstream = spread(cotangent, devices)
    sent, last_rows, first_rows = pack(streams, upstream, spread(long_filter, devices), devices)
    received = lax.all_to_all(sent, "seq", 0, 0, tiled=True)
    last_rows = shift(last_rows, 1)
    next_rows = shift(first_rows, -1)
    results = lax.all_to_all(operator(taps, received), "seq", 0, 0, tiled=True)
    outs = finish(results, streams, upstream, last_rows, next_rows)
    *outs, skip_grad = (gathered(value, share) for value in outs)
    return (*outs, skip_grad[0])


def solution(mesh):
    in_specs = (
        P("seq", "chan"),
        P("seq", "chan"),
        P("seq", "chan"),
        P("seq", "chan"),
        P(None, None, ("seq", "chan")),
        P(("seq", "chan")),
        P("seq", "chan"),
    )
    out_specs = (
        P("seq", "chan"),
        P("seq", "chan"),
        P("seq", "chan"),
        P("seq", "chan"),
        P("seq", "chan"),
        P(None, None, "chan"),
        P("chan"),
    )
    return jax.shard_map(
        per_device, mesh=mesh, in_specs=in_specs, out_specs=out_specs, check_vma=False
    )
```

```python
import math

import jax
import jax.numpy as jnp
import numpy as np
from jax import lax
from jax.experimental import pallas as pl
from jax.experimental.pallas import tpu as pltpu
from jax.sharding import PartitionSpec as P

HALF = 64
LANES = 2 * HALF
EDGE = 16
MISC = 16
SPAN = 252.0
FLOOR = 125.0
MEBIBYTE = 1024 * 1024
VMEM_BYTES = 62 * MEBIBYTE
UNROLLED = 8


def swap(value):
    return pltpu.roll(value, HALF, 1)


def left_lanes(shape):
    return lax.broadcasted_iota(jnp.int32, shape, 1) < HALF


def head_tail(value):
    head = value.astype(jnp.bfloat16)
    tail = (value - head.astype(jnp.float32)).astype(jnp.bfloat16)
    return head, tail


def transform_matrices(rows):
    freq = np.concatenate([np.arange(0, rows, 2), np.arange(1, rows, 2)])
    turn = (2 * freq[:, None] + 1) * np.arange(rows)[None, :] % (4 * rows)
    theta = turn * (math.pi / (2 * rows))
    forward = np.concatenate([np.cos(theta), -np.sin(theta)])
    inverse = forward.T / rows

    def split(matrix):
        single = matrix.astype(np.float32)
        head = single.astype(jnp.bfloat16)
        tail = (single - head.astype(np.float32)).astype(jnp.bfloat16)
        return np.concatenate([head, head, tail], axis=1)

    return split(forward), split(inverse)


def encode(value, scale):
    code = jnp.exp2(jnp.abs(value) * (SPAN / scale) - FLOOR)
    return jnp.where(value < 0.0, -code, code)


def decode(code, scale):
    size = (jnp.log2(jnp.abs(code)) + FLOOR) * (scale * (1.0 / SPAN))
    return jnp.where(code < 0.0, -size, size)


def scale_of(value):
    peak = jnp.max(jnp.abs(value), axis=0, keepdims=True)
    return jnp.maximum(peak * 1.0001, 1e-30)


def pack_kernel(
    query_ref, key_ref, value_ref, cot_ref, filter_ref, out_ref, last_ref, first_ref
):
    rows = query_ref.shape[0]
    half = rows // 2
    left = left_lanes((rows, LANES))
    left_half = left_lanes((half, LANES))
    for first, second, place in ((query_ref, key_ref, 0), (cot_ref, value_ref, 1)):
        one = first[...].astype(jnp.float32)
        two = second[...].astype(jnp.float32)
        here = pl.ds(place * rows, rows)
        out_ref[0, here, :] = jnp.where(left, one, swap(two)).astype(jnp.bfloat16)
        out_ref[1, here, :] = jnp.where(left, swap(one), two).astype(jnp.bfloat16)
    upper = filter_ref[pl.ds(0, half), :]
    lower = filter_ref[pl.ds(half, half), :]
    for dest, pair in enumerate(
        (jnp.where(left_half, upper, swap(lower)), jnp.where(left_half, swap(upper), lower))
    ):
        scale = scale_of(pair)
        out_ref[dest, pl.ds(2 * rows, half), :] = encode(pair, scale).astype(jnp.bfloat16)
        head, tail = head_tail(jnp.broadcast_to(scale, (8, LANES)))
        both = jnp.concatenate([head.astype(jnp.float32), tail.astype(jnp.float32)], axis=0)
        out_ref[dest, pl.ds(2 * rows + half, 16), :] = both.astype(jnp.bfloat16)
    for stream, source in enumerate((query_ref, key_ref, value_ref, cot_ref)):
        first_ref[stream] = source[pl.ds(0, EDGE), :]
        if stream < 3:
            last_ref[stream] = source[pl.ds(rows - EDGE, EDGE), :]


def pack(streams, cotangent, long_filter, devices):
    rows, channels = cotangent.shape
    sent_rows = 2 * rows + rows // 2 + 16
    whole = pl.BlockSpec((rows, LANES), lambda tile: (0, tile))
    return pl.pallas_call(
        pack_kernel,
        grid=(channels // LANES,),
        in_specs=[whole] * 5,
        out_specs=(
            pl.BlockSpec((2, sent_rows, LANES), lambda tile: (tile, 0, 0)),
            pl.BlockSpec((3, EDGE, LANES), lambda tile: (0, 0, tile)),
            pl.BlockSpec((4, EDGE, LANES), lambda tile: (0, 0, tile)),
        ),
        out_shape=(
            jax.ShapeDtypeStruct((devices, sent_rows, LANES), jnp.bfloat16),
            jax.ShapeDtypeStruct((3, EDGE, channels), jnp.bfloat16),
            jax.ShapeDtypeStruct((4, EDGE, channels), jnp.bfloat16),
        ),
        compiler_params=pltpu.CompilerParams(vmem_limit_bytes=VMEM_BYTES),
    )(*streams, cotangent, long_filter)


def finish_kernel(
    in_ref, query_ref, key_ref, value_ref, cot_ref, last_ref, first_ref,
    gated_out, query_out, key_out, value_out, filter_out, taps_out, skip_out,
    before, after,
):
    rows, channels = query_ref.shape
    half = rows // 2
    left = left_lanes((rows, LANES))
    left_half = left_lanes((half, LANES))
    left_misc = left_lanes((MISC, LANES))
    for tile in range(channels // LANES):
        at = pl.ds(tile * LANES, LANES)
        miscs, results, grads = [], [], []
        for source in (2 * tile, 2 * tile + 1):
            pair = in_ref[source, pl.ds(rows + half, 2 * MISC), :].astype(jnp.float32)
            misc = pair[:MISC] + pair[MISC:]
            miscs.append(misc)
            code = in_ref[source, pl.ds(0, rows), :].astype(jnp.float32)
            results.append(decode(code, misc[0:1]))
            code = in_ref[source, pl.ds(rows, half), :].astype(jnp.float32)
            grads.append(decode(code, misc[1:2]))
        one, two = grads
        filter_out[pl.ds(0, half), at] = jnp.where(left_half, one, swap(two))
        filter_out[pl.ds(half, half), at] = jnp.where(left_half, swap(one), two)
        one, two = results
        back = jnp.where(left, one, swap(two))
        mixed = jnp.where(left, swap(one), two)
        one, two = miscs
        lefts = jnp.where(left_misc, one, swap(two))
        rights = jnp.where(left_misc, swap(one), two)
        taps = (lefts[4:7], rights[4:7], rights[7:10])
        for offset in range(3):
            taps_out[0, offset : offset + 1, at] = lefts[10 + offset : 11 + offset]
            taps_out[1, offset : offset + 1, at] = rights[10 + offset : 11 + offset]
            taps_out[2, offset : offset + 1, at] = rights[13 + offset : 14 + offset]
        skip_out[0:1, at] = lefts[13:14]
        back_edge, mixed_edge = lefts[2:4], rights[2:4]
        convs, edges = [], []
        for stream, source in enumerate((query_ref, key_ref, value_ref)):
            now = source[:, at].astype(jnp.float32)
            before[pl.ds(0, 8), :] = last_ref[stream, :, at].astype(jnp.float32)[EDGE - 8 :]
            before[pl.ds(8, rows), :] = now
            before[pl.ds(8 + rows, 8), :] = first_ref[stream, :, at].astype(jnp.float32)[:8]
            conv = taps[stream][0:1] * now
            edge = taps[stream][0:1] * before[pl.ds(8 + rows, 2), :]
            for offset in (1, 2):
                weight = taps[stream][offset : offset + 1]
                conv = conv + weight * before[pl.ds(8 - offset, rows), :]
                edge = edge + weight * before[pl.ds(8 + rows - offset, 2), :]
            convs.append(conv)
            edges.append(edge)
        cotangent = cot_ref[:, at].astype(jnp.float32)
        cot_edge = first_ref[3, :, at].astype(jnp.float32)[0:2]
        gated_out[:, at] = (convs[0] * mixed).astype(jnp.bfloat16)
        for stream, (out, grad, edge) in enumerate(
            (
                (query_out, cotangent * mixed, cot_edge * mixed_edge),
                (key_out, back * convs[2], back_edge * edges[2]),
                (value_out, back * convs[1], back_edge * edges[1]),
            )
        ):
            after[pl.ds(0, rows), :] = grad
            after[pl.ds(rows, 2), :] = edge
            total = taps[stream][0:1] * grad
            for offset in (1, 2):
                weight = taps[stream][offset : offset + 1]
                total = total + weight * after[pl.ds(offset, rows), :]
            out[:, at] = total.astype(jnp.bfloat16)


def finish(received, streams, cotangent, last_rows, next_rows):
    rows, channels = cotangent.shape
    low = jax.ShapeDtypeStruct((rows, channels), jnp.bfloat16)
    return pl.pallas_call(
        finish_kernel,
        out_shape=(
            low,
            low,
            low,
            low,
            jax.ShapeDtypeStruct((rows, channels), jnp.float32),
            jax.ShapeDtypeStruct((3, 3, channels), jnp.float32),
            jax.ShapeDtypeStruct((1, channels), jnp.float32),
        ),
        scratch_shapes=[
            pltpu.VMEM((rows + 16, LANES), jnp.float32),
            pltpu.VMEM((rows + 8, LANES), jnp.float32),
        ],
        compiler_params=pltpu.CompilerParams(vmem_limit_bytes=3 * received.shape[0] * MEBIBYTE // 2),
    )(received, *streams, cotangent, last_rows, next_rows)


def loop(count, body, carry, unrolled):
    if unrolled:
        for index in range(count):
            carry = body(index, carry)
        return carry
    return lax.fori_loop(0, count, body, carry)


def operator_kernel(
    forward_ref, inverse_ref, taps_ref, in_ref, out_ref,
    edged, first_ref, second_ref, fields, spectra, filters, rhs, rhs_back, shared, misc,
):
    blocks = in_ref.shape[0]
    rows = forward_ref.shape[0] // 2
    half = blocks // 2
    half_rows = rows // 2
    unrolled = blocks <= UNROLLED
    grad_scale = 1.0 / math.sqrt(blocks * rows)
    left = left_lanes((rows, LANES))
    left_half = left_lanes((half_rows, LANES))
    taps = taps_ref[...]
    query_taps = [taps[i : i + 1] for i in range(3)]
    value_taps = [taps[3 + i : 4 + i] for i in range(3)]
    gain = taps[6:7]
    nothing = jnp.zeros((8, LANES), jnp.float32)

    def lay(buffer, side, place, value):
        head, tail = head_tail(value)
        count = value.shape[0]
        at = pl.ds(side * LANES, LANES)
        rhs[buffer, pl.ds(place, count), at] = head
        rhs[buffer, pl.ds(rows + place, count), at] = tail
        rhs[buffer, pl.ds(2 * rows + place, count), at] = head

    def transformed(buffer):
        return jnp.dot(forward_ref[...], rhs[buffer], preferred_element_type=jnp.float32)

    def transform(pair, carry):
        spot = 2 * pair if unrolled else 0
        for side in range(2):
            block = 2 * pair + side
            ends = in_ref[block, pl.ds(2 * rows + half_rows, 16), :].astype(jnp.float32)
            code = in_ref[block, pl.ds(2 * rows, half_rows), :].astype(jnp.float32)
            taken = decode(code, ends[0:1] + ends[8:9])
            turned = swap(taken)
            lay(spot, side, 0, jnp.where(left_half, taken, turned))
            lay(spot, side, half_rows, jnp.where(left_half, turned, taken))
        result = transformed(spot)
        for side in range(2):
            filters[2 * pair + side] = result[:, side * LANES : (side + 1) * LANES]
        for side in range(2):
            block = 2 * pair + side
            outs, ends = [], []
            for place, weights in ((0, query_taps), (1, value_taps)):
                now = in_ref[block, pl.ds(place * rows, rows), :].astype(jnp.float32)
                edged[block, place, pl.ds(0, 8), :] = carry[place]
                edged[block, place, pl.ds(8, rows), :] = now
                total = weights[0] * now
                for offset in (1, 2):
                    shifted = edged[block, place, pl.ds(8 - offset, rows), :]
                    total = total + weights[offset] * shifted
                outs.append(total)
                ends.append(now[rows - 8 :])
            carry = tuple(ends)
            first_ref[block] = outs[0]
            second_ref[block] = outs[1]
            field = outs[0] * outs[1]
            fields[block] = field
            lay(spot + 1, side, 0, field)
        result = transformed(spot + 1)
        for side in range(2):
            spectra[2 * pair + side] = result[:, side * LANES : (side + 1) * LANES]
        return carry

    loop(half, transform, (nothing, nothing), unrolled)

    chunk = 8
    left_chunk = left_lanes((chunk, LANES))
    conjugate = jnp.where(left_chunk, -1.0, 1.0)

    def products(pairs):
        one = two = three = None
        for (re, im, both), (join_re, join_less, join_more) in pairs:
            terms = join_re * both, re * join_less, im * join_more
            if one is None:
                one, two, three = terms
            else:
                one, two, three = one + terms[0], two + terms[1], three + terms[2]
        return one - three, one + two

    def spectral(step, sign):
        real_at = pl.ds(pl.multiple_of(step * chunk, chunk), chunk)
        imag_at = pl.ds(pl.multiple_of(rows + step * chunk, chunk), chunk)
        field_re = [spectra[block, real_at, :] for block in range(blocks)]
        field_im = [spectra[block, imag_at, :] for block in range(blocks)]

        def joined(re, im, block):
            if block == 0:
                return re[0], im[0]
            if sign > 0:
                return re[block] - im[block - 1], im[block] + re[block - 1]
            return re[block] + im[block - 1], im[block] - re[block - 1]

        turned = []
        for block in range(blocks):
            re = jnp.where(left_chunk, field_re[blocks - 1 - block], field_re[block])
            im = jnp.where(left_chunk, field_im[blocks - 1 - block], field_im[block])
            turned.append((re, im, re + im))
        filt_re = [filters[block, real_at, :] for block in range(blocks)]
        filt_im = [filters[block, imag_at, :] for block in range(blocks)]
        joins = []
        for block in range(blocks):
            re, im = joined(filt_re, filt_im, block)
            im = im * conjugate
            joins.append((re, im - re, re + im))
        outs = [
            products([(turned[block - lag], joins[lag]) for lag in range(block + 1)])
            for block in range(blocks)
        ]
        grads = []
        for block in range(blocks):
            re = jnp.where(left_chunk, field_re[block], swap(field_re[block]))
            im = jnp.where(left_chunk, field_im[block], swap(field_im[block]))
            grads.append((re, im, re + im))
        sums = [joined(field_re, field_im, block) for block in range(blocks)]
        joins = []
        for block in range(blocks):
            parts = []
            for part in range(2):
                far = sums[block - half][part] if block >= half else 0.0
                parts.append(jnp.where(left_chunk, swap(sums[block][part]), far))
            re, im = parts
            joins.append((re, -im - re, re - im))
        for block in range(blocks):
            for part, at in ((0, real_at), (1, imag_at)):
                spectra[block, at, :] = jnp.where(
                    left_chunk, outs[blocks - 1 - block][part], outs[block][part]
                )
        for lag in range(half):
            out = products([(grads[block], joins[block - lag]) for block in range(lag, blocks)])
            filters[lag, real_at, :] = out[0]
            filters[lag, imag_at, :] = out[1]

    def even(step, _):
        spectral(step, 1)
        return 0

    def odd(step, _):
        spectral(step, -1)
        return 0

    steps = rows // chunk
    lax.fori_loop(0, steps // 2, even, 0)
    lax.fori_loop(steps // 2, steps, odd, 0)

    def back(source, pair, buffer):
        for side in range(2):
            head, tail = head_tail(source[2 * pair + side])
            at = pl.ds(side * LANES, LANES)
            rhs_back[buffer, pl.ds(0, 2 * rows), at] = head
            rhs_back[buffer, pl.ds(2 * rows, 2 * rows), at] = tail
            rhs_back[buffer, pl.ds(4 * rows, 2 * rows), at] = head
        return jnp.dot(inverse_ref[...], rhs_back[buffer], preferred_element_type=jnp.float32)

    def filter_grads(pair, _):
        result = back(filters, pair, pair if unrolled else 0) * grad_scale
        for side in range(2):
            value = result[:, side * LANES : (side + 1) * LANES]
            upper, lower = value[:half_rows], value[half_rows:]
            near = 2 * pair + side
            for dest, halves in (
                (near, jnp.where(left_half, upper, swap(lower))),
                (near + half, jnp.where(left_half, swap(upper), lower)),
            ):
                scale = scale_of(halves)
                code = encode(halves, scale).astype(jnp.bfloat16)
                out_ref[dest, pl.ds(rows, half_rows), :] = code
                misc[dest, 1:2, :] = scale
        return 0

    loop(half // 2, filter_grads, 0, unrolled)

    def fold(value):
        return jnp.sum(value.reshape(rows // 8, 8, LANES), axis=0)

    def outputs(step, carry):
        pair = half - 1 - step
        results = back(spectra, pair, (half // 2 + step) if unrolled else 0)
        for side in (1, 0):
            block = 2 * pair + side
            start, totals = carry[0], carry[1:]
            field = fields[block]
            result = results[:, side * LANES : (side + 1) * LANES] + gain * field
            scale = scale_of(result)
            out_ref[block, pl.ds(0, rows), :] = encode(result, scale).astype(jnp.bfloat16)
            misc[block, 0:1, :] = scale
            misc[block, 2:4, :] = start[0:2]
            turned = swap(result)
            grads = (second_ref[block] * turned, first_ref[block] * turned)
            new_totals = []
            for place in (0, 1):
                grad = grads[place]
                stream = edged[block, place, pl.ds(8, rows), :]
                new_totals.append(totals[3 * place] + fold(grad * stream))
                for offset in (1, 2):
                    earlier = edged[block, place, pl.ds(8 - offset, rows), :]
                    new_totals.append(totals[3 * place + offset] + fold(grad * earlier))
            new_totals.append(totals[6] + fold(field * swap(field)))
            carry = (result[:8], *new_totals)
        return carry

    totals = loop(half, outputs, (nothing,) * 8, unrolled)[1:]
    sums = [grad_scale * jnp.sum(total, axis=0, keepdims=True) for total in totals]
    shared[0:6, :] = taps[0:6]
    for row in range(6):
        value = sums[row]
        if row == 3:
            value = jnp.where(left_lanes((1, LANES)), sums[6], value)
        shared[6 + row : 7 + row, :] = value

    def close(block, _):
        misc[block, 4:16, :] = shared[0:12, :]
        head, tail = head_tail(misc[block])
        here = rows + half_rows
        out_ref[block, pl.ds(here, MISC), :] = head
        out_ref[block, pl.ds(here + MISC, MISC), :] = tail
        return 0

    loop(blocks, close, 0, unrolled)


def operator(taps, streams):
    blocks = streams.shape[0]
    rows = (streams.shape[1] - 16) * 2 // 5
    forward, inverse = transform_matrices(rows)
    wide = (blocks, rows, LANES)
    backs = 3 * blocks // 4 if blocks <= UNROLLED else 1
    return pl.pallas_call(
        operator_kernel,
        out_shape=jax.ShapeDtypeStruct(
            (blocks, rows + rows // 2 + 2 * MISC, LANES), jnp.bfloat16
        ),
        scratch_shapes=[
            pltpu.VMEM((blocks, 2, rows + 8, LANES), jnp.float32),
            pltpu.VMEM(wide, jnp.float32),
            pltpu.VMEM(wide, jnp.float32),
            pltpu.VMEM(wide, jnp.float32),
            pltpu.VMEM((blocks, 2 * rows, LANES), jnp.float32),
            pltpu.VMEM((blocks, 2 * rows, LANES), jnp.float32),
            pltpu.VMEM((blocks if blocks <= UNROLLED else 2, 3 * rows, 2 * LANES), jnp.bfloat16),
            pltpu.VMEM((backs, 6 * rows, 2 * LANES), jnp.bfloat16),
            pltpu.VMEM((16, LANES), jnp.float32),
            pltpu.VMEM((blocks, MISC, LANES), jnp.float32),
        ],
        compiler_params=pltpu.CompilerParams(
            vmem_limit_bytes=min(4 * blocks * MEBIBYTE, VMEM_BYTES)
        ),
    )(jnp.asarray(forward), jnp.asarray(inverse), taps, streams)


def own_taps(short_taps, skip_gain):
    places = lax.axis_size("seq")
    columns = lax.axis_size("chan")
    share = skip_gain.shape[0]

    def pair(one, two):
        fill = ((0, 0), (0, HALF - share))
        return jnp.concatenate([jnp.pad(one, fill), jnp.pad(two, fill)], axis=1)

    straight = jnp.concatenate([jnp.ones((1, share)), jnp.zeros((2, share))]).astype(jnp.float32)
    rows = jnp.concatenate(
        [
            pair(short_taps[0], short_taps[1]),
            pair(straight, short_taps[2]),
            pair(skip_gain[None], skip_gain[None]),
            jnp.zeros((1, LANES), jnp.float32),
        ]
    )
    route = [
        (flat, (flat % places) * columns + flat // places) for flat in range(places * columns)
    ]
    return lax.ppermute(rows, ("seq", "chan"), route)


def spread(value, devices):
    rows, channels = value.shape
    share = channels // devices
    if share == HALF:
        return value
    wide = jnp.pad(value.reshape(rows, devices, share), ((0, 0), (0, 0), (0, HALF - share)))
    return wide.reshape(rows, devices * HALF)


def gathered(value, share):
    if share == HALF:
        return value
    groups = value.reshape(*value.shape[:-1], value.shape[-1] // HALF, HALF)[..., :share]
    return groups.reshape(*value.shape[:-1], -1)


def shift(value, by):
    length = lax.axis_size("seq")
    pairs = [(i, i + by) for i in range(length) if 0 <= i + by < length]
    return lax.ppermute(value, "seq", pairs)


def per_device(query_rows, key_rows, value_rows, long_filter, short_taps, skip_gain, cotangent):
    devices = lax.axis_size("seq")
    share = query_rows.shape[1] // devices
    taps = own_taps(short_taps, skip_gain)
    streams = [spread(value, devices) for value in (query_rows, key_rows, value_rows)]
    upstream = spread(cotangent, devices)
    sent, last_rows, first_rows = pack(streams, upstream, spread(long_filter, devices), devices)
    received = lax.all_to_all(sent, "seq", 0, 0, tiled=True)
    last_rows = shift(last_rows, 1)
    next_rows = shift(first_rows, -1)
    results = lax.all_to_all(operator(taps, received), "seq", 0, 0, tiled=True)
    outs = finish(results, streams, upstream, last_rows, next_rows)
    *outs, skip_grad = (gathered(value, share) for value in outs)
    return (*outs, skip_grad[0])


def solution(mesh):
    in_specs = (
        P("seq", "chan"),
        P("seq", "chan"),
        P("seq", "chan"),
        P("seq", "chan"),
        P(None, None, ("seq", "chan")),
        P(("seq", "chan")),
        P("seq", "chan"),
    )
    out_specs = (
        P("seq", "chan"),
        P("seq", "chan"),
        P("seq", "chan"),
        P("seq", "chan"),
        P("seq", "chan"),
        P(None, None, "chan"),
        P("chan"),
    )
    return jax.shard_map(
        per_device, mesh=mesh, in_specs=in_specs, out_specs=out_specs, check_vma=False
    )
```

```python
import math

import jax
import jax.numpy as jnp
import numpy as np
from jax import lax
from jax.experimental import pallas as pl
from jax.experimental.pallas import tpu as pltpu
from jax.sharding import PartitionSpec as P

HALF = 64
LANES = 2 * HALF
ENDS = 16
MISC = 16
SPAN = 252.0
FLOOR = 125.0
MEBIBYTE = 1024 * 1024
VMEM_BYTES = 62 * MEBIBYTE
LISTED = 8
ORDER = (0, 7, 6, 3, 2, 5, 4, 1)


def swap(value):
    return pltpu.roll(value, HALF, 1)


def left_lanes(shape):
    return lax.broadcasted_iota(jnp.int32, shape, 1) < HALF


def head_tail(value):
    head = value.astype(jnp.bfloat16)
    tail = (value - head.astype(jnp.float32)).astype(jnp.bfloat16)
    return head, tail


def transform_matrices(rows):
    freq = np.concatenate([np.arange(0, rows, 2), np.arange(1, rows, 2)])
    turn = (2 * freq[:, None] + 1) * np.arange(rows)[None, :] % (4 * rows)
    theta = turn * (math.pi / (2 * rows))
    forward = np.concatenate([np.cos(theta), -np.sin(theta)])
    inverse = forward.T / rows

    def split(matrix):
        single = matrix.astype(np.float32)
        head = single.astype(jnp.bfloat16)
        tail = (single - head.astype(np.float32)).astype(jnp.bfloat16)
        return np.concatenate([head, head, tail], axis=1)

    return split(forward), split(inverse)


def encode(value, scale):
    code = jnp.exp2(jnp.abs(value) * (SPAN / scale) - FLOOR)
    return jnp.where(value < 0.0, -code, code)


def decode(code, scale):
    size = (jnp.log2(jnp.abs(code)) + FLOOR) * (scale * (1.0 / SPAN))
    return jnp.where(code < 0.0, -size, size)


def scale_of(value):
    peak = jnp.max(jnp.abs(value), axis=0, keepdims=True)
    return jnp.maximum(peak * 1.0001, 1e-30)


def loop(count, body, carry, unrolled):
    if unrolled:
        for index in range(count):
            carry = body(index, carry)
        return carry
    return lax.fori_loop(0, count, body, carry)


def piece(refs, index, place):
    return refs[index] if len(refs) > 1 else refs[0].at[index ^ place]


def exchange(pieces):
    if len(pieces) == 1:
        return [lax.all_to_all(pieces[0], "seq", 0, 0, tiled=True)]
    others = [
        lax.ppermute(value, "seq", [(one, one ^ index) for one in range(len(pieces))])
        for index, value in enumerate(pieces[1:], 1)
    ]
    return [pieces[0], *others]


def in_order(pieces):
    return [pieces[index] for index in ORDER] if len(pieces) > 1 else pieces


def by_index(refs):
    if len(refs) == 1:
        return refs
    return [refs[ORDER.index(index)] for index in range(len(refs))]


def piece_shapes(devices, rows):
    if devices == LISTED:
        return [jax.ShapeDtypeStruct((rows, LANES), jnp.bfloat16)] * devices
    return [jax.ShapeDtypeStruct((devices, rows, LANES), jnp.bfloat16)]


def join(mask, one, two, side):
    return jnp.where(mask, pltpu.roll(one, side * HALF, 1), pltpu.roll(two, HALF - side * HALF, 1))


def pack_kernel(query_ref, key_ref, value_ref, cot_ref, filter_ref, *out_refs):
    rows, channels = query_ref.shape
    devices = channels // HALF
    half = rows // 2
    place = lax.axis_index("seq")
    left = left_lanes((rows, LANES))
    left_half = left_lanes((half, LANES))

    def one_piece(index, _):
        out_ref = piece(out_refs, index, place)
        dest = index ^ place
        side = lax.rem(dest, 2)
        at = pl.ds(pl.multiple_of(dest // 2 * LANES, LANES), LANES)
        for first, second, start in ((query_ref, key_ref, 0), (cot_ref, value_ref, rows)):
            one = first[:, at].astype(jnp.float32)
            two = second[:, at].astype(jnp.float32)
            out_ref[pl.ds(start, rows), :] = join(left, one, two, side).astype(jnp.bfloat16)
        upper = filter_ref[pl.ds(0, half), at]
        lower = filter_ref[pl.ds(half, half), at]
        pair = join(left_half, upper, lower, side)
        scale = scale_of(pair)
        out_ref[pl.ds(2 * rows, half), :] = encode(pair, scale).astype(jnp.bfloat16)
        head, tail = head_tail(jnp.broadcast_to(scale, (8, LANES)))
        both = jnp.concatenate([head.astype(jnp.float32), tail.astype(jnp.float32)], axis=0)
        out_ref[pl.ds(2 * rows + half, 16), :] = both.astype(jnp.bfloat16)
        return 0

    loop(devices, one_piece, 0, len(out_refs) > 1)


def pack(streams, cotangent, long_filter, devices):
    rows = cotangent.shape[0]
    return pl.pallas_call(
        pack_kernel,
        out_shape=piece_shapes(devices, 2 * rows + rows // 2 + 16),
        compiler_params=pltpu.CompilerParams(vmem_limit_bytes=VMEM_BYTES),
    )(*streams, cotangent, long_filter)


def finish_kernel(
    pieces, query_ref, key_ref, value_ref, cot_ref, gated_out, query_out, key_out, value_out,
    filter_out, taps_out, skip_out, before, after,
):
    in_refs = by_index(pieces)
    rows, channels = query_ref.shape
    half = rows // 2
    place = lax.axis_index("seq")
    odd = lax.rem(place, 2) == 1
    left = left_lanes((rows, LANES))
    left_half = left_lanes((half, LANES))
    left_misc = left_lanes((MISC, LANES))

    def one_tile(step, _):
        refs = piece(in_refs, 2 * step, place), piece(in_refs, 2 * step + 1, place)
        at = pl.ds(pl.multiple_of((step ^ (place // 2)) * LANES, LANES), LANES)

        def both(start, count):
            one, two = (ref[pl.ds(start, count), :].astype(jnp.float32) for ref in refs)
            return jnp.where(odd, two, one), jnp.where(odd, one, two)

        def sides(mask, values):
            one, two = values
            return jnp.where(mask, one, swap(two)), jnp.where(mask, swap(one), two)

        miscs = [
            head + tail
            for head, tail in zip(both(rows + half, MISC), both(rows + half + MISC, MISC))
        ]
        codes = both(0, rows)
        back, mixed = sides(left, [decode(code, misc[0:1]) for code, misc in zip(codes, miscs)])
        codes = both(rows, half)
        upper, lower = sides(
            left_half, [decode(code, misc[1:2]) for code, misc in zip(codes, miscs)]
        )
        filter_out[pl.ds(0, half), at] = upper
        filter_out[pl.ds(half, half), at] = lower
        ends = sides(left_misc, both(rows + half + 2 * MISC, ENDS))
        lefts, rights = sides(left_misc, miscs)
        taps = (lefts[4:7], rights[4:7], rights[7:10])
        for offset in range(3):
            taps_out[0, offset : offset + 1, at] = lefts[10 + offset : 11 + offset]
            taps_out[1, offset : offset + 1, at] = rights[10 + offset : 11 + offset]
            taps_out[2, offset : offset + 1, at] = rights[13 + offset : 14 + offset]
        skip_out[0:1, at] = lefts[13:14]
        back_edge, mixed_edge = lefts[2:4], rights[2:4]
        convs, edges = [], []
        for stream, (source, end, row) in enumerate(
            ((query_ref, ends[0], 0), (key_ref, ends[1], 0), (value_ref, ends[1], 2))
        ):
            now = source[:, at].astype(jnp.float32)
            before[stream, 6:8, :] = end[row : row + 2]
            before[stream, pl.ds(8, rows), :] = now
            before[stream, pl.ds(8 + rows, 2), :] = end[row + 4 : row + 6]
            conv = taps[stream][0:1] * now
            edge = taps[stream][0:1] * end[row + 4 : row + 6]
            for offset in (1, 2):
                weight = taps[stream][offset : offset + 1]
                conv = conv + weight * before[stream, pl.ds(8 - offset, rows), :]
                edge = edge + weight * before[stream, pl.ds(8 + rows - offset, 2), :]
            convs.append(conv)
            edges.append(edge)
        cotangent = cot_ref[:, at].astype(jnp.float32)
        cot_edge = ends[0][6:8]
        gated_out[:, at] = (convs[0] * mixed).astype(jnp.bfloat16)
        for stream, (out, grad, edge) in enumerate(
            (
                (query_out, cotangent * mixed, cot_edge * mixed_edge),
                (key_out, back * convs[2], back_edge * edges[2]),
                (value_out, back * convs[1], back_edge * edges[1]),
            )
        ):
            after[stream, pl.ds(0, rows), :] = grad
            after[stream, pl.ds(rows, 2), :] = edge
            total = taps[stream][0:1] * grad
            for offset in (1, 2):
                weight = taps[stream][offset : offset + 1]
                total = total + weight * after[stream, pl.ds(offset, rows), :]
            out[:, at] = total.astype(jnp.bfloat16)
        return 0

    loop(channels // LANES, one_tile, 0, len(in_refs) > 1)


def finish(received, streams, cotangent):
    rows, channels = cotangent.shape
    count = len(received)
    low = jax.ShapeDtypeStruct((rows, channels), jnp.bfloat16)

    def kernel(*refs):
        finish_kernel(refs[:count], *refs[count:])

    return pl.pallas_call(
        kernel,
        out_shape=(
            low,
            low,
            low,
            low,
            jax.ShapeDtypeStruct((rows, channels), jnp.float32),
            jax.ShapeDtypeStruct((3, 3, channels), jnp.float32),
            jax.ShapeDtypeStruct((1, channels), jnp.float32),
        ),
        scratch_shapes=[
            pltpu.VMEM((3, rows + 16, LANES), jnp.float32),
            pltpu.VMEM((3, rows + 8, LANES), jnp.float32),
        ],
        compiler_params=pltpu.CompilerParams(
            vmem_limit_bytes=3 * (channels // HALF) * MEBIBYTE // 2
        ),
    )(*in_order(received), *streams, cotangent)


def operator_kernel(
    pieces, out_refs, forward_ref, inverse_ref, taps_ref,
    ends, starts, edged, first_ref, second_ref, fields, spectra, filters, rhs, rhs_back,
    shared, misc,
):
    in_refs = by_index(pieces)
    blocks = fields.shape[0]
    place = lax.axis_index("seq")
    rows = forward_ref.shape[0] // 2
    half = blocks // 2
    half_rows = rows // 2
    unrolled = len(in_refs) > 1
    grad_scale = 1.0 / math.sqrt(blocks * rows)
    left = left_lanes((rows, LANES))
    left_half = left_lanes((half_rows, LANES))
    taps = taps_ref[...]
    query_taps = [taps[i : i + 1] for i in range(3)]
    value_taps = [taps[3 + i : 4 + i] for i in range(3)]
    gain = taps[6:7]
    nothing = jnp.zeros((8, LANES), jnp.float32)

    def lay(buffer, side, place, value):
        head, tail = head_tail(value)
        count = value.shape[0]
        at = pl.ds(side * LANES, LANES)
        rhs[buffer, pl.ds(place, count), at] = head
        rhs[buffer, pl.ds(rows + place, count), at] = tail
        rhs[buffer, pl.ds(2 * rows + place, count), at] = head

    def transformed(buffer):
        return jnp.dot(forward_ref[...], rhs[buffer], preferred_element_type=jnp.float32)

    def keep_ends(index, _):
        ref = piece(in_refs, index, place)
        block = index ^ place
        for stream in (0, 1):
            start = stream * rows
            last = ref[pl.ds(start + rows - 16, 16), :].astype(jnp.float32)
            first = ref[pl.ds(start, 16), :].astype(jnp.float32)
            ends[block + 1, 2 * stream : 2 * stream + 2, :] = last[14:16]
            ends[block + 1, 2 * stream + 4 : 2 * stream + 6, :] = first[0:2]
        return 0

    ends[0] = nothing
    ends[blocks + 1] = nothing
    loop(blocks, keep_ends, 0, unrolled)

    def transform(pair, _):
        spot = 2 * pair if unrolled else 0
        for side in range(2):
            ref = piece(in_refs, 2 * pair + side, place)
            scale = ref[pl.ds(2 * rows + half_rows, 16), :].astype(jnp.float32)
            code = ref[pl.ds(2 * rows, half_rows), :].astype(jnp.float32)
            taken = decode(code, scale[0:1] + scale[8:9])
            turned = swap(taken)
            lay(spot, side, 0, jnp.where(left_half, taken, turned))
            lay(spot, side, half_rows, jnp.where(left_half, turned, taken))
        result = transformed(spot)
        for side in range(2):
            filters[(2 * pair + side) ^ place] = result[:, side * LANES : (side + 1) * LANES]
        for side in range(2):
            index = 2 * pair + side
            ref = piece(in_refs, index, place)
            outs = []
            for stream, weights in ((0, query_taps), (1, value_taps)):
                now = ref[pl.ds(stream * rows, rows), :].astype(jnp.float32)
                last = ends[index ^ place, 2 * stream : 2 * stream + 2, :]
                edged[index, stream, 6:8, :] = last
                edged[index, stream, pl.ds(8, rows), :] = now
                total = weights[0] * now
                for offset in (1, 2):
                    shifted = edged[index, stream, pl.ds(8 - offset, rows), :]
                    total = total + weights[offset] * shifted
                outs.append(total)
            first_ref[index] = outs[0]
            second_ref[index] = outs[1]
            field = outs[0] * outs[1]
            fields[index] = field
            lay(spot + 1, side, 0, field)
        result = transformed(spot + 1)
        for side in range(2):
            spectra[(2 * pair + side) ^ place] = result[:, side * LANES : (side + 1) * LANES]
        return 0

    loop(half, transform, 0, unrolled)

    chunk = 8
    left_chunk = left_lanes((chunk, LANES))
    conjugate = jnp.where(left_chunk, -1.0, 1.0)

    def products(pairs):
        one = two = three = None
        for (re, im, both), (join_re, join_less, join_more) in pairs:
            terms = join_re * both, re * join_less, im * join_more
            if one is None:
                one, two, three = terms
            else:
                one, two, three = one + terms[0], two + terms[1], three + terms[2]
        return one - three, one + two

    def spectral(step, sign):
        real_at = pl.ds(pl.multiple_of(step * chunk, chunk), chunk)
        imag_at = pl.ds(pl.multiple_of(rows + step * chunk, chunk), chunk)
        field_re = [spectra[block, real_at, :] for block in range(blocks)]
        field_im = [spectra[block, imag_at, :] for block in range(blocks)]

        def joined(re, im, block):
            if block == 0:
                return re[0], im[0]
            if sign > 0:
                return re[block] - im[block - 1], im[block] + re[block - 1]
            return re[block] + im[block - 1], im[block] - re[block - 1]

        turned = []
        for block in range(blocks):
            re = jnp.where(left_chunk, field_re[blocks - 1 - block], field_re[block])
            im = jnp.where(left_chunk, field_im[blocks - 1 - block], field_im[block])
            turned.append((re, im, re + im))
        filt_re = [filters[block, real_at, :] for block in range(blocks)]
        filt_im = [filters[block, imag_at, :] for block in range(blocks)]
        joins = []
        for block in range(blocks):
            re, im = joined(filt_re, filt_im, block)
            im = im * conjugate
            joins.append((re, im - re, re + im))
        outs = [
            products([(turned[block - lag], joins[lag]) for lag in range(block + 1)])
            for block in range(blocks)
        ]
        grads = []
        for block in range(blocks):
            re = jnp.where(left_chunk, field_re[block], swap(field_re[block]))
            im = jnp.where(left_chunk, field_im[block], swap(field_im[block]))
            grads.append((re, im, re + im))
        sums = [joined(field_re, field_im, block) for block in range(blocks)]
        joins = []
        for block in range(blocks):
            parts = []
            for part in range(2):
                far = sums[block - half][part] if block >= half else 0.0
                parts.append(jnp.where(left_chunk, swap(sums[block][part]), far))
            re, im = parts
            joins.append((re, -im - re, re - im))
        for block in range(blocks):
            for part, at in ((0, real_at), (1, imag_at)):
                spectra[block, at, :] = jnp.where(
                    left_chunk, outs[blocks - 1 - block][part], outs[block][part]
                )
        for lag in range(half):
            out = products([(grads[block], joins[block - lag]) for block in range(lag, blocks)])
            filters[lag, real_at, :] = out[0]
            filters[lag, imag_at, :] = out[1]

    def even(step, _):
        spectral(step, 1)
        return 0

    def odd(step, _):
        spectral(step, -1)
        return 0

    steps = rows // chunk
    lax.fori_loop(0, steps // 2, even, 0)
    lax.fori_loop(steps // 2, steps, odd, 0)

    def back(values, buffer):
        for side, value in enumerate(values):
            head, tail = head_tail(value)
            at = pl.ds(side * LANES, LANES)
            rhs_back[buffer, pl.ds(0, 2 * rows), at] = head
            rhs_back[buffer, pl.ds(2 * rows, 2 * rows), at] = tail
            rhs_back[buffer, pl.ds(4 * rows, 2 * rows), at] = head
        result = jnp.dot(inverse_ref[...], rhs_back[buffer], preferred_element_type=jnp.float32)
        return result[:, :LANES], result[:, LANES:]

    def filter_grads(pair, _):
        values = filters[2 * pair], filters[2 * pair + 1]
        for side, value in enumerate(back(values, pair if unrolled else 0)):
            filters[2 * pair + side, pl.ds(0, rows), :] = value * grad_scale
        return 0

    loop(half // 2, filter_grads, 0, unrolled)

    def fold(value):
        return jnp.sum(value.reshape(rows // 8, 8, LANES), axis=0)

    def outputs(pair, totals):
        values = [spectra[(2 * pair + side) ^ place] for side in range(2)]
        results = back(values, (half // 2 + pair) if unrolled else 0)
        for side, result in enumerate(results):
            index = 2 * pair + side
            block = index ^ place
            out_ref = piece(out_refs, index, place)
            field = fields[index]
            result = result + gain * field
            scale = scale_of(result)
            out_ref[pl.ds(0, rows), :] = encode(result, scale).astype(jnp.bfloat16)
            misc[index, 0:1, :] = scale
            starts[block] = result[:8]
            turned = swap(result)
            grads = (second_ref[index] * turned, first_ref[index] * turned)
            new_totals = []
            for stream in (0, 1):
                for offset in range(3):
                    earlier = edged[index, stream, pl.ds(8 - offset, rows), :]
                    total = totals[3 * stream + offset]
                    new_totals.append(total + fold(grads[stream] * earlier))
            new_totals.append(totals[6] + fold(field * swap(field)))
            totals = tuple(new_totals)

            upper_half = block // half
            value = filters[lax.rem(block, half), pl.ds(0, rows), :]
            halves = join(left_half, value[:half_rows], value[half_rows:], upper_half)
            scale = scale_of(halves)
            code = encode(halves, scale).astype(jnp.bfloat16)
            out_ref[pl.ds(rows, half_rows), :] = code
            misc[index, 1:2, :] = scale
        return totals

    starts[blocks] = nothing
    totals = loop(half, outputs, (nothing,) * 7, unrolled)
    sums = [grad_scale * jnp.sum(total, axis=0, keepdims=True) for total in totals]
    shared[0:6, :] = taps[0:6]
    for row in range(6):
        value = sums[row]
        if row == 3:
            value = jnp.where(left_lanes((1, LANES)), sums[6], value)
        shared[6 + row : 7 + row, :] = value

    def close(index, _):
        out_ref = piece(out_refs, index, place)
        block = index ^ place
        misc[index, 2:4, :] = starts[block + 1, 0:2, :]
        misc[index, 4:16, :] = shared[0:12, :]
        head, tail = head_tail(misc[index])
        here = rows + half_rows
        out_ref[pl.ds(here, MISC), :] = head
        out_ref[pl.ds(here + MISC, MISC), :] = tail
        near = jnp.concatenate([ends[block, 0:4, :], ends[block + 2, 4:8, :], nothing], axis=0)
        out_ref[pl.ds(here + 2 * MISC, ENDS), :] = near.astype(jnp.bfloat16)
        return 0

    loop(blocks, close, 0, unrolled)


def operator(taps, received, devices):
    count = len(received)
    blocks = devices
    rows = (received[0].shape[-2] - 16) * 2 // 5
    forward, inverse = transform_matrices(rows)
    wide = (blocks, rows, LANES)
    listed = count > 1

    def kernel(*refs):
        ins, (forward_ref, inverse_ref, taps_ref) = refs[:count], refs[count : count + 3]
        outs, scratch = refs[count + 3 : 2 * count + 3], refs[2 * count + 3 :]
        operator_kernel(ins, outs, forward_ref, inverse_ref, taps_ref, *scratch)

    return pl.pallas_call(
        kernel,
        out_shape=piece_shapes(devices, rows + rows // 2 + 2 * MISC + ENDS),
        scratch_shapes=[
            pltpu.VMEM((blocks + 2, 8, LANES), jnp.float32),
            pltpu.VMEM((blocks + 1, 8, LANES), jnp.float32),
            pltpu.VMEM((blocks, 2, rows + 8, LANES), jnp.float32),
            pltpu.VMEM(wide, jnp.float32),
            pltpu.VMEM(wide, jnp.float32),
            pltpu.VMEM(wide, jnp.float32),
            pltpu.VMEM((blocks, 2 * rows, LANES), jnp.float32),
            pltpu.VMEM((blocks, 2 * rows, LANES), jnp.float32),
            pltpu.VMEM((blocks if listed else 2, 3 * rows, 2 * LANES), jnp.bfloat16),
            pltpu.VMEM((3 * blocks // 4 if listed else 1, 6 * rows, 2 * LANES), jnp.bfloat16),
            pltpu.VMEM((16, LANES), jnp.float32),
            pltpu.VMEM((blocks, MISC, LANES), jnp.float32),
        ],
        compiler_params=pltpu.CompilerParams(
            vmem_limit_bytes=min(4 * blocks * MEBIBYTE, VMEM_BYTES)
        ),
    )(*in_order(received), jnp.asarray(forward), jnp.asarray(inverse), taps)


def own_taps(short_taps, skip_gain):
    places = lax.axis_size("seq")
    columns = lax.axis_size("chan")
    share = skip_gain.shape[0]

    def pair(one, two):
        fill = ((0, 0), (0, HALF - share))
        return jnp.concatenate([jnp.pad(one, fill), jnp.pad(two, fill)], axis=1)

    straight = jnp.concatenate([jnp.ones((1, share)), jnp.zeros((2, share))]).astype(jnp.float32)
    rows = jnp.concatenate(
        [
            pair(short_taps[0], short_taps[1]),
            pair(straight, short_taps[2]),
            pair(skip_gain[None], skip_gain[None]),
            jnp.zeros((1, LANES), jnp.float32),
        ]
    )
    route = [
        (flat, (flat % places) * columns + flat // places) for flat in range(places * columns)
    ]
    return lax.ppermute(rows, ("seq", "chan"), route)


def spread(value, devices):
    rows, channels = value.shape
    share = channels // devices
    if share == HALF:
        return value
    wide = jnp.pad(value.reshape(rows, devices, share), ((0, 0), (0, 0), (0, HALF - share)))
    return wide.reshape(rows, devices * HALF)


def gathered(value, share):
    if share == HALF:
        return value
    groups = value.reshape(*value.shape[:-1], value.shape[-1] // HALF, HALF)[..., :share]
    return groups.reshape(*value.shape[:-1], -1)


def per_device(query_rows, key_rows, value_rows, long_filter, short_taps, skip_gain, cotangent):
    devices = lax.axis_size("seq")
    share = query_rows.shape[1] // devices
    taps = own_taps(short_taps, skip_gain)
    streams = [spread(value, devices) for value in (query_rows, key_rows, value_rows)]
    upstream = spread(cotangent, devices)
    received = exchange(pack(streams, upstream, spread(long_filter, devices), devices))
    results = exchange(operator(taps, received, devices))
    outs = finish(results, streams, upstream)
    *outs, skip_grad = (gathered(value, share) for value in outs)
    return (*outs, skip_grad[0])


def solution(mesh):
    in_specs = (
        P("seq", "chan"),
        P("seq", "chan"),
        P("seq", "chan"),
        P("seq", "chan"),
        P(None, None, ("seq", "chan")),
        P(("seq", "chan")),
        P("seq", "chan"),
    )
    out_specs = (
        P("seq", "chan"),
        P("seq", "chan"),
        P("seq", "chan"),
        P("seq", "chan"),
        P("seq", "chan"),
        P(None, None, "chan"),
        P("chan"),
    )
    return jax.shard_map(
        per_device, mesh=mesh, in_specs=in_specs, out_specs=out_specs, check_vma=False
    )
```

```python
import math

import jax
import jax.numpy as jnp
import numpy as np
from jax import lax
from jax.experimental import pallas as pl
from jax.experimental.pallas import tpu as pltpu
from jax.sharding import PartitionSpec as P

HALF = 64
LANES = 2 * HALF
ENDS = 16
MISC = 16
SPAN = 252.0
FLOOR = 125.0
MEBIBYTE = 1024 * 1024
VMEM_BYTES = 62 * MEBIBYTE
LISTED = 8
OUT_ORDER = (0, 7, 6, 3, 2, 5, 4, 1)
BACK_ORDER = (0, 7, 6, 4, 2, 5, 3, 1)


def swap(value):
    return pltpu.roll(value, HALF, 1)


def left_lanes(shape):
    return lax.broadcasted_iota(jnp.int32, shape, 1) < HALF


def head_tail(value):
    head = value.astype(jnp.bfloat16)
    tail = (value - head.astype(jnp.float32)).astype(jnp.bfloat16)
    return head, tail


def transform_matrices(rows):
    freq = np.concatenate([np.arange(0, rows, 2), np.arange(1, rows, 2)])
    turn = (2 * freq[:, None] + 1) * np.arange(rows)[None, :] % (4 * rows)
    theta = turn * (math.pi / (2 * rows))
    forward = np.concatenate([np.cos(theta), -np.sin(theta)])
    inverse = forward.T / rows

    def split(matrix):
        single = matrix.astype(np.float32)
        head = single.astype(jnp.bfloat16)
        tail = (single - head.astype(np.float32)).astype(jnp.bfloat16)
        return np.concatenate([head, head, tail], axis=1)

    return split(forward), split(inverse)


def encode(value, scale):
    code = jnp.exp2(jnp.abs(value) * (SPAN / scale) - FLOOR)
    return jnp.where(value < 0.0, -code, code)


def decode(code, scale):
    size = (jnp.log2(jnp.abs(code)) + FLOOR) * (scale * (1.0 / SPAN))
    return jnp.where(code < 0.0, -size, size)


def scale_of(value):
    peak = jnp.max(jnp.abs(value), axis=0, keepdims=True)
    return jnp.maximum(peak * 1.0001, 1e-30)


def loop(count, body, carry, unrolled):
    if unrolled:
        for index in range(count):
            carry = body(index, carry)
        return carry
    return lax.fori_loop(0, count, body, carry)


def piece(refs, index, place):
    return refs[index] if len(refs) > 1 else refs[0].at[index ^ place]


def exchange(pieces):
    if len(pieces) == 1:
        return [lax.all_to_all(pieces[0], "seq", 0, 0, tiled=True)]
    others = [
        lax.ppermute(value, "seq", [(one, one ^ index) for one in range(len(pieces))])
        for index, value in enumerate(pieces[1:], 1)
    ]
    return [pieces[0], *others]


def in_order(pieces, order):
    return [pieces[index] for index in order] if len(pieces) > 1 else pieces


def by_index(refs, order):
    if len(refs) == 1:
        return refs
    return [refs[order.index(index)] for index in range(len(refs))]


def piece_shapes(devices, rows):
    if devices == LISTED:
        return [jax.ShapeDtypeStruct((rows, LANES), jnp.bfloat16)] * devices
    return [jax.ShapeDtypeStruct((devices, rows, LANES), jnp.bfloat16)]


def join(mask, one, two, side):
    return jnp.where(mask, pltpu.roll(one, side * HALF, 1), pltpu.roll(two, HALF - side * HALF, 1))


def pack_kernel(query_ref, key_ref, value_ref, cot_ref, filter_ref, *out_refs):
    rows, channels = query_ref.shape
    devices = channels // HALF
    half = rows // 2
    place = lax.axis_index("seq")
    left = left_lanes((rows, LANES))
    left_half = left_lanes((half, LANES))

    def one_piece(index, _):
        out_ref = piece(out_refs, index, place)
        dest = index ^ place
        side = lax.rem(dest, 2)
        at = pl.ds(pl.multiple_of(dest // 2 * LANES, LANES), LANES)
        for first, second, start in ((query_ref, key_ref, 0), (cot_ref, value_ref, rows)):
            one = first[:, at].astype(jnp.float32)
            two = second[:, at].astype(jnp.float32)
            out_ref[pl.ds(start, rows), :] = join(left, one, two, side).astype(jnp.bfloat16)
        upper = filter_ref[pl.ds(0, half), at]
        lower = filter_ref[pl.ds(half, half), at]
        pair = join(left_half, upper, lower, side)
        scale = scale_of(pair)
        out_ref[pl.ds(2 * rows, half), :] = encode(pair, scale).astype(jnp.bfloat16)
        head, tail = head_tail(jnp.broadcast_to(scale, (8, LANES)))
        both = jnp.concatenate([head.astype(jnp.float32), tail.astype(jnp.float32)], axis=0)
        out_ref[pl.ds(2 * rows + half, 16), :] = both.astype(jnp.bfloat16)
        return 0

    loop(devices, one_piece, 0, len(out_refs) > 1)


def pack(streams, cotangent, long_filter, devices):
    rows = cotangent.shape[0]
    return pl.pallas_call(
        pack_kernel,
        out_shape=piece_shapes(devices, 2 * rows + rows // 2 + 16),
        compiler_params=pltpu.CompilerParams(vmem_limit_bytes=VMEM_BYTES),
    )(*streams, cotangent, long_filter)


def finish_kernel(
    pieces, query_ref, key_ref, value_ref, cot_ref, gated_out, query_out, key_out, value_out,
    filter_out, taps_out, skip_out, before, after,
):
    in_refs = by_index(pieces, BACK_ORDER)
    rows, channels = query_ref.shape
    half = rows // 2
    place = lax.axis_index("seq")
    odd = lax.rem(place, 2) == 1
    left = left_lanes((rows, LANES))
    left_half = left_lanes((half, LANES))
    left_misc = left_lanes((MISC, LANES))

    def one_tile(step, _):
        refs = piece(in_refs, 2 * step, place), piece(in_refs, 2 * step + 1, place)
        at = pl.ds(pl.multiple_of((step ^ (place // 2)) * LANES, LANES), LANES)

        def both(start, count):
            one, two = (ref[pl.ds(start, count), :].astype(jnp.float32) for ref in refs)
            return jnp.where(odd, two, one), jnp.where(odd, one, two)

        def sides(mask, values):
            one, two = values
            return jnp.where(mask, one, swap(two)), jnp.where(mask, swap(one), two)

        miscs = [
            head + tail
            for head, tail in zip(both(rows + half, MISC), both(rows + half + MISC, MISC))
        ]
        codes = both(0, rows)
        back, mixed = sides(left, [decode(code, misc[0:1]) for code, misc in zip(codes, miscs)])
        codes = both(rows, half)
        upper, lower = sides(
            left_half, [decode(code, misc[1:2]) for code, misc in zip(codes, miscs)]
        )
        filter_out[pl.ds(0, half), at] = upper
        filter_out[pl.ds(half, half), at] = lower
        ends = sides(left_misc, both(rows + half + 2 * MISC, ENDS))
        lefts, rights = sides(left_misc, miscs)
        taps = (lefts[4:7], rights[4:7], rights[7:10])
        for offset in range(3):
            taps_out[0, offset : offset + 1, at] = lefts[10 + offset : 11 + offset]
            taps_out[1, offset : offset + 1, at] = rights[10 + offset : 11 + offset]
            taps_out[2, offset : offset + 1, at] = rights[13 + offset : 14 + offset]
        skip_out[0:1, at] = lefts[13:14]
        back_edge, mixed_edge = lefts[2:4], rights[2:4]
        convs, edges = [], []
        for stream, (source, end, row) in enumerate(
            ((query_ref, ends[0], 0), (key_ref, ends[1], 0), (value_ref, ends[1], 2))
        ):
            now = source[:, at].astype(jnp.float32)
            before[stream, 6:8, :] = end[row : row + 2]
            before[stream, pl.ds(8, rows), :] = now
            before[stream, pl.ds(8 + rows, 2), :] = end[row + 4 : row + 6]
            conv = taps[stream][0:1] * now
            edge = taps[stream][0:1] * end[row + 4 : row + 6]
            for offset in (1, 2):
                weight = taps[stream][offset : offset + 1]
                conv = conv + weight * before[stream, pl.ds(8 - offset, rows), :]
                edge = edge + weight * before[stream, pl.ds(8 + rows - offset, 2), :]
            convs.append(conv)
            edges.append(edge)
        cotangent = cot_ref[:, at].astype(jnp.float32)
        cot_edge = ends[0][6:8]
        gated_out[:, at] = (convs[0] * mixed).astype(jnp.bfloat16)
        for stream, (out, grad, edge) in enumerate(
            (
                (query_out, cotangent * mixed, cot_edge * mixed_edge),
                (key_out, back * convs[2], back_edge * edges[2]),
                (value_out, back * convs[1], back_edge * edges[1]),
            )
        ):
            after[stream, pl.ds(0, rows), :] = grad
            after[stream, pl.ds(rows, 2), :] = edge
            total = taps[stream][0:1] * grad
            for offset in (1, 2):
                weight = taps[stream][offset : offset + 1]
                total = total + weight * after[stream, pl.ds(offset, rows), :]
            out[:, at] = total.astype(jnp.bfloat16)
        return 0

    loop(channels // LANES, one_tile, 0, len(in_refs) > 1)


def finish(received, streams, cotangent):
    rows, channels = cotangent.shape
    count = len(received)
    low = jax.ShapeDtypeStruct((rows, channels), jnp.bfloat16)

    def kernel(*refs):
        finish_kernel(refs[:count], *refs[count:])

    return pl.pallas_call(
        kernel,
        out_shape=(
            low,
            low,
            low,
            low,
            jax.ShapeDtypeStruct((rows, channels), jnp.float32),
            jax.ShapeDtypeStruct((3, 3, channels), jnp.float32),
            jax.ShapeDtypeStruct((1, channels), jnp.float32),
        ),
        scratch_shapes=[
            pltpu.VMEM((3, rows + 16, LANES), jnp.float32),
            pltpu.VMEM((3, rows + 8, LANES), jnp.float32),
        ],
        compiler_params=pltpu.CompilerParams(
            vmem_limit_bytes=3 * (channels // HALF) * MEBIBYTE // 2
        ),
    )(*in_order(received, BACK_ORDER), *streams, cotangent)


def operator_kernel(
    pieces, out_refs, forward_ref, inverse_ref, taps_ref,
    ends, starts, edged, first_ref, second_ref, fields, spectra, filters, rhs, rhs_back,
    shared, misc,
):
    in_refs = by_index(pieces, OUT_ORDER)
    blocks = fields.shape[0]
    place = lax.axis_index("seq")
    rows = forward_ref.shape[0] // 2
    half = blocks // 2
    half_rows = rows // 2
    unrolled = len(in_refs) > 1
    grad_scale = 1.0 / math.sqrt(blocks * rows)
    left = left_lanes((rows, LANES))
    left_half = left_lanes((half_rows, LANES))
    taps = taps_ref[...]
    query_taps = [taps[i : i + 1] for i in range(3)]
    value_taps = [taps[3 + i : 4 + i] for i in range(3)]
    gain = taps[6:7]
    nothing = jnp.zeros((8, LANES), jnp.float32)

    def lay(buffer, side, place, value):
        head, tail = head_tail(value)
        count = value.shape[0]
        at = pl.ds(side * LANES, LANES)
        rhs[buffer, pl.ds(place, count), at] = head
        rhs[buffer, pl.ds(rows + place, count), at] = tail
        rhs[buffer, pl.ds(2 * rows + place, count), at] = head

    def transformed(buffer):
        return jnp.dot(forward_ref[...], rhs[buffer], preferred_element_type=jnp.float32)

    def keep_ends(index, _):
        ref = piece(in_refs, index, place)
        block = index ^ place
        for stream in (0, 1):
            start = stream * rows
            last = ref[pl.ds(start + rows - 16, 16), :].astype(jnp.float32)
            first = ref[pl.ds(start, 16), :].astype(jnp.float32)
            ends[block + 1, 2 * stream : 2 * stream + 2, :] = last[14:16]
            ends[block + 1, 2 * stream + 4 : 2 * stream + 6, :] = first[0:2]
        return 0

    ends[0] = nothing
    ends[blocks + 1] = nothing
    loop(blocks, keep_ends, 0, unrolled)

    def transform(pair, _):
        spot = 2 * pair if unrolled else 0
        for side in range(2):
            ref = piece(in_refs, 2 * pair + side, place)
            scale = ref[pl.ds(2 * rows + half_rows, 16), :].astype(jnp.float32)
            code = ref[pl.ds(2 * rows, half_rows), :].astype(jnp.float32)
            taken = decode(code, scale[0:1] + scale[8:9])
            turned = swap(taken)
            lay(spot, side, 0, jnp.where(left_half, taken, turned))
            lay(spot, side, half_rows, jnp.where(left_half, turned, taken))
        result = transformed(spot)
        for side in range(2):
            filters[(2 * pair + side) ^ place] = result[:, side * LANES : (side + 1) * LANES]
        for side in range(2):
            index = 2 * pair + side
            ref = piece(in_refs, index, place)
            outs = []
            for stream, weights in ((0, query_taps), (1, value_taps)):
                now = ref[pl.ds(stream * rows, rows), :].astype(jnp.float32)
                last = ends[index ^ place, 2 * stream : 2 * stream + 2, :]
                edged[index, stream, 6:8, :] = last
                edged[index, stream, pl.ds(8, rows), :] = now
                total = weights[0] * now
                for offset in (1, 2):
                    shifted = edged[index, stream, pl.ds(8 - offset, rows), :]
                    total = total + weights[offset] * shifted
                outs.append(total)
            first_ref[index] = outs[0]
            second_ref[index] = outs[1]
            field = outs[0] * outs[1]
            fields[index] = field
            lay(spot + 1, side, 0, field)
        result = transformed(spot + 1)
        for side in range(2):
            spectra[(2 * pair + side) ^ place] = result[:, side * LANES : (side + 1) * LANES]
        return 0

    loop(half, transform, 0, unrolled)

    chunk = 8
    left_chunk = left_lanes((chunk, LANES))
    conjugate = jnp.where(left_chunk, -1.0, 1.0)

    def products(pairs):
        one = two = three = None
        for (re, im, both), (join_re, join_less, join_more) in pairs:
            terms = join_re * both, re * join_less, im * join_more
            if one is None:
                one, two, three = terms
            else:
                one, two, three = one + terms[0], two + terms[1], three + terms[2]
        return one - three, one + two

    def spectral(step, sign):
        real_at = pl.ds(pl.multiple_of(step * chunk, chunk), chunk)
        imag_at = pl.ds(pl.multiple_of(rows + step * chunk, chunk), chunk)
        field_re = [spectra[block, real_at, :] for block in range(blocks)]
        field_im = [spectra[block, imag_at, :] for block in range(blocks)]

        def joined(re, im, block):
            if block == 0:
                return re[0], im[0]
            if sign > 0:
                return re[block] - im[block - 1], im[block] + re[block - 1]
            return re[block] + im[block - 1], im[block] - re[block - 1]

        turned = []
        for block in range(blocks):
            re = jnp.where(left_chunk, field_re[blocks - 1 - block], field_re[block])
            im = jnp.where(left_chunk, field_im[blocks - 1 - block], field_im[block])
            turned.append((re, im, re + im))
        filt_re = [filters[block, real_at, :] for block in range(blocks)]
        filt_im = [filters[block, imag_at, :] for block in range(blocks)]
        joins = []
        for block in range(blocks):
            re, im = joined(filt_re, filt_im, block)
            im = im * conjugate
            joins.append((re, im - re, re + im))
        outs = [
            products([(turned[block - lag], joins[lag]) for lag in range(block + 1)])
            for block in range(blocks)
        ]
        grads = []
        for block in range(blocks):
            re = jnp.where(left_chunk, field_re[block], swap(field_re[block]))
            im = jnp.where(left_chunk, field_im[block], swap(field_im[block]))
            grads.append((re, im, re + im))
        sums = [joined(field_re, field_im, block) for block in range(blocks)]
        joins = []
        for block in range(blocks):
            parts = []
            for part in range(2):
                far = sums[block - half][part] if block >= half else 0.0
                parts.append(jnp.where(left_chunk, swap(sums[block][part]), far))
            re, im = parts
            joins.append((re, -im - re, re - im))
        for block in range(blocks):
            for part, at in ((0, real_at), (1, imag_at)):
                spectra[block, at, :] = jnp.where(
                    left_chunk, outs[blocks - 1 - block][part], outs[block][part]
                )
        for lag in range(half):
            out = products([(grads[block], joins[block - lag]) for block in range(lag, blocks)])
            filters[lag, real_at, :] = out[0]
            filters[lag, imag_at, :] = out[1]

    trips = rows // chunk // 4

    def even(trip, _):
        for part in range(2):
            spectral(2 * trip + part, 1)
        return 0

    def odd(trip, _):
        for part in range(2):
            spectral(2 * trip + part, -1)
        return 0

    lax.fori_loop(0, trips, even, 0)
    lax.fori_loop(trips, 2 * trips, odd, 0)

    def back(values, buffer):
        for side, value in enumerate(values):
            head, tail = head_tail(value)
            at = pl.ds(side * LANES, LANES)
            rhs_back[buffer, pl.ds(0, 2 * rows), at] = head
            rhs_back[buffer, pl.ds(2 * rows, 2 * rows), at] = tail
            rhs_back[buffer, pl.ds(4 * rows, 2 * rows), at] = head
        result = jnp.dot(inverse_ref[...], rhs_back[buffer], preferred_element_type=jnp.float32)
        return result[:, :LANES], result[:, LANES:]

    def filter_grads(pair, _):
        values = filters[2 * pair], filters[2 * pair + 1]
        for side, value in enumerate(back(values, pair if unrolled else 0)):
            filters[2 * pair + side, pl.ds(0, rows), :] = value * grad_scale
        return 0

    loop(half // 2, filter_grads, 0, unrolled)

    def fold(value):
        return jnp.sum(value.reshape(rows // 8, 8, LANES), axis=0)

    def outputs(pair, totals):
        values = [spectra[(2 * pair + side) ^ place] for side in range(2)]
        results = back(values, (half // 2 + pair) if unrolled else 0)
        for side, result in enumerate(results):
            index = 2 * pair + side
            block = index ^ place
            out_ref = piece(out_refs, index, place)
            field = fields[index]
            result = result + gain * field
            scale = scale_of(result)
            out_ref[pl.ds(0, rows), :] = encode(result, scale).astype(jnp.bfloat16)
            misc[index, 0:1, :] = scale
            starts[block] = result[:8]
            turned = swap(result)
            grads = (second_ref[index] * turned, first_ref[index] * turned)
            new_totals = []
            for stream in (0, 1):
                for offset in range(3):
                    earlier = edged[index, stream, pl.ds(8 - offset, rows), :]
                    total = totals[3 * stream + offset]
                    new_totals.append(total + fold(grads[stream] * earlier))
            new_totals.append(totals[6] + fold(field * swap(field)))
            totals = tuple(new_totals)

            upper_half = block // half
            value = filters[lax.rem(block, half), pl.ds(0, rows), :]
            halves = join(left_half, value[:half_rows], value[half_rows:], upper_half)
            scale = scale_of(halves)
            code = encode(halves, scale).astype(jnp.bfloat16)
            out_ref[pl.ds(rows, half_rows), :] = code
            misc[index, 1:2, :] = scale
        return totals

    starts[blocks] = nothing
    totals = loop(half, outputs, (nothing,) * 7, unrolled)
    sums = [grad_scale * jnp.sum(total, axis=0, keepdims=True) for total in totals]
    shared[0:6, :] = taps[0:6]
    for row in range(6):
        value = sums[row]
        if row == 3:
            value = jnp.where(left_lanes((1, LANES)), sums[6], value)
        shared[6 + row : 7 + row, :] = value

    def close(index, _):
        out_ref = piece(out_refs, index, place)
        block = index ^ place
        misc[index, 2:4, :] = starts[block + 1, 0:2, :]
        misc[index, 4:16, :] = shared[0:12, :]
        head, tail = head_tail(misc[index])
        here = rows + half_rows
        out_ref[pl.ds(here, MISC), :] = head
        out_ref[pl.ds(here + MISC, MISC), :] = tail
        near = jnp.concatenate([ends[block, 0:4, :], ends[block + 2, 4:8, :], nothing], axis=0)
        out_ref[pl.ds(here + 2 * MISC, ENDS), :] = near.astype(jnp.bfloat16)
        return 0

    loop(blocks, close, 0, unrolled)


def operator(taps, received, devices):
    count = len(received)
    blocks = devices
    rows = (received[0].shape[-2] - 16) * 2 // 5
    forward, inverse = transform_matrices(rows)
    wide = (blocks, rows, LANES)
    listed = count > 1

    def kernel(*refs):
        ins, (forward_ref, inverse_ref, taps_ref) = refs[:count], refs[count : count + 3]
        outs, scratch = refs[count + 3 : 2 * count + 3], refs[2 * count + 3 :]
        operator_kernel(ins, outs, forward_ref, inverse_ref, taps_ref, *scratch)

    return pl.pallas_call(
        kernel,
        out_shape=piece_shapes(devices, rows + rows // 2 + 2 * MISC + ENDS),
        scratch_shapes=[
            pltpu.VMEM((blocks + 2, 8, LANES), jnp.float32),
            pltpu.VMEM((blocks + 1, 8, LANES), jnp.float32),
            pltpu.VMEM((blocks, 2, rows + 8, LANES), jnp.float32),
            pltpu.VMEM(wide, jnp.float32),
            pltpu.VMEM(wide, jnp.float32),
            pltpu.VMEM(wide, jnp.float32),
            pltpu.VMEM((blocks, 2 * rows, LANES), jnp.float32),
            pltpu.VMEM((blocks, 2 * rows, LANES), jnp.float32),
            pltpu.VMEM((blocks if listed else 2, 3 * rows, 2 * LANES), jnp.bfloat16),
            pltpu.VMEM((3 * blocks // 4 if listed else 1, 6 * rows, 2 * LANES), jnp.bfloat16),
            pltpu.VMEM((16, LANES), jnp.float32),
            pltpu.VMEM((blocks, MISC, LANES), jnp.float32),
        ],
        compiler_params=pltpu.CompilerParams(
            vmem_limit_bytes=min(4 * blocks * MEBIBYTE, VMEM_BYTES)
        ),
    )(*in_order(received, OUT_ORDER), jnp.asarray(forward), jnp.asarray(inverse), taps)


def own_taps(short_taps, skip_gain, received):
    places = lax.axis_size("seq")
    columns = lax.axis_size("chan")
    share = skip_gain.shape[0]

    def pair(one, two):
        fill = ((0, 0), (0, HALF - share))
        return jnp.concatenate([jnp.pad(one, fill), jnp.pad(two, fill)], axis=1)

    straight = jnp.concatenate([jnp.ones((1, share)), jnp.zeros((2, share))]).astype(jnp.float32)
    rows = jnp.concatenate(
        [
            pair(short_taps[0], short_taps[1]),
            pair(straight, short_taps[2]),
            pair(skip_gain[None], skip_gain[None]),
            jnp.zeros((1, LANES), jnp.float32),
        ]
    )
    route = [
        (flat, (flat % places) * columns + flat // places) for flat in range(places * columns)
    ]
    if len(received) > 1:
        rows, received[-1] = lax.optimization_barrier((rows, received[-1]))
    return lax.ppermute(rows, ("seq", "chan"), route), received


def spread(value, devices):
    rows, channels = value.shape
    share = channels // devices
    if share == HALF:
        return value
    wide = jnp.pad(value.reshape(rows, devices, share), ((0, 0), (0, 0), (0, HALF - share)))
    return wide.reshape(rows, devices * HALF)


def gathered(value, share):
    if share == HALF:
        return value
    groups = value.reshape(*value.shape[:-1], value.shape[-1] // HALF, HALF)[..., :share]
    return groups.reshape(*value.shape[:-1], -1)


def per_device(query_rows, key_rows, value_rows, long_filter, short_taps, skip_gain, cotangent):
    devices = lax.axis_size("seq")
    share = query_rows.shape[1] // devices
    streams = [spread(value, devices) for value in (query_rows, key_rows, value_rows)]
    upstream = spread(cotangent, devices)
    received = exchange(pack(streams, upstream, spread(long_filter, devices), devices))
    taps, received = own_taps(short_taps, skip_gain, received)
    results = exchange(operator(taps, received, devices))
    outs = finish(results, streams, upstream)
    *outs, skip_grad = (gathered(value, share) for value in outs)
    return (*outs, skip_grad[0])


def solution(mesh):
    in_specs = (
        P("seq", "chan"),
        P("seq", "chan"),
        P("seq", "chan"),
        P("seq", "chan"),
        P(None, None, ("seq", "chan")),
        P(("seq", "chan")),
        P("seq", "chan"),
    )
    out_specs = (
        P("seq", "chan"),
        P("seq", "chan"),
        P("seq", "chan"),
        P("seq", "chan"),
        P("seq", "chan"),
        P(None, None, "chan"),
        P("chan"),
    )
    return jax.shard_map(
        per_device, mesh=mesh, in_specs=in_specs, out_specs=out_specs, check_vma=False
    )
```

```python
import functools
import math

import jax
import jax.numpy as jnp
import numpy as np
from jax import lax
from jax.experimental import pallas as pl
from jax.experimental.pallas import tpu as pltpu
from jax.sharding import PartitionSpec as P

HALF = 64
LANES = 2 * HALF
ENDS = 16
MISC = 16
SPAN = 252.0
FLOOR = 125.0
MEBIBYTE = 1024 * 1024
VMEM_BYTES = 62 * MEBIBYTE
LISTED = 8
OUT_ORDER = (0, 7, 6, 3, 2, 5, 4, 1)
PACK_STEPS = ((3,), (1, 2, 0))
BACK_ORDER = (0, 7, 6, 4, 2, 5, 3, 1)


def swap(value):
    return pltpu.roll(value, HALF, 1)


def left_lanes(shape):
    return lax.broadcasted_iota(jnp.int32, shape, 1) < HALF


def head_tail(value):
    head = value.astype(jnp.bfloat16)
    tail = (value - head.astype(jnp.float32)).astype(jnp.bfloat16)
    return head, tail


def transform_matrices(rows):
    freq = np.concatenate([np.arange(0, rows, 2), np.arange(1, rows, 2)])
    turn = (2 * freq[:, None] + 1) * np.arange(rows)[None, :] % (4 * rows)
    theta = turn * (math.pi / (2 * rows))
    forward = np.concatenate([np.cos(theta), -np.sin(theta)])
    inverse = forward.T / rows

    def split(matrix):
        single = matrix.astype(np.float32)
        head = single.astype(jnp.bfloat16)
        tail = (single - head.astype(np.float32)).astype(jnp.bfloat16)
        return np.concatenate([head, head, tail], axis=1)

    return split(forward), split(inverse)


def encode(value, scale):
    code = jnp.exp2(jnp.abs(value) * (SPAN / scale) - FLOOR)
    return jnp.where(value < 0.0, -code, code)


def decode(code, scale):
    size = (jnp.log2(jnp.abs(code)) + FLOOR) * (scale * (1.0 / SPAN))
    return jnp.where(code < 0.0, -size, size)


def scale_of(value):
    peak = jnp.max(jnp.abs(value), axis=0, keepdims=True)
    return jnp.maximum(peak * 1.0001, 1e-30)


def loop(count, body, carry, unrolled):
    if unrolled:
        for index in range(count):
            carry = body(index, carry)
        return carry
    return lax.fori_loop(0, count, body, carry)


def piece(refs, index, place):
    return refs[index] if len(refs) > 1 else refs[0].at[index ^ place]


def exchange(pieces):
    if len(pieces) == 1:
        return [lax.all_to_all(pieces[0], "seq", 0, 0, tiled=True)]
    others = [
        lax.ppermute(value, "seq", [(one, one ^ index) for one in range(len(pieces))])
        for index, value in enumerate(pieces[1:], 1)
    ]
    return [pieces[0], *others]


def in_order(pieces, order):
    return [pieces[index] for index in order] if len(pieces) > 1 else pieces


def by_index(refs, order):
    if len(refs) == 1:
        return refs
    return [refs[order.index(index)] for index in range(len(refs))]


def piece_shapes(devices, rows):
    if devices == LISTED:
        return [jax.ShapeDtypeStruct((rows, LANES), jnp.bfloat16)] * devices
    return [jax.ShapeDtypeStruct((devices, rows, LANES), jnp.bfloat16)]


def join(mask, one, two, side):
    return jnp.where(mask, pltpu.roll(one, side * HALF, 1), pltpu.roll(two, HALF - side * HALF, 1))


def pack_kernel(steps, *refs):
    low_refs, filter_ref, refs = refs[:4], refs[4], refs[5:]
    low, high, staged, in_sems, out_sems = refs[-5:]
    out_refs = refs[:-5]
    rows, channels = filter_ref.shape
    devices = channels // HALF
    half = rows // 2
    place = lax.axis_index("seq")
    left = left_lanes((rows, LANES))
    left_half = left_lanes((half, LANES))
    copies = {}
    for step in steps:
        tile = step ^ (place // 2)
        at = pl.ds(pl.multiple_of(tile * LANES, LANES), LANES)
        pairs = [(ref.at[:, at], low.at[step, stream]) for stream, ref in enumerate(low_refs)]
        pairs.append((filter_ref.at[:, at], high.at[step]))
        copies[step] = [
            pltpu.make_async_copy(source, target, in_sems.at[step, stream])
            for stream, (source, target) in enumerate(pairs)
        ]
        for copy in copies[step]:
            copy.start()
    leaving = []
    for step in steps:
        for copy in copies[step]:
            copy.wait()
        for index in (2 * step + 1, 2 * step):
            side = lax.rem(index ^ place, 2)
            for first, second, start in ((0, 1, 0), (3, 2, rows)):
                one = low[step, first].astype(jnp.float32)
                two = low[step, second].astype(jnp.float32)
                joined = join(left, one, two, side).astype(jnp.bfloat16)
                staged[index, pl.ds(start, rows), :] = joined
            pair = join(left_half, high[step, :half], high[step, half:], side)
            scale = scale_of(pair)
            staged[index, pl.ds(2 * rows, half), :] = encode(pair, scale).astype(jnp.bfloat16)
            head, tail = head_tail(jnp.broadcast_to(scale, (8, LANES)))
            both = jnp.concatenate([head.astype(jnp.float32), tail.astype(jnp.float32)], axis=0)
            staged[index, pl.ds(2 * rows + half, 16), :] = both.astype(jnp.bfloat16)
            if len(out_refs) == 1:
                target = out_refs[0].at[index ^ place]
            else:
                target = out_refs[2 * steps.index(step) + index % 2]
            leaving.append(pltpu.make_async_copy(staged.at[index], target, out_sems.at[index]))
            leaving[-1].start()
    for copy in leaving:
        copy.wait()


def pack_steps(arrays, devices, steps):
    rows = arrays[-1].shape[0]
    sent_rows = 2 * rows + rows // 2 + 16
    shapes = piece_shapes(devices, sent_rows)
    if len(shapes) > 1:
        shapes = shapes[: 2 * len(steps)]
    anywhere = pl.BlockSpec(memory_space=pl.ANY)
    return pl.pallas_call(
        functools.partial(pack_kernel, steps),
        in_specs=[anywhere] * 5,
        out_specs=[anywhere] * len(shapes),
        out_shape=shapes,
        scratch_shapes=[
            pltpu.VMEM((devices // 2, 4, rows, LANES), jnp.bfloat16),
            pltpu.VMEM((devices // 2, rows, LANES), jnp.float32),
            pltpu.VMEM((devices, sent_rows, LANES), jnp.bfloat16),
            pltpu.SemaphoreType.DMA((devices // 2, 5)),
            pltpu.SemaphoreType.DMA((devices,)),
        ],
        compiler_params=pltpu.CompilerParams(vmem_limit_bytes=VMEM_BYTES),
    )(*arrays)


def pack(streams, cotangent, long_filter, devices):
    arrays = (*streams, cotangent, long_filter)
    if devices != LISTED:
        return pack_steps(arrays, devices, tuple(range(devices // 2)))
    pieces = [None] * devices
    for steps in PACK_STEPS:
        made = pack_steps(arrays, devices, steps)
        for at, step in enumerate(steps):
            pieces[2 * step], pieces[2 * step + 1] = made[2 * at], made[2 * at + 1]
    return pieces


def finish_kernel(
    pieces, query_ref, key_ref, value_ref, cot_ref, gated_out, query_out, key_out, value_out,
    filter_out, taps_out, skip_out, before, after,
):
    in_refs = by_index(pieces, BACK_ORDER)
    rows, channels = query_ref.shape
    half = rows // 2
    place = lax.axis_index("seq")
    odd = lax.rem(place, 2) == 1
    left = left_lanes((rows, LANES))
    left_half = left_lanes((half, LANES))
    left_misc = left_lanes((MISC, LANES))

    def one_tile(step, _):
        refs = piece(in_refs, 2 * step, place), piece(in_refs, 2 * step + 1, place)
        at = pl.ds(pl.multiple_of((step ^ (place // 2)) * LANES, LANES), LANES)

        def both(start, count):
            one, two = (ref[pl.ds(start, count), :].astype(jnp.float32) for ref in refs)
            return jnp.where(odd, two, one), jnp.where(odd, one, two)

        def sides(mask, values):
            one, two = values
            return jnp.where(mask, one, swap(two)), jnp.where(mask, swap(one), two)

        miscs = [
            head + tail
            for head, tail in zip(both(rows + half, MISC), both(rows + half + MISC, MISC))
        ]
        codes = both(0, rows)
        back, mixed = sides(left, [decode(code, misc[0:1]) for code, misc in zip(codes, miscs)])
        codes = both(rows, half)
        upper, lower = sides(
            left_half, [decode(code, misc[1:2]) for code, misc in zip(codes, miscs)]
        )
        filter_out[pl.ds(0, half), at] = upper
        filter_out[pl.ds(half, half), at] = lower
        ends = sides(left_misc, both(rows + half + 2 * MISC, ENDS))
        lefts, rights = sides(left_misc, miscs)
        taps = (lefts[4:7], rights[4:7], rights[7:10])
        for offset in range(3):
            taps_out[0, offset : offset + 1, at] = lefts[10 + offset : 11 + offset]
            taps_out[1, offset : offset + 1, at] = rights[10 + offset : 11 + offset]
            taps_out[2, offset : offset + 1, at] = rights[13 + offset : 14 + offset]
        skip_out[0:1, at] = lefts[13:14]
        back_edge, mixed_edge = lefts[2:4], rights[2:4]
        convs, edges = [], []
        for stream, (source, end, row) in enumerate(
            ((query_ref, ends[0], 0), (key_ref, ends[1], 0), (value_ref, ends[1], 2))
        ):
            now = source[:, at].astype(jnp.float32)
            before[stream, 6:8, :] = end[row : row + 2]
            before[stream, pl.ds(8, rows), :] = now
            before[stream, pl.ds(8 + rows, 2), :] = end[row + 4 : row + 6]
            conv = taps[stream][0:1] * now
            edge = taps[stream][0:1] * end[row + 4 : row + 6]
            for offset in (1, 2):
                weight = taps[stream][offset : offset + 1]
                conv = conv + weight * before[stream, pl.ds(8 - offset, rows), :]
                edge = edge + weight * before[stream, pl.ds(8 + rows - offset, 2), :]
            convs.append(conv)
            edges.append(edge)
        cotangent = cot_ref[:, at].astype(jnp.float32)
        cot_edge = ends[0][6:8]
        gated_out[:, at] = (convs[0] * mixed).astype(jnp.bfloat16)
        for stream, (out, grad, edge) in enumerate(
            (
                (query_out, cotangent * mixed, cot_edge * mixed_edge),
                (key_out, back * convs[2], back_edge * edges[2]),
                (value_out, back * convs[1], back_edge * edges[1]),
            )
        ):
            after[stream, pl.ds(0, rows), :] = grad
            after[stream, pl.ds(rows, 2), :] = edge
            total = taps[stream][0:1] * grad
            for offset in (1, 2):
                weight = taps[stream][offset : offset + 1]
                total = total + weight * after[stream, pl.ds(offset, rows), :]
            out[:, at] = total.astype(jnp.bfloat16)
        return 0

    loop(channels // LANES, one_tile, 0, len(in_refs) > 1)


def finish(received, streams, cotangent):
    rows, channels = cotangent.shape
    count = len(received)
    low = jax.ShapeDtypeStruct((rows, channels), jnp.bfloat16)

    def kernel(*refs):
        finish_kernel(refs[:count], *refs[count:])

    return pl.pallas_call(
        kernel,
        out_shape=(
            low,
            low,
            low,
            low,
            jax.ShapeDtypeStruct((rows, channels), jnp.float32),
            jax.ShapeDtypeStruct((3, 3, channels), jnp.float32),
            jax.ShapeDtypeStruct((1, channels), jnp.float32),
        ),
        scratch_shapes=[
            pltpu.VMEM((3, rows + 16, LANES), jnp.float32),
            pltpu.VMEM((3, rows + 8, LANES), jnp.float32),
        ],
        compiler_params=pltpu.CompilerParams(
            vmem_limit_bytes=3 * (channels // HALF) * MEBIBYTE // 2
        ),
    )(*in_order(received, BACK_ORDER), *streams, cotangent)


def operator_kernel(
    pieces, out_refs, forward_ref, inverse_ref, taps_ref,
    ends, starts, edged, first_ref, second_ref, fields, spectra, filters, rhs, rhs_back,
    shared, misc,
):
    in_refs = by_index(pieces, OUT_ORDER)
    blocks = fields.shape[0]
    place = lax.axis_index("seq")
    rows = forward_ref.shape[0] // 2
    half = blocks // 2
    half_rows = rows // 2
    unrolled = len(in_refs) > 1
    grad_scale = 1.0 / math.sqrt(blocks * rows)
    left = left_lanes((rows, LANES))
    left_half = left_lanes((half_rows, LANES))
    taps = taps_ref[...]
    query_taps = [taps[i : i + 1] for i in range(3)]
    value_taps = [taps[3 + i : 4 + i] for i in range(3)]
    gain = taps[6:7]
    nothing = jnp.zeros((8, LANES), jnp.float32)

    def lay(buffer, side, place, value):
        head, tail = head_tail(value)
        count = value.shape[0]
        at = pl.ds(side * LANES, LANES)
        rhs[buffer, pl.ds(place, count), at] = head
        rhs[buffer, pl.ds(rows + place, count), at] = tail
        rhs[buffer, pl.ds(2 * rows + place, count), at] = head

    def transformed(buffer):
        return jnp.dot(forward_ref[...], rhs[buffer], preferred_element_type=jnp.float32)

    def keep_ends(index, _):
        ref = piece(in_refs, index, place)
        block = index ^ place
        for stream in (0, 1):
            start = stream * rows
            last = ref[pl.ds(start + rows - 16, 16), :].astype(jnp.float32)
            first = ref[pl.ds(start, 16), :].astype(jnp.float32)
            ends[block + 1, 2 * stream : 2 * stream + 2, :] = last[14:16]
            ends[block + 1, 2 * stream + 4 : 2 * stream + 6, :] = first[0:2]
        return 0

    ends[0] = nothing
    ends[blocks + 1] = nothing
    loop(blocks, keep_ends, 0, unrolled)

    def transform(pair, _):
        spot = 2 * pair if unrolled else 0
        for side in range(2):
            ref = piece(in_refs, 2 * pair + side, place)
            scale = ref[pl.ds(2 * rows + half_rows, 16), :].astype(jnp.float32)
            code = ref[pl.ds(2 * rows, half_rows), :].astype(jnp.float32)
            taken = decode(code, scale[0:1] + scale[8:9])
            turned = swap(taken)
            lay(spot, side, 0, jnp.where(left_half, taken, turned))
            lay(spot, side, half_rows, jnp.where(left_half, turned, taken))
        result = transformed(spot)
        for side in range(2):
            filters[(2 * pair + side) ^ place] = result[:, side * LANES : (side + 1) * LANES]
        for side in range(2):
            index = 2 * pair + side
            ref = piece(in_refs, index, place)
            outs = []
            for stream, weights in ((0, query_taps), (1, value_taps)):
                now = ref[pl.ds(stream * rows, rows), :].astype(jnp.float32)
                last = ends[index ^ place, 2 * stream : 2 * stream + 2, :]
                edged[index, stream, 6:8, :] = last
                edged[index, stream, pl.ds(8, rows), :] = now
                total = weights[0] * now
                for offset in (1, 2):
                    shifted = edged[index, stream, pl.ds(8 - offset, rows), :]
                    total = total + weights[offset] * shifted
                outs.append(total)
            first_ref[index] = outs[0]
            second_ref[index] = outs[1]
            field = outs[0] * outs[1]
            fields[index] = field
            lay(spot + 1, side, 0, field)
        result = transformed(spot + 1)
        for side in range(2):
            spectra[(2 * pair + side) ^ place] = result[:, side * LANES : (side + 1) * LANES]
        return 0

    loop(half, transform, 0, unrolled)

    chunk = 8
    left_chunk = left_lanes((chunk, LANES))
    conjugate = jnp.where(left_chunk, -1.0, 1.0)

    def products(pairs):
        one = two = three = None
        for (re, im, both), (join_re, join_less, join_more) in pairs:
            terms = join_re * both, re * join_less, im * join_more
            if one is None:
                one, two, three = terms
            else:
                one, two, three = one + terms[0], two + terms[1], three + terms[2]
        return one - three, one + two

    def spectral(step, sign):
        real_at = pl.ds(pl.multiple_of(step * chunk, chunk), chunk)
        imag_at = pl.ds(pl.multiple_of(rows + step * chunk, chunk), chunk)
        field_re = [spectra[block, real_at, :] for block in range(blocks)]
        field_im = [spectra[block, imag_at, :] for block in range(blocks)]

        def joined(re, im, block):
            if block == 0:
                return re[0], im[0]
            if sign > 0:
                return re[block] - im[block - 1], im[block] + re[block - 1]
            return re[block] + im[block - 1], im[block] - re[block - 1]

        turned = []
        for block in range(blocks):
            re = jnp.where(left_chunk, field_re[blocks - 1 - block], field_re[block])
            im = jnp.where(left_chunk, field_im[blocks - 1 - block], field_im[block])
            turned.append((re, im, re + im))
        filt_re = [filters[block, real_at, :] for block in range(blocks)]
        filt_im = [filters[block, imag_at, :] for block in range(blocks)]
        joins = []
        for block in range(blocks):
            re, im = joined(filt_re, filt_im, block)
            im = im * conjugate
            joins.append((re, im - re, re + im))
        outs = [
            products([(turned[block - lag], joins[lag]) for lag in range(block + 1)])
            for block in range(blocks)
        ]
        grads = []
        for block in range(blocks):
            re = jnp.where(left_chunk, field_re[block], swap(field_re[block]))
            im = jnp.where(left_chunk, field_im[block], swap(field_im[block]))
            grads.append((re, im, re + im))
        sums = [joined(field_re, field_im, block) for block in range(blocks)]
        joins = []
        for block in range(blocks):
            parts = []
            for part in range(2):
                far = sums[block - half][part] if block >= half else 0.0
                parts.append(jnp.where(left_chunk, swap(sums[block][part]), far))
            re, im = parts
            joins.append((re, -im - re, re - im))
        for block in range(blocks):
            for part, at in ((0, real_at), (1, imag_at)):
                spectra[block, at, :] = jnp.where(
                    left_chunk, outs[blocks - 1 - block][part], outs[block][part]
                )
        for lag in range(half):
            out = products([(grads[block], joins[block - lag]) for block in range(lag, blocks)])
            filters[lag, real_at, :] = out[0]
            filters[lag, imag_at, :] = out[1]

    trips = rows // chunk // 4

    def even(trip, _):
        for part in range(2):
            spectral(2 * trip + part, 1)
        return 0

    def odd(trip, _):
        for part in range(2):
            spectral(2 * trip + part, -1)
        return 0

    lax.fori_loop(0, trips, even, 0)
    lax.fori_loop(trips, 2 * trips, odd, 0)

    def back(values, buffer):
        for side, value in enumerate(values):
            head, tail = head_tail(value)
            at = pl.ds(side * LANES, LANES)
            rhs_back[buffer, pl.ds(0, 2 * rows), at] = head
            rhs_back[buffer, pl.ds(2 * rows, 2 * rows), at] = tail
            rhs_back[buffer, pl.ds(4 * rows, 2 * rows), at] = head
        result = jnp.dot(inverse_ref[...], rhs_back[buffer], preferred_element_type=jnp.float32)
        return result[:, :LANES], result[:, LANES:]

    def filter_grads(pair, _):
        values = filters[2 * pair], filters[2 * pair + 1]
        for side, value in enumerate(back(values, pair if unrolled else 0)):
            filters[2 * pair + side, pl.ds(0, rows), :] = value * grad_scale
        return 0

    loop(half // 2, filter_grads, 0, unrolled)

    def fold(value):
        return jnp.sum(value.reshape(rows // 8, 8, LANES), axis=0)

    def outputs(pair, totals):
        values = [spectra[(2 * pair + side) ^ place] for side in range(2)]
        results = back(values, (half // 2 + pair) if unrolled else 0)
        for side, result in enumerate(results):
            index = 2 * pair + side
            block = index ^ place
            out_ref = piece(out_refs, index, place)
            field = fields[index]
            result = result + gain * field
            scale = scale_of(result)
            out_ref[pl.ds(0, rows), :] = encode(result, scale).astype(jnp.bfloat16)
            misc[index, 0:1, :] = scale
            starts[block] = result[:8]
            turned = swap(result)
            grads = (second_ref[index] * turned, first_ref[index] * turned)
            new_totals = []
            for stream in (0, 1):
                for offset in range(3):
                    earlier = edged[index, stream, pl.ds(8 - offset, rows), :]
                    total = totals[3 * stream + offset]
                    new_totals.append(total + fold(grads[stream] * earlier))
            totals = tuple(new_totals)

            upper_half = block // half
            value = filters[lax.rem(block, half), pl.ds(0, rows), :]
            halves = join(left_half, value[:half_rows], value[half_rows:], upper_half)
            scale = scale_of(halves)
            code = encode(halves, scale).astype(jnp.bfloat16)
            out_ref[pl.ds(rows, half_rows), :] = code
            misc[index, 1:2, :] = scale
        return totals

    starts[blocks] = nothing
    totals = loop(half, outputs, (nothing,) * 6, unrolled)
    sums = [grad_scale * jnp.sum(total, axis=0, keepdims=True) for total in totals]
    shared[0:6, :] = taps[0:6]
    for row in range(6):
        value = sums[row]
        if row == 3:
            value = jnp.where(left_lanes((1, LANES)), filters[0, 0:1, :], value)
        shared[6 + row : 7 + row, :] = value

    def close(index, _):
        out_ref = piece(out_refs, index, place)
        block = index ^ place
        misc[index, 2:4, :] = starts[block + 1, 0:2, :]
        misc[index, 4:16, :] = shared[0:12, :]
        head, tail = head_tail(misc[index])
        here = rows + half_rows
        out_ref[pl.ds(here, MISC), :] = head
        out_ref[pl.ds(here + MISC, MISC), :] = tail
        near = jnp.concatenate([ends[block, 0:4, :], ends[block + 2, 4:8, :], nothing], axis=0)
        out_ref[pl.ds(here + 2 * MISC, ENDS), :] = near.astype(jnp.bfloat16)
        return 0

    loop(blocks, close, 0, unrolled)


def operator(taps, received, devices):
    count = len(received)
    blocks = devices
    rows = (received[0].shape[-2] - 16) * 2 // 5
    forward, inverse = transform_matrices(rows)
    wide = (blocks, rows, LANES)
    listed = count > 1

    def kernel(*refs):
        ins, (forward_ref, inverse_ref, taps_ref) = refs[:count], refs[count : count + 3]
        outs, scratch = refs[count + 3 : 2 * count + 3], refs[2 * count + 3 :]
        operator_kernel(ins, outs, forward_ref, inverse_ref, taps_ref, *scratch)

    return pl.pallas_call(
        kernel,
        out_shape=piece_shapes(devices, rows + rows // 2 + 2 * MISC + ENDS),
        scratch_shapes=[
            pltpu.VMEM((blocks + 2, 8, LANES), jnp.float32),
            pltpu.VMEM((blocks + 1, 8, LANES), jnp.float32),
            pltpu.VMEM((blocks, 2, rows + 8, LANES), jnp.float32),
            pltpu.VMEM(wide, jnp.float32),
            pltpu.VMEM(wide, jnp.float32),
            pltpu.VMEM(wide, jnp.float32),
            pltpu.VMEM((blocks, 2 * rows, LANES), jnp.float32),
            pltpu.VMEM((blocks, 2 * rows, LANES), jnp.float32),
            pltpu.VMEM((blocks if listed else 2, 3 * rows, 2 * LANES), jnp.bfloat16),
            pltpu.VMEM((3 * blocks // 4 if listed else 1, 6 * rows, 2 * LANES), jnp.bfloat16),
            pltpu.VMEM((16, LANES), jnp.float32),
            pltpu.VMEM((blocks, MISC, LANES), jnp.float32),
        ],
        compiler_params=pltpu.CompilerParams(
            vmem_limit_bytes=min(4 * blocks * MEBIBYTE, VMEM_BYTES)
        ),
    )(*in_order(received, OUT_ORDER), jnp.asarray(forward), jnp.asarray(inverse), taps)


def own_taps(short_taps, skip_gain, received):
    places = lax.axis_size("seq")
    columns = lax.axis_size("chan")
    share = skip_gain.shape[0]

    def pair(one, two):
        fill = ((0, 0), (0, HALF - share))
        return jnp.concatenate([jnp.pad(one, fill), jnp.pad(two, fill)], axis=1)

    straight = jnp.concatenate([jnp.ones((1, share)), jnp.zeros((2, share))]).astype(jnp.float32)
    rows = jnp.concatenate(
        [
            pair(short_taps[0], short_taps[1]),
            pair(straight, short_taps[2]),
            pair(skip_gain[None], skip_gain[None]),
            jnp.zeros((1, LANES), jnp.float32),
        ]
    )
    route = [
        (flat, (flat % places) * columns + flat // places) for flat in range(places * columns)
    ]
    if len(received) > 1:
        unit = jnp.ones((1, 1), jnp.bfloat16)
        rows, unit, received[-1] = lax.optimization_barrier((rows, unit, received[-1]))
        received[0] = received[0] * unit
    return lax.ppermute(rows, ("seq", "chan"), route), received


def spread(value, devices):
    rows, channels = value.shape
    share = channels // devices
    if share == HALF:
        return value
    wide = jnp.pad(value.reshape(rows, devices, share), ((0, 0), (0, 0), (0, HALF - share)))
    return wide.reshape(rows, devices * HALF)


def gathered(value, share):
    if share == HALF:
        return value
    groups = value.reshape(*value.shape[:-1], value.shape[-1] // HALF, HALF)[..., :share]
    return groups.reshape(*value.shape[:-1], -1)


def per_device(query_rows, key_rows, value_rows, long_filter, short_taps, skip_gain, cotangent):
    devices = lax.axis_size("seq")
    share = query_rows.shape[1] // devices
    streams = [spread(value, devices) for value in (query_rows, key_rows, value_rows)]
    upstream = spread(cotangent, devices)
    received = exchange(pack(streams, upstream, spread(long_filter, devices), devices))
    taps, received = own_taps(short_taps, skip_gain, received)
    results = exchange(operator(taps, received, devices))
    outs = finish(results, streams, upstream)
    *outs, skip_grad = (gathered(value, share) for value in outs)
    return (*outs, skip_grad[0])


def solution(mesh):
    in_specs = (
        P("seq", "chan"),
        P("seq", "chan"),
        P("seq", "chan"),
        P("seq", "chan"),
        P(None, None, ("seq", "chan")),
        P(("seq", "chan")),
        P("seq", "chan"),
    )
    out_specs = (
        P("seq", "chan"),
        P("seq", "chan"),
        P("seq", "chan"),
        P("seq", "chan"),
        P("seq", "chan"),
        P(None, None, "chan"),
        P("chan"),
    )
    return jax.shard_map(
        per_device, mesh=mesh, in_specs=in_specs, out_specs=out_specs, check_vma=False
    )
```

```python
import functools
import math

import jax
import jax.numpy as jnp
import numpy as np
from jax import lax
from jax.experimental import pallas as pl
from jax.experimental.pallas import tpu as pltpu
from jax.sharding import PartitionSpec as P

HALF = 64
LANES = 2 * HALF
ENDS = 16
MISC = 16
SPAN = 252.0
FLOOR = 125.0
MEBIBYTE = 1024 * 1024
VMEM_BYTES = 62 * MEBIBYTE
LISTED = 8
OUT_ORDER = (0, 7, 6, 3, 2, 5, 4, 1)
PACK_STEPS = ((3,), (1, 2, 0))
BACK_ORDER = (0, 7, 2, 5, 4, 6, 3, 1)


def swap(value):
    return pltpu.roll(value, HALF, 1)


def left_lanes(shape):
    return lax.broadcasted_iota(jnp.int32, shape, 1) < HALF


def head_tail(value):
    head = value.astype(jnp.bfloat16)
    tail = (value - head.astype(jnp.float32)).astype(jnp.bfloat16)
    return head, tail


def transform_matrices(rows):
    freq = np.concatenate([np.arange(0, rows, 2), np.arange(1, rows, 2)])
    turn = (2 * freq[:, None] + 1) * np.arange(rows)[None, :] % (4 * rows)
    theta = turn * (math.pi / (2 * rows))
    forward = np.concatenate([np.cos(theta), -np.sin(theta)])
    inverse = forward.T / rows

    def split(matrix):
        single = matrix.astype(np.float32)
        head = single.astype(jnp.bfloat16)
        tail = (single - head.astype(np.float32)).astype(jnp.bfloat16)
        return np.concatenate([head, head, tail], axis=1)

    return split(forward), split(inverse)


def encode(value, scale):
    code = jnp.exp2(jnp.abs(value) * (SPAN / scale) - FLOOR)
    return jnp.where(value < 0.0, -code, code)


def decode(code, scale):
    size = (jnp.log2(jnp.abs(code)) + FLOOR) * (scale * (1.0 / SPAN))
    return jnp.where(code < 0.0, -size, size)


def scale_of(value):
    peak = jnp.max(jnp.abs(value), axis=0, keepdims=True)
    return jnp.maximum(peak * 1.0001, 1e-30)


def loop(count, body, carry, unrolled):
    if unrolled:
        for index in range(count):
            carry = body(index, carry)
        return carry
    return lax.fori_loop(0, count, body, carry)


def piece(refs, index, place):
    return refs[index] if len(refs) > 1 else refs[0].at[index ^ place]


def exchange(pieces):
    if len(pieces) == 1:
        return [lax.all_to_all(pieces[0], "seq", 0, 0, tiled=True)]
    others = [
        lax.ppermute(value, "seq", [(one, one ^ index) for one in range(len(pieces))])
        for index, value in enumerate(pieces[1:], 1)
    ]
    return [pieces[0], *others]


def in_order(pieces, order):
    return [pieces[index] for index in order] if len(pieces) > 1 else pieces


def by_index(refs, order):
    if len(refs) == 1:
        return refs
    return [refs[order.index(index)] for index in range(len(refs))]


def piece_shapes(devices, rows):
    if devices == LISTED:
        return [jax.ShapeDtypeStruct((rows, LANES), jnp.bfloat16)] * devices
    return [jax.ShapeDtypeStruct((devices, rows, LANES), jnp.bfloat16)]


def join(mask, one, two, side):
    return jnp.where(mask, pltpu.roll(one, side * HALF, 1), pltpu.roll(two, HALF - side * HALF, 1))


def pack_kernel(steps, *refs):
    low_refs, filter_ref, refs = refs[:4], refs[4], refs[5:]
    low, high, staged, in_sems, out_sems = refs[-5:]
    out_refs = refs[:-5]
    rows, channels = filter_ref.shape
    devices = channels // HALF
    half = rows // 2
    place = lax.axis_index("seq")
    left = left_lanes((rows, LANES))
    left_half = left_lanes((half, LANES))
    copies = {}
    for step in steps:
        tile = step ^ (place // 2)
        at = pl.ds(pl.multiple_of(tile * LANES, LANES), LANES)
        pairs = [(ref.at[:, at], low.at[step, stream]) for stream, ref in enumerate(low_refs)]
        pairs.append((filter_ref.at[:, at], high.at[step]))
        copies[step] = [
            pltpu.make_async_copy(source, target, in_sems.at[step, stream])
            for stream, (source, target) in enumerate(pairs)
        ]
        for copy in copies[step]:
            copy.start()
    leaving = []
    for step in steps:
        for copy in copies[step]:
            copy.wait()
        for index in (2 * step + 1, 2 * step):
            side = lax.rem(index ^ place, 2)
            for first, second, start in ((0, 1, 0), (3, 2, rows)):
                one = low[step, first].astype(jnp.float32)
                two = low[step, second].astype(jnp.float32)
                joined = join(left, one, two, side).astype(jnp.bfloat16)
                staged[index, pl.ds(start, rows), :] = joined
            pair = join(left_half, high[step, :half], high[step, half:], side)
            scale = scale_of(pair)
            staged[index, pl.ds(2 * rows, half), :] = encode(pair, scale).astype(jnp.bfloat16)
            head, tail = head_tail(jnp.broadcast_to(scale, (8, LANES)))
            both = jnp.concatenate([head.astype(jnp.float32), tail.astype(jnp.float32)], axis=0)
            staged[index, pl.ds(2 * rows + half, 16), :] = both.astype(jnp.bfloat16)
            if len(out_refs) == 1:
                target = out_refs[0].at[index ^ place]
            else:
                target = out_refs[2 * steps.index(step) + index % 2]
            leaving.append(pltpu.make_async_copy(staged.at[index], target, out_sems.at[index]))
            leaving[-1].start()
    for copy in leaving:
        copy.wait()


def pack_steps(arrays, devices, steps):
    rows = arrays[-1].shape[0]
    sent_rows = 2 * rows + rows // 2 + 16
    shapes = piece_shapes(devices, sent_rows)
    if len(shapes) > 1:
        shapes = shapes[: 2 * len(steps)]
    anywhere = pl.BlockSpec(memory_space=pl.ANY)
    return pl.pallas_call(
        functools.partial(pack_kernel, steps),
        in_specs=[anywhere] * 5,
        out_specs=[anywhere] * len(shapes),
        out_shape=shapes,
        scratch_shapes=[
            pltpu.VMEM((devices // 2, 4, rows, LANES), jnp.bfloat16),
            pltpu.VMEM((devices // 2, rows, LANES), jnp.float32),
            pltpu.VMEM((devices, sent_rows, LANES), jnp.bfloat16),
            pltpu.SemaphoreType.DMA((devices // 2, 5)),
            pltpu.SemaphoreType.DMA((devices,)),
        ],
        compiler_params=pltpu.CompilerParams(vmem_limit_bytes=VMEM_BYTES),
    )(*arrays)


def pack(streams, cotangent, long_filter, devices):
    arrays = (*streams, cotangent, long_filter)
    if devices != LISTED:
        return pack_steps(arrays, devices, tuple(range(devices // 2)))
    pieces = [None] * devices
    for steps in PACK_STEPS:
        made = pack_steps(arrays, devices, steps)
        for at, step in enumerate(steps):
            pieces[2 * step], pieces[2 * step + 1] = made[2 * at], made[2 * at + 1]
    return pieces


def finish_kernel(
    pieces, query_ref, key_ref, value_ref, cot_ref, gated_out, query_out, key_out, value_out,
    filter_out, taps_out, skip_out, before, after,
):
    in_refs = by_index(pieces, BACK_ORDER)
    rows, channels = query_ref.shape
    half = rows // 2
    place = lax.axis_index("seq")
    odd = lax.rem(place, 2) == 1
    left = left_lanes((rows, LANES))
    left_half = left_lanes((half, LANES))
    left_misc = left_lanes((MISC, LANES))

    def one_tile(step, _):
        refs = piece(in_refs, 2 * step, place), piece(in_refs, 2 * step + 1, place)
        at = pl.ds(pl.multiple_of((step ^ (place // 2)) * LANES, LANES), LANES)

        def both(start, count):
            one, two = (ref[pl.ds(start, count), :].astype(jnp.float32) for ref in refs)
            return jnp.where(odd, two, one), jnp.where(odd, one, two)

        def sides(mask, values):
            one, two = values
            return jnp.where(mask, one, swap(two)), jnp.where(mask, swap(one), two)

        miscs = [
            head + tail
            for head, tail in zip(both(rows + half, MISC), both(rows + half + MISC, MISC))
        ]
        codes = both(0, rows)
        back, mixed = sides(left, [decode(code, misc[0:1]) for code, misc in zip(codes, miscs)])
        codes = both(rows, half)
        upper, lower = sides(
            left_half, [decode(code, misc[1:2]) for code, misc in zip(codes, miscs)]
        )
        filter_out[pl.ds(0, half), at] = upper
        filter_out[pl.ds(half, half), at] = lower
        ends = sides(left_misc, both(rows + half + 2 * MISC, ENDS))
        lefts, rights = sides(left_misc, miscs)
        taps = (lefts[4:7], rights[4:7], rights[7:10])
        for offset in range(3):
            taps_out[0, offset : offset + 1, at] = lefts[10 + offset : 11 + offset]
            taps_out[1, offset : offset + 1, at] = rights[10 + offset : 11 + offset]
            taps_out[2, offset : offset + 1, at] = rights[13 + offset : 14 + offset]
        skip_out[0:1, at] = lefts[13:14]
        back_edge, mixed_edge = lefts[2:4], rights[2:4]
        convs, edges = [], []
        for stream, (source, end, row) in enumerate(
            ((query_ref, ends[0], 0), (key_ref, ends[1], 0), (value_ref, ends[1], 2))
        ):
            now = source[:, at].astype(jnp.float32)
            before[stream, 6:8, :] = end[row : row + 2]
            before[stream, pl.ds(8, rows), :] = now
            before[stream, pl.ds(8 + rows, 2), :] = end[row + 4 : row + 6]
            conv = taps[stream][0:1] * now
            edge = taps[stream][0:1] * end[row + 4 : row + 6]
            for offset in (1, 2):
                weight = taps[stream][offset : offset + 1]
                conv = conv + weight * before[stream, pl.ds(8 - offset, rows), :]
                edge = edge + weight * before[stream, pl.ds(8 + rows - offset, 2), :]
            convs.append(conv)
            edges.append(edge)
        cotangent = cot_ref[:, at].astype(jnp.float32)
        cot_edge = ends[0][6:8]
        gated_out[:, at] = (convs[0] * mixed).astype(jnp.bfloat16)
        for stream, (out, grad, edge) in enumerate(
            (
                (query_out, cotangent * mixed, cot_edge * mixed_edge),
                (key_out, back * convs[2], back_edge * edges[2]),
                (value_out, back * convs[1], back_edge * edges[1]),
            )
        ):
            after[stream, pl.ds(0, rows), :] = grad
            after[stream, pl.ds(rows, 2), :] = edge
            total = taps[stream][0:1] * grad
            for offset in (1, 2):
                weight = taps[stream][offset : offset + 1]
                total = total + weight * after[stream, pl.ds(offset, rows), :]
            out[:, at] = total.astype(jnp.bfloat16)
        return 0

    loop(channels // LANES, one_tile, 0, len(in_refs) > 1)


def finish(received, streams, cotangent):
    rows, channels = cotangent.shape
    count = len(received)
    low = jax.ShapeDtypeStruct((rows, channels), jnp.bfloat16)

    def kernel(*refs):
        finish_kernel(refs[:count], *refs[count:])

    return pl.pallas_call(
        kernel,
        out_shape=(
            low,
            low,
            low,
            low,
            jax.ShapeDtypeStruct((rows, channels), jnp.float32),
            jax.ShapeDtypeStruct((3, 3, channels), jnp.float32),
            jax.ShapeDtypeStruct((1, channels), jnp.float32),
        ),
        scratch_shapes=[
            pltpu.VMEM((3, rows + 16, LANES), jnp.float32),
            pltpu.VMEM((3, rows + 8, LANES), jnp.float32),
        ],
        compiler_params=pltpu.CompilerParams(
            vmem_limit_bytes=3 * (channels // HALF) * MEBIBYTE // 2
        ),
    )(*in_order(received, BACK_ORDER), *streams, cotangent)


def operator_kernel(
    pieces, out_refs, forward_ref, inverse_ref, taps_ref,
    ends, starts, edged, first_ref, second_ref, fields, spectra, filters, rhs, rhs_back,
    shared, misc,
):
    in_refs = by_index(pieces, OUT_ORDER)
    blocks = fields.shape[0]
    place = lax.axis_index("seq")
    rows = forward_ref.shape[0] // 2
    half = blocks // 2
    half_rows = rows // 2
    unrolled = len(in_refs) > 1
    grad_scale = 1.0 / math.sqrt(blocks * rows)
    left = left_lanes((rows, LANES))
    left_half = left_lanes((half_rows, LANES))
    taps = taps_ref[...]
    query_taps = [taps[i : i + 1] for i in range(3)]
    value_taps = [taps[3 + i : 4 + i] for i in range(3)]
    gain = taps[6:7]
    nothing = jnp.zeros((8, LANES), jnp.float32)

    def lay(buffer, side, place, value):
        head, tail = head_tail(value)
        count = value.shape[0]
        at = pl.ds(side * LANES, LANES)
        rhs[buffer, pl.ds(place, count), at] = head
        rhs[buffer, pl.ds(rows + place, count), at] = tail
        rhs[buffer, pl.ds(2 * rows + place, count), at] = head

    def transformed(buffer):
        return jnp.dot(forward_ref[...], rhs[buffer], preferred_element_type=jnp.float32)

    def keep_ends(index, _):
        ref = piece(in_refs, index, place)
        block = index ^ place
        for stream in (0, 1):
            start = stream * rows
            last = ref[pl.ds(start + rows - 16, 16), :].astype(jnp.float32)
            first = ref[pl.ds(start, 16), :].astype(jnp.float32)
            ends[block + 1, 2 * stream : 2 * stream + 2, :] = last[14:16]
            ends[block + 1, 2 * stream + 4 : 2 * stream + 6, :] = first[0:2]
        return 0

    ends[0] = nothing
    ends[blocks + 1] = nothing
    loop(blocks, keep_ends, 0, unrolled)

    def transform(pair, _):
        spot = 2 * pair if unrolled else 0
        for side in range(2):
            ref = piece(in_refs, 2 * pair + side, place)
            scale = ref[pl.ds(2 * rows + half_rows, 16), :].astype(jnp.float32)
            code = ref[pl.ds(2 * rows, half_rows), :].astype(jnp.float32)
            taken = decode(code, scale[0:1] + scale[8:9])
            turned = swap(taken)
            lay(spot, side, 0, jnp.where(left_half, taken, turned))
            lay(spot, side, half_rows, jnp.where(left_half, turned, taken))
        result = transformed(spot)
        for side in range(2):
            filters[(2 * pair + side) ^ place] = result[:, side * LANES : (side + 1) * LANES]
        for side in range(2):
            index = 2 * pair + side
            ref = piece(in_refs, index, place)
            outs = []
            for stream, weights in ((0, query_taps), (1, value_taps)):
                now = ref[pl.ds(stream * rows, rows), :].astype(jnp.float32)
                last = ends[index ^ place, 2 * stream : 2 * stream + 2, :]
                edged[index, stream, 6:8, :] = last
                edged[index, stream, pl.ds(8, rows), :] = now
                total = weights[0] * now
                for offset in (1, 2):
                    shifted = edged[index, stream, pl.ds(8 - offset, rows), :]
                    total = total + weights[offset] * shifted
                outs.append(total)
            first_ref[index] = outs[0]
            second_ref[index] = outs[1]
            field = outs[0] * outs[1]
            fields[index] = field
            lay(spot + 1, side, 0, field)
        result = transformed(spot + 1)
        for side in range(2):
            spectra[(2 * pair + side) ^ place] = result[:, side * LANES : (side + 1) * LANES]
        return 0

    loop(half, transform, 0, unrolled)

    chunk = 8
    left_chunk = left_lanes((chunk, LANES))
    conjugate = jnp.where(left_chunk, -1.0, 1.0)

    def products(pairs):
        one = two = three = None
        for (re, im, both), (join_re, join_less, join_more) in pairs:
            terms = join_re * both, re * join_less, im * join_more
            if one is None:
                one, two, three = terms
            else:
                one, two, three = one + terms[0], two + terms[1], three + terms[2]
        return one - three, one + two

    def spectral(step, sign):
        real_at = pl.ds(pl.multiple_of(step * chunk, chunk), chunk)
        imag_at = pl.ds(pl.multiple_of(rows + step * chunk, chunk), chunk)
        field_re = [spectra[block, real_at, :] for block in range(blocks)]
        field_im = [spectra[block, imag_at, :] for block in range(blocks)]

        def joined(re, im, block):
            if block == 0:
                return re[0], im[0]
            if sign > 0:
                return re[block] - im[block - 1], im[block] + re[block - 1]
            return re[block] + im[block - 1], im[block] - re[block - 1]

        turned = []
        for block in range(blocks):
            re = jnp.where(left_chunk, field_re[blocks - 1 - block], field_re[block])
            im = jnp.where(left_chunk, field_im[blocks - 1 - block], field_im[block])
            turned.append((re, im, re + im))
        filt_re = [filters[block, real_at, :] for block in range(blocks)]
        filt_im = [filters[block, imag_at, :] for block in range(blocks)]
        joins = []
        for block in range(blocks):
            re, im = joined(filt_re, filt_im, block)
            im = im * conjugate
            joins.append((re, im - re, re + im))
        outs = [
            products([(turned[block - lag], joins[lag]) for lag in range(block + 1)])
            for block in range(blocks)
        ]
        grads = []
        for block in range(blocks):
            re = jnp.where(left_chunk, field_re[block], swap(field_re[block]))
            im = jnp.where(left_chunk, field_im[block], swap(field_im[block]))
            grads.append((re, im, re + im))
        sums = [joined(field_re, field_im, block) for block in range(blocks)]
        joins = []
        for block in range(blocks):
            parts = []
            for part in range(2):
                far = sums[block - half][part] if block >= half else 0.0
                parts.append(jnp.where(left_chunk, swap(sums[block][part]), far))
            re, im = parts
            joins.append((re, -im - re, re - im))
        for block in range(blocks):
            for part, at in ((0, real_at), (1, imag_at)):
                spectra[block, at, :] = jnp.where(
                    left_chunk, outs[blocks - 1 - block][part], outs[block][part]
                )
        for lag in range(half):
            out = products([(grads[block], joins[block - lag]) for block in range(lag, blocks)])
            filters[lag, real_at, :] = out[0]
            filters[lag, imag_at, :] = out[1]

    trips = rows // chunk // 4

    def even(trip, _):
        for part in range(2):
            spectral(2 * trip + part, 1)
        return 0

    def odd(trip, _):
        for part in range(2):
            spectral(2 * trip + part, -1)
        return 0

    lax.fori_loop(0, trips, even, 0)
    lax.fori_loop(trips, 2 * trips, odd, 0)

    def back(values, buffer):
        for side, value in enumerate(values):
            head, tail = head_tail(value)
            at = pl.ds(side * LANES, LANES)
            rhs_back[buffer, pl.ds(0, 2 * rows), at] = head
            rhs_back[buffer, pl.ds(2 * rows, 2 * rows), at] = tail
            rhs_back[buffer, pl.ds(4 * rows, 2 * rows), at] = head
        result = jnp.dot(inverse_ref[...], rhs_back[buffer], preferred_element_type=jnp.float32)
        return result[:, :LANES], result[:, LANES:]

    def filter_grads(pair, _):
        values = filters[2 * pair], filters[2 * pair + 1]
        for side, value in enumerate(back(values, pair if unrolled else 0)):
            filters[2 * pair + side, pl.ds(0, rows), :] = value * grad_scale
        return 0

    loop(half // 2, filter_grads, 0, unrolled)

    def fold(value):
        return jnp.sum(value.reshape(rows // 8, 8, LANES), axis=0)

    def outputs(pair, totals):
        values = [spectra[(2 * pair + side) ^ place] for side in range(2)]
        results = back(values, (half // 2 + pair) if unrolled else 0)
        for side, result in enumerate(results):
            index = 2 * pair + side
            block = index ^ place
            out_ref = piece(out_refs, index, place)
            field = fields[index]
            result = result + gain * field
            scale = scale_of(result)
            out_ref[pl.ds(0, rows), :] = encode(result, scale).astype(jnp.bfloat16)
            misc[index, 0:1, :] = scale
            starts[block] = result[:8]
            turned = swap(result)
            grads = (second_ref[index] * turned, first_ref[index] * turned)
            new_totals = []
            for stream in (0, 1):
                for offset in range(3):
                    earlier = edged[index, stream, pl.ds(8 - offset, rows), :]
                    total = totals[3 * stream + offset]
                    new_totals.append(total + fold(grads[stream] * earlier))
            totals = tuple(new_totals)

            upper_half = block // half
            value = filters[lax.rem(block, half), pl.ds(0, rows), :]
            halves = join(left_half, value[:half_rows], value[half_rows:], upper_half)
            scale = scale_of(halves)
            code = encode(halves, scale).astype(jnp.bfloat16)
            out_ref[pl.ds(rows, half_rows), :] = code
            misc[index, 1:2, :] = scale
        return totals

    starts[blocks] = nothing
    totals = loop(half, outputs, (nothing,) * 6, unrolled)
    sums = [grad_scale * jnp.sum(total, axis=0, keepdims=True) for total in totals]
    shared[0:6, :] = taps[0:6]
    for row in range(6):
        value = sums[row]
        if row == 3:
            value = jnp.where(left_lanes((1, LANES)), filters[0, 0:1, :], value)
        shared[6 + row : 7 + row, :] = value

    def close(index, _):
        out_ref = piece(out_refs, index, place)
        block = index ^ place
        misc[index, 2:4, :] = starts[block + 1, 0:2, :]
        misc[index, 4:16, :] = shared[0:12, :]
        head, tail = head_tail(misc[index])
        here = rows + half_rows
        out_ref[pl.ds(here, MISC), :] = head
        out_ref[pl.ds(here + MISC, MISC), :] = tail
        near = jnp.concatenate([ends[block, 0:4, :], ends[block + 2, 4:8, :], nothing], axis=0)
        out_ref[pl.ds(here + 2 * MISC, ENDS), :] = near.astype(jnp.bfloat16)
        return 0

    loop(blocks, close, 0, unrolled)


def operator(taps, received, devices):
    count = len(received)
    blocks = devices
    rows = (received[0].shape[-2] - 16) * 2 // 5
    forward, inverse = transform_matrices(rows)
    wide = (blocks, rows, LANES)
    listed = count > 1

    def kernel(*refs):
        ins, (forward_ref, inverse_ref, taps_ref) = refs[:count], refs[count : count + 3]
        outs, scratch = refs[count + 3 : 2 * count + 3], refs[2 * count + 3 :]
        operator_kernel(ins, outs, forward_ref, inverse_ref, taps_ref, *scratch)

    return pl.pallas_call(
        kernel,
        out_shape=piece_shapes(devices, rows + rows // 2 + 2 * MISC + ENDS),
        scratch_shapes=[
            pltpu.VMEM((blocks + 2, 8, LANES), jnp.float32),
            pltpu.VMEM((blocks + 1, 8, LANES), jnp.float32),
            pltpu.VMEM((blocks, 2, rows + 8, LANES), jnp.float32),
            pltpu.VMEM(wide, jnp.float32),
            pltpu.VMEM(wide, jnp.float32),
            pltpu.VMEM(wide, jnp.float32),
            pltpu.VMEM((blocks, 2 * rows, LANES), jnp.float32),
            pltpu.VMEM((blocks, 2 * rows, LANES), jnp.float32),
            pltpu.VMEM((blocks if listed else 2, 3 * rows, 2 * LANES), jnp.bfloat16),
            pltpu.VMEM((3 * blocks // 4 if listed else 1, 6 * rows, 2 * LANES), jnp.bfloat16),
            pltpu.VMEM((16, LANES), jnp.float32),
            pltpu.VMEM((blocks, MISC, LANES), jnp.float32),
        ],
        compiler_params=pltpu.CompilerParams(
            vmem_limit_bytes=min(4 * blocks * MEBIBYTE, VMEM_BYTES)
        ),
    )(*in_order(received, OUT_ORDER), jnp.asarray(forward), jnp.asarray(inverse), taps)


def own_taps(short_taps, skip_gain, received):
    places = lax.axis_size("seq")
    columns = lax.axis_size("chan")
    share = skip_gain.shape[0]

    def pair(one, two):
        fill = ((0, 0), (0, HALF - share))
        return jnp.concatenate([jnp.pad(one, fill), jnp.pad(two, fill)], axis=1)

    straight = jnp.concatenate([jnp.ones((1, share)), jnp.zeros((2, share))]).astype(jnp.float32)
    rows = jnp.concatenate(
        [
            pair(short_taps[0], short_taps[1]),
            pair(straight, short_taps[2]),
            pair(skip_gain[None], skip_gain[None]),
            jnp.zeros((1, LANES), jnp.float32),
        ]
    )
    route = [
        (flat, (flat % places) * columns + flat // places) for flat in range(places * columns)
    ]
    if len(received) > 1:
        unit = jnp.ones((1, 1), jnp.bfloat16)
        rows, unit, received[-1] = lax.optimization_barrier((rows, unit, received[-1]))
        received[0] = received[0] * unit
    return lax.ppermute(rows, ("seq", "chan"), route), received


def spread(value, devices):
    rows, channels = value.shape
    share = channels // devices
    if share == HALF:
        return value
    wide = jnp.pad(value.reshape(rows, devices, share), ((0, 0), (0, 0), (0, HALF - share)))
    return wide.reshape(rows, devices * HALF)


def gathered(value, share):
    if share == HALF:
        return value
    groups = value.reshape(*value.shape[:-1], value.shape[-1] // HALF, HALF)[..., :share]
    return groups.reshape(*value.shape[:-1], -1)


def per_device(query_rows, key_rows, value_rows, long_filter, short_taps, skip_gain, cotangent):
    devices = lax.axis_size("seq")
    share = query_rows.shape[1] // devices
    streams = [spread(value, devices) for value in (query_rows, key_rows, value_rows)]
    upstream = spread(cotangent, devices)
    received = exchange(pack(streams, upstream, spread(long_filter, devices), devices))
    taps, received = own_taps(short_taps, skip_gain, received)
    results = exchange(operator(taps, received, devices))
    outs = finish(results, streams, upstream)
    *outs, skip_grad = (gathered(value, share) for value in outs)
    return (*outs, skip_grad[0])


def solution(mesh):
    in_specs = (
        P("seq", "chan"),
        P("seq", "chan"),
        P("seq", "chan"),
        P("seq", "chan"),
        P(None, None, ("seq", "chan")),
        P(("seq", "chan")),
        P("seq", "chan"),
    )
    out_specs = (
        P("seq", "chan"),
        P("seq", "chan"),
        P("seq", "chan"),
        P("seq", "chan"),
        P("seq", "chan"),
        P(None, None, "chan"),
        P("chan"),
    )
    return jax.shard_map(
        per_device, mesh=mesh, in_specs=in_specs, out_specs=out_specs, check_vma=False
    )
```

```python
import functools
import math

import jax
import jax.numpy as jnp
import numpy as np
from jax import lax
from jax.experimental import pallas as pl
from jax.experimental.pallas import tpu as pltpu
from jax.sharding import PartitionSpec as P

HALF = 64
LANES = 2 * HALF
MISC = 32
SPAN = 252.0
FLOOR = 125.0
MEBIBYTE = 1024 * 1024
VMEM_BYTES = 62 * MEBIBYTE
LISTED = 8
OUT_ORDER = (0, 7, 6, 3, 2, 5, 4, 1)
PACK_STEPS = ((3,), (1, 2, 0))
BACK_ORDER = (0, 7, 2, 5, 4, 6, 3, 1)


def swap(value):
    return pltpu.roll(value, HALF, 1)


def left_lanes(shape):
    return lax.broadcasted_iota(jnp.int32, shape, 1) < HALF


def head_tail(value):
    head = value.astype(jnp.bfloat16)
    tail = (value - head.astype(jnp.float32)).astype(jnp.bfloat16)
    return head, tail


def transform_matrices(rows):
    freq = np.concatenate([np.arange(0, rows, 2), np.arange(1, rows, 2)])
    turn = (2 * freq[:, None] + 1) * np.arange(rows)[None, :] % (4 * rows)
    theta = turn * (math.pi / (2 * rows))
    forward = np.concatenate([np.cos(theta), -np.sin(theta)])
    inverse = forward.T / rows

    def split(matrix):
        single = matrix.astype(np.float32)
        head = single.astype(jnp.bfloat16)
        tail = (single - head.astype(np.float32)).astype(jnp.bfloat16)
        return np.concatenate([head, head, tail], axis=1)

    return split(forward), split(inverse)


def encode(value, scale):
    code = jnp.exp2(jnp.abs(value) * (SPAN / scale) - FLOOR)
    return jnp.where(value < 0.0, -code, code)


def decode(code, scale):
    size = (jnp.log2(jnp.abs(code)) + FLOOR) * (scale * (1.0 / SPAN))
    return jnp.where(code < 0.0, -size, size)


def scale_of(value):
    peak = jnp.max(jnp.abs(value), axis=0, keepdims=True)
    return jnp.maximum(peak * 1.0001, 1e-30)


def loop(count, body, carry, unrolled):
    if unrolled:
        for index in range(count):
            carry = body(index, carry)
        return carry
    return lax.fori_loop(0, count, body, carry)


def piece(refs, index, place):
    return refs[index] if len(refs) > 1 else refs[0].at[index ^ place]


def exchange(pieces):
    if len(pieces) == 1:
        return [lax.all_to_all(pieces[0], "seq", 0, 0, tiled=True)]
    others = [
        lax.ppermute(value, "seq", [(one, one ^ index) for one in range(len(pieces))])
        for index, value in enumerate(pieces[1:], 1)
    ]
    return [pieces[0], *others]


def in_order(pieces, order):
    return [pieces[index] for index in order] if len(pieces) > 1 else pieces


def by_index(refs, order):
    if len(refs) == 1:
        return refs
    return [refs[order.index(index)] for index in range(len(refs))]


def piece_shapes(devices, rows):
    if devices == LISTED:
        return [jax.ShapeDtypeStruct((rows, LANES), jnp.bfloat16)] * devices
    return [jax.ShapeDtypeStruct((devices, rows, LANES), jnp.bfloat16)]


def join(mask, one, two, side):
    return jnp.where(mask, pltpu.roll(one, side * HALF, 1), pltpu.roll(two, HALF - side * HALF, 1))


def pack_kernel(steps, *refs):
    low_refs, filter_ref, refs = refs[:4], refs[4], refs[5:]
    low, high, staged, in_sems, out_sems = refs[-5:]
    out_refs = refs[:-5]
    rows, channels = filter_ref.shape
    devices = channels // HALF
    half = rows // 2
    place = lax.axis_index("seq")
    left = left_lanes((rows, LANES))
    left_half = left_lanes((half, LANES))
    copies = {}
    for step in steps:
        tile = step ^ (place // 2)
        at = pl.ds(pl.multiple_of(tile * LANES, LANES), LANES)
        pairs = [(ref.at[:, at], low.at[step, stream]) for stream, ref in enumerate(low_refs)]
        pairs.append((filter_ref.at[:, at], high.at[step]))
        copies[step] = [
            pltpu.make_async_copy(source, target, in_sems.at[step, stream])
            for stream, (source, target) in enumerate(pairs)
        ]
        for copy in copies[step]:
            copy.start()
    leaving = []
    for step in steps:
        for copy in copies[step]:
            copy.wait()
        for index in (2 * step + 1, 2 * step):
            side = lax.rem(index ^ place, 2)
            for first, second, start in ((0, 1, 0), (3, 2, rows)):
                one = low[step, first].astype(jnp.float32)
                two = low[step, second].astype(jnp.float32)
                joined = join(left, one, two, side).astype(jnp.bfloat16)
                staged[index, pl.ds(start, rows), :] = joined
            pair = join(left_half, high[step, :half], high[step, half:], side)
            scale = scale_of(pair)
            staged[index, pl.ds(2 * rows, half), :] = encode(pair, scale).astype(jnp.bfloat16)
            head, tail = head_tail(jnp.broadcast_to(scale, (8, LANES)))
            both = jnp.concatenate([head.astype(jnp.float32), tail.astype(jnp.float32)], axis=0)
            staged[index, pl.ds(2 * rows + half, 16), :] = both.astype(jnp.bfloat16)
            if len(out_refs) == 1:
                target = out_refs[0].at[index ^ place]
            else:
                target = out_refs[2 * steps.index(step) + index % 2]
            leaving.append(pltpu.make_async_copy(staged.at[index], target, out_sems.at[index]))
            leaving[-1].start()
    for copy in leaving:
        copy.wait()


def pack_steps(arrays, devices, steps):
    rows = arrays[-1].shape[0]
    sent_rows = 2 * rows + rows // 2 + 16
    shapes = piece_shapes(devices, sent_rows)
    if len(shapes) > 1:
        shapes = shapes[: 2 * len(steps)]
    anywhere = pl.BlockSpec(memory_space=pl.ANY)
    return pl.pallas_call(
        functools.partial(pack_kernel, steps),
        in_specs=[anywhere] * 5,
        out_specs=[anywhere] * len(shapes),
        out_shape=shapes,
        scratch_shapes=[
            pltpu.VMEM((devices // 2, 4, rows, LANES), jnp.bfloat16),
            pltpu.VMEM((devices // 2, rows, LANES), jnp.float32),
            pltpu.VMEM((devices, sent_rows, LANES), jnp.bfloat16),
            pltpu.SemaphoreType.DMA((devices // 2, 5)),
            pltpu.SemaphoreType.DMA((devices,)),
        ],
        compiler_params=pltpu.CompilerParams(vmem_limit_bytes=VMEM_BYTES),
    )(*arrays)


def pack(streams, cotangent, long_filter, devices):
    arrays = (*streams, cotangent, long_filter)
    if devices != LISTED:
        return pack_steps(arrays, devices, tuple(range(devices // 2)))
    pieces = [None] * devices
    for steps in PACK_STEPS:
        made = pack_steps(arrays, devices, steps)
        for at, step in enumerate(steps):
            pieces[2 * step], pieces[2 * step + 1] = made[2 * at], made[2 * at + 1]
    return pieces


def finish_kernel(
    pieces, query_ref, key_ref, value_ref, cot_ref, gated_out, query_out, key_out, value_out,
    filter_out, taps_out, skip_out, before, after,
):
    in_refs = by_index(pieces, BACK_ORDER)
    rows, channels = query_ref.shape
    half = rows // 2
    place = lax.axis_index("seq")
    odd = lax.rem(place, 2) == 1
    left = left_lanes((rows, LANES))
    left_half = left_lanes((half, LANES))

    def one_tile(step, _):
        refs = piece(in_refs, 2 * step, place), piece(in_refs, 2 * step + 1, place)
        at = pl.ds(pl.multiple_of((step ^ (place // 2)) * LANES, LANES), LANES)

        def both(start, count):
            one, two = (ref[pl.ds(start, count), :].astype(jnp.float32) for ref in refs)
            return jnp.where(odd, two, one), jnp.where(odd, one, two)

        def sides(mask, values):
            one, two = values
            return jnp.where(mask, one, swap(two)), jnp.where(mask, swap(one), two)

        miscs = both(rows + half, MISC)
        scales = [misc[0:5] + misc[5:10] for misc in miscs]

        def small(start, stop, scale):
            return [
                decode(misc[start:stop], row[scale : scale + 1])
                for misc, row in zip(miscs, scales)
            ]

        codes = both(0, rows)
        back, mixed = sides(left, [decode(code, row[0:1]) for code, row in zip(codes, scales)])
        codes = both(rows, half)
        upper, lower = sides(
            left_half, [decode(code, row[1:2]) for code, row in zip(codes, scales)]
        )
        filter_out[pl.ds(0, half), at] = upper
        filter_out[pl.ds(half, half), at] = lower
        ends = sides(left_lanes((8, LANES)), [misc[24:32] for misc in miscs])
        lefts, rights = sides(left_lanes((6, LANES)), small(12, 18, 3))
        taps = (lefts[0:3], rights[0:3], rights[3:6])
        lefts, rights = sides(left_lanes((6, LANES)), small(18, 24, 4))
        for offset in range(3):
            taps_out[0, offset : offset + 1, at] = lefts[offset : offset + 1]
            taps_out[1, offset : offset + 1, at] = rights[offset : offset + 1]
            taps_out[2, offset : offset + 1, at] = rights[3 + offset : 4 + offset]
        skip_out[0:1, at] = lefts[3:4]
        back_edge, mixed_edge = sides(left_lanes((2, LANES)), small(10, 12, 2))
        convs, edges = [], []
        for stream, (source, end, row) in enumerate(
            ((query_ref, ends[0], 0), (key_ref, ends[1], 0), (value_ref, ends[1], 2))
        ):
            now = source[:, at].astype(jnp.float32)
            before[stream, 6:8, :] = end[row : row + 2]
            before[stream, pl.ds(8, rows), :] = now
            before[stream, pl.ds(8 + rows, 2), :] = end[row + 4 : row + 6]
            conv = taps[stream][0:1] * now
            edge = taps[stream][0:1] * end[row + 4 : row + 6]
            for offset in (1, 2):
                weight = taps[stream][offset : offset + 1]
                conv = conv + weight * before[stream, pl.ds(8 - offset, rows), :]
                edge = edge + weight * before[stream, pl.ds(8 + rows - offset, 2), :]
            convs.append(conv)
            edges.append(edge)
        cotangent = cot_ref[:, at].astype(jnp.float32)
        cot_edge = ends[0][6:8]
        gated_out[:, at] = (convs[0] * mixed).astype(jnp.bfloat16)
        for stream, (out, grad, edge) in enumerate(
            (
                (query_out, cotangent * mixed, cot_edge * mixed_edge),
                (key_out, back * convs[2], back_edge * edges[2]),
                (value_out, back * convs[1], back_edge * edges[1]),
            )
        ):
            after[stream, pl.ds(0, rows), :] = grad
            after[stream, pl.ds(rows, 2), :] = edge
            total = taps[stream][0:1] * grad
            for offset in (1, 2):
                weight = taps[stream][offset : offset + 1]
                total = total + weight * after[stream, pl.ds(offset, rows), :]
            out[:, at] = total.astype(jnp.bfloat16)
        return 0

    loop(channels // LANES, one_tile, 0, len(in_refs) > 1)


def finish(received, streams, cotangent):
    rows, channels = cotangent.shape
    count = len(received)
    low = jax.ShapeDtypeStruct((rows, channels), jnp.bfloat16)

    def kernel(*refs):
        finish_kernel(refs[:count], *refs[count:])

    return pl.pallas_call(
        kernel,
        out_shape=(
            low,
            low,
            low,
            low,
            jax.ShapeDtypeStruct((rows, channels), jnp.float32),
            jax.ShapeDtypeStruct((3, 3, channels), jnp.float32),
            jax.ShapeDtypeStruct((1, channels), jnp.float32),
        ),
        scratch_shapes=[
            pltpu.VMEM((3, rows + 16, LANES), jnp.float32),
            pltpu.VMEM((3, rows + 8, LANES), jnp.float32),
        ],
        compiler_params=pltpu.CompilerParams(
            vmem_limit_bytes=3 * (channels // HALF) * MEBIBYTE // 2
        ),
    )(*in_order(received, BACK_ORDER), *streams, cotangent)


def operator_kernel(
    pieces, out_refs, forward_ref, inverse_ref, taps_ref,
    ends, starts, edged, first_ref, second_ref, fields, spectra, filters, rhs, rhs_back,
    shared, misc,
):
    in_refs = by_index(pieces, OUT_ORDER)
    blocks = fields.shape[0]
    place = lax.axis_index("seq")
    rows = forward_ref.shape[0] // 2
    half = blocks // 2
    half_rows = rows // 2
    unrolled = len(in_refs) > 1
    grad_scale = 1.0 / math.sqrt(blocks * rows)
    left = left_lanes((rows, LANES))
    left_half = left_lanes((half_rows, LANES))
    taps = taps_ref[...]
    query_taps = [taps[i : i + 1] for i in range(3)]
    value_taps = [taps[3 + i : 4 + i] for i in range(3)]
    gain = taps[6:7]
    nothing = jnp.zeros((8, LANES), jnp.float32)

    def lay(buffer, side, place, value):
        head, tail = head_tail(value)
        count = value.shape[0]
        at = pl.ds(side * LANES, LANES)
        rhs[buffer, pl.ds(place, count), at] = head
        rhs[buffer, pl.ds(rows + place, count), at] = tail
        rhs[buffer, pl.ds(2 * rows + place, count), at] = head

    def transformed(buffer):
        return jnp.dot(forward_ref[...], rhs[buffer], preferred_element_type=jnp.float32)

    def keep_ends(index, _):
        ref = piece(in_refs, index, place)
        block = index ^ place
        for stream in (0, 1):
            start = stream * rows
            last = ref[pl.ds(start + rows - 16, 16), :].astype(jnp.float32)
            first = ref[pl.ds(start, 16), :].astype(jnp.float32)
            ends[block + 1, 2 * stream : 2 * stream + 2, :] = last[14:16]
            ends[block + 1, 2 * stream + 4 : 2 * stream + 6, :] = first[0:2]
        return 0

    ends[0] = nothing
    ends[blocks + 1] = nothing
    loop(blocks, keep_ends, 0, unrolled)

    def transform(pair, _):
        spot = 2 * pair if unrolled else 0
        for side in range(2):
            ref = piece(in_refs, 2 * pair + side, place)
            scale = ref[pl.ds(2 * rows + half_rows, 16), :].astype(jnp.float32)
            code = ref[pl.ds(2 * rows, half_rows), :].astype(jnp.float32)
            taken = decode(code, scale[0:1] + scale[8:9])
            turned = swap(taken)
            lay(spot, side, 0, jnp.where(left_half, taken, turned))
            lay(spot, side, half_rows, jnp.where(left_half, turned, taken))
        result = transformed(spot)
        for side in range(2):
            filters[(2 * pair + side) ^ place] = result[:, side * LANES : (side + 1) * LANES]
        for side in range(2):
            index = 2 * pair + side
            ref = piece(in_refs, index, place)
            outs = []
            for stream, weights in ((0, query_taps), (1, value_taps)):
                now = ref[pl.ds(stream * rows, rows), :].astype(jnp.float32)
                last = ends[index ^ place, 2 * stream : 2 * stream + 2, :]
                edged[index, stream, 6:8, :] = last
                edged[index, stream, pl.ds(8, rows), :] = now
                total = weights[0] * now
                for offset in (1, 2):
                    shifted = edged[index, stream, pl.ds(8 - offset, rows), :]
                    total = total + weights[offset] * shifted
                outs.append(total)
            first_ref[index] = outs[0]
            second_ref[index] = outs[1]
            field = outs[0] * outs[1]
            fields[index] = field
            lay(spot + 1, side, 0, field)
        result = transformed(spot + 1)
        for side in range(2):
            spectra[(2 * pair + side) ^ place] = result[:, side * LANES : (side + 1) * LANES]
        return 0

    loop(half, transform, 0, unrolled)

    chunk = 8
    left_chunk = left_lanes((chunk, LANES))
    conjugate = jnp.where(left_chunk, -1.0, 1.0)

    def products(pairs):
        one = two = three = None
        for (re, im, both), (join_re, join_less, join_more) in pairs:
            terms = join_re * both, re * join_less, im * join_more
            if one is None:
                one, two, three = terms
            else:
                one, two, three = one + terms[0], two + terms[1], three + terms[2]
        return one - three, one + two

    def spectral(step, sign):
        real_at = pl.ds(pl.multiple_of(step * chunk, chunk), chunk)
        imag_at = pl.ds(pl.multiple_of(rows + step * chunk, chunk), chunk)
        field_re = [spectra[block, real_at, :] for block in range(blocks)]
        field_im = [spectra[block, imag_at, :] for block in range(blocks)]

        def joined(re, im, block):
            if block == 0:
                return re[0], im[0]
            if sign > 0:
                return re[block] - im[block - 1], im[block] + re[block - 1]
            return re[block] + im[block - 1], im[block] - re[block - 1]

        turned = []
        for block in range(blocks):
            re = jnp.where(left_chunk, field_re[blocks - 1 - block], field_re[block])
            im = jnp.where(left_chunk, field_im[blocks - 1 - block], field_im[block])
            turned.append((re, im, re + im))
        filt_re = [filters[block, real_at, :] for block in range(blocks)]
        filt_im = [filters[block, imag_at, :] for block in range(blocks)]
        joins = []
        for block in range(blocks):
            re, im = joined(filt_re, filt_im, block)
            im = im * conjugate
            joins.append((re, im - re, re + im))
        outs = [
            products([(turned[block - lag], joins[lag]) for lag in range(block + 1)])
            for block in range(blocks)
        ]
        grads = []
        for block in range(blocks):
            re = jnp.where(left_chunk, field_re[block], swap(field_re[block]))
            im = jnp.where(left_chunk, field_im[block], swap(field_im[block]))
            grads.append((re, im, re + im))
        sums = [joined(field_re, field_im, block) for block in range(blocks)]
        joins = []
        for block in range(blocks):
            parts = []
            for part in range(2):
                far = sums[block - half][part] if block >= half else 0.0
                parts.append(jnp.where(left_chunk, swap(sums[block][part]), far))
            re, im = parts
            joins.append((re, -im - re, re - im))
        for block in range(blocks):
            for part, at in ((0, real_at), (1, imag_at)):
                spectra[block, at, :] = jnp.where(
                    left_chunk, outs[blocks - 1 - block][part], outs[block][part]
                )
        for lag in range(half):
            out = products([(grads[block], joins[block - lag]) for block in range(lag, blocks)])
            filters[lag, real_at, :] = out[0]
            filters[lag, imag_at, :] = out[1]

    trips = rows // chunk // 4

    def even(trip, _):
        for part in range(2):
            spectral(2 * trip + part, 1)
        return 0

    def odd(trip, _):
        for part in range(2):
            spectral(2 * trip + part, -1)
        return 0

    lax.fori_loop(0, trips, even, 0)
    lax.fori_loop(trips, 2 * trips, odd, 0)

    def back(values, buffer):
        for side, value in enumerate(values):
            head, tail = head_tail(value)
            at = pl.ds(side * LANES, LANES)
            rhs_back[buffer, pl.ds(0, 2 * rows), at] = head
            rhs_back[buffer, pl.ds(2 * rows, 2 * rows), at] = tail
            rhs_back[buffer, pl.ds(4 * rows, 2 * rows), at] = head
        result = jnp.dot(inverse_ref[...], rhs_back[buffer], preferred_element_type=jnp.float32)
        return result[:, :LANES], result[:, LANES:]

    def filter_grads(pair, _):
        values = filters[2 * pair], filters[2 * pair + 1]
        for side, value in enumerate(back(values, pair if unrolled else 0)):
            filters[2 * pair + side, pl.ds(0, rows), :] = value * grad_scale
        return 0

    loop(half // 2, filter_grads, 0, unrolled)

    def fold(value):
        return jnp.sum(value.reshape(rows // 8, 8, LANES), axis=0)

    def outputs(pair, totals):
        values = [spectra[(2 * pair + side) ^ place] for side in range(2)]
        results = back(values, (half // 2 + pair) if unrolled else 0)
        for side, result in enumerate(results):
            index = 2 * pair + side
            block = index ^ place
            out_ref = piece(out_refs, index, place)
            field = fields[index]
            result = result + gain * field
            scale = scale_of(result)
            out_ref[pl.ds(0, rows), :] = encode(result, scale).astype(jnp.bfloat16)
            misc[index, 0:1, :] = scale
            starts[block] = result[:8]
            turned = swap(result)
            grads = (second_ref[index] * turned, first_ref[index] * turned)
            new_totals = []
            for stream in (0, 1):
                for offset in range(3):
                    earlier = edged[index, stream, pl.ds(8 - offset, rows), :]
                    total = totals[3 * stream + offset]
                    new_totals.append(total + fold(grads[stream] * earlier))
            totals = tuple(new_totals)

            upper_half = block // half
            value = filters[lax.rem(block, half), pl.ds(0, rows), :]
            halves = join(left_half, value[:half_rows], value[half_rows:], upper_half)
            scale = scale_of(halves)
            code = encode(halves, scale).astype(jnp.bfloat16)
            out_ref[pl.ds(rows, half_rows), :] = code
            misc[index, 1:2, :] = scale
        return totals

    starts[blocks] = nothing
    totals = loop(half, outputs, (nothing,) * 6, unrolled)
    sums = [grad_scale * jnp.sum(total, axis=0, keepdims=True) for total in totals]
    shared[0:6, :] = taps[0:6]
    for row in range(6):
        value = sums[row]
        if row == 3:
            value = jnp.where(left_lanes((1, LANES)), filters[0, 0:1, :], value)
        shared[6 + row : 7 + row, :] = value
    tap_rows, sum_rows = shared[0:6, :], shared[6:12, :]
    tap_scale, sum_scale = scale_of(tap_rows), scale_of(sum_rows)
    tap_codes, sum_codes = encode(tap_rows, tap_scale), encode(sum_rows, sum_scale)

    def close(index, _):
        out_ref = piece(out_refs, index, place)
        block = index ^ place
        edge = starts[block + 1, 0:2, :]
        scale = scale_of(edge)
        misc[index, 2:3, :] = scale
        misc[index, 3:4, :] = tap_scale
        misc[index, 4:5, :] = sum_scale
        scales = misc[index, 0:5, :]
        misc[index, 5:10, :] = scales - scales.astype(jnp.bfloat16).astype(jnp.float32)
        misc[index, 10:12, :] = encode(edge, scale)
        misc[index, 12:18, :] = tap_codes
        misc[index, 18:24, :] = sum_codes
        misc[index, 24:28, :] = ends[block, 0:4, :]
        misc[index, 28:32, :] = ends[block + 2, 4:8, :]
        out_ref[pl.ds(rows + half_rows, MISC), :] = misc[index].astype(jnp.bfloat16)
        return 0

    loop(blocks, close, 0, unrolled)


def operator(taps, received, devices):
    count = len(received)
    blocks = devices
    rows = (received[0].shape[-2] - 16) * 2 // 5
    forward, inverse = transform_matrices(rows)
    wide = (blocks, rows, LANES)
    listed = count > 1

    def kernel(*refs):
        ins, (forward_ref, inverse_ref, taps_ref) = refs[:count], refs[count : count + 3]
        outs, scratch = refs[count + 3 : 2 * count + 3], refs[2 * count + 3 :]
        operator_kernel(ins, outs, forward_ref, inverse_ref, taps_ref, *scratch)

    return pl.pallas_call(
        kernel,
        out_shape=piece_shapes(devices, rows + rows // 2 + MISC),
        scratch_shapes=[
            pltpu.VMEM((blocks + 2, 8, LANES), jnp.float32),
            pltpu.VMEM((blocks + 1, 8, LANES), jnp.float32),
            pltpu.VMEM((blocks, 2, rows + 8, LANES), jnp.float32),
            pltpu.VMEM(wide, jnp.float32),
            pltpu.VMEM(wide, jnp.float32),
            pltpu.VMEM(wide, jnp.float32),
            pltpu.VMEM((blocks, 2 * rows, LANES), jnp.float32),
            pltpu.VMEM((blocks, 2 * rows, LANES), jnp.float32),
            pltpu.VMEM((blocks if listed else 2, 3 * rows, 2 * LANES), jnp.bfloat16),
            pltpu.VMEM((3 * blocks // 4 if listed else 1, 6 * rows, 2 * LANES), jnp.bfloat16),
            pltpu.VMEM((16, LANES), jnp.float32),
            pltpu.VMEM((blocks, MISC, LANES), jnp.float32),
        ],
        compiler_params=pltpu.CompilerParams(
            vmem_limit_bytes=min(4 * blocks * MEBIBYTE, VMEM_BYTES)
        ),
    )(*in_order(received, OUT_ORDER), jnp.asarray(forward), jnp.asarray(inverse), taps)


def own_taps(short_taps, skip_gain, received):
    places = lax.axis_size("seq")
    columns = lax.axis_size("chan")
    share = skip_gain.shape[0]

    def pair(one, two):
        fill = ((0, 0), (0, HALF - share))
        return jnp.concatenate([jnp.pad(one, fill), jnp.pad(two, fill)], axis=1)

    straight = jnp.concatenate([jnp.ones((1, share)), jnp.zeros((2, share))]).astype(jnp.float32)
    rows = jnp.concatenate(
        [
            pair(short_taps[0], short_taps[1]),
            pair(straight, short_taps[2]),
            pair(skip_gain[None], skip_gain[None]),
            jnp.zeros((1, LANES), jnp.float32),
        ]
    )
    route = [
        (flat, (flat % places) * columns + flat // places) for flat in range(places * columns)
    ]
    if len(received) > 1:
        unit = jnp.ones((1, 1), jnp.bfloat16)
        rows, unit, received[-1] = lax.optimization_barrier((rows, unit, received[-1]))
        received[0] = received[0] * unit
    return lax.ppermute(rows, ("seq", "chan"), route), received


def spread(value, devices):
    rows, channels = value.shape
    share = channels // devices
    if share == HALF:
        return value
    wide = jnp.pad(value.reshape(rows, devices, share), ((0, 0), (0, 0), (0, HALF - share)))
    return wide.reshape(rows, devices * HALF)


def gathered(value, share):
    if share == HALF:
        return value
    groups = value.reshape(*value.shape[:-1], value.shape[-1] // HALF, HALF)[..., :share]
    return groups.reshape(*value.shape[:-1], -1)


def per_device(query_rows, key_rows, value_rows, long_filter, short_taps, skip_gain, cotangent):
    devices = lax.axis_size("seq")
    share = query_rows.shape[1] // devices
    streams = [spread(value, devices) for value in (query_rows, key_rows, value_rows)]
    upstream = spread(cotangent, devices)
    received = exchange(pack(streams, upstream, spread(long_filter, devices), devices))
    taps, received = own_taps(short_taps, skip_gain, received)
    results = exchange(operator(taps, received, devices))
    outs = finish(results, streams, upstream)
    *outs, skip_grad = (gathered(value, share) for value in outs)
    return (*outs, skip_grad[0])


def solution(mesh):
    in_specs = (
        P("seq", "chan"),
        P("seq", "chan"),
        P("seq", "chan"),
        P("seq", "chan"),
        P(None, None, ("seq", "chan")),
        P(("seq", "chan")),
        P("seq", "chan"),
    )
    out_specs = (
        P("seq", "chan"),
        P("seq", "chan"),
        P("seq", "chan"),
        P("seq", "chan"),
        P("seq", "chan"),
        P(None, None, "chan"),
        P("chan"),
    )
    return jax.shard_map(
        per_device, mesh=mesh, in_specs=in_specs, out_specs=out_specs, check_vma=False
    )
```

```python
import functools
import math

import jax
import jax.numpy as jnp
import numpy as np
from jax import lax
from jax.experimental import pallas as pl
from jax.experimental.pallas import tpu as pltpu
from jax.sharding import PartitionSpec as P

HALF = 64
LANES = 2 * HALF
MISC = 32
SPAN = 252.0
FLOOR = 125.0
MEBIBYTE = 1024 * 1024
VMEM_BYTES = 62 * MEBIBYTE
LISTED = 8
OUT_ORDER = (0, 7, 6, 3, 2, 5, 4, 1)
PACK_STEPS = ((3,), (1, 2, 0))
BACK_ORDER = (0, 7, 2, 5, 4, 6, 3, 1)


def swap(value):
    return pltpu.roll(value, HALF, 1)


def left_lanes(shape):
    return lax.broadcasted_iota(jnp.int32, shape, 1) < HALF


def head_tail(value):
    head = value.astype(jnp.bfloat16)
    tail = (value - head.astype(jnp.float32)).astype(jnp.bfloat16)
    return head, tail


def transform_matrices(rows):
    freq = np.concatenate([np.arange(0, rows, 2), np.arange(1, rows, 2)])
    turn = (2 * freq[:, None] + 1) * np.arange(rows)[None, :] % (4 * rows)
    theta = turn * (math.pi / (2 * rows))
    forward = np.concatenate([np.cos(theta), -np.sin(theta)])
    inverse = forward.T / rows

    def split(matrix):
        single = matrix.astype(np.float32)
        head = single.astype(jnp.bfloat16)
        tail = (single - head.astype(np.float32)).astype(jnp.bfloat16)
        return np.concatenate([head, head, tail], axis=1)

    return split(forward), split(inverse)


def encode(value, scale):
    code = jnp.exp2(jnp.abs(value) * (SPAN / scale) - FLOOR)
    return jnp.where(value < 0.0, -code, code)


def decode(code, scale):
    size = (jnp.log2(jnp.abs(code)) + FLOOR) * (scale * (1.0 / SPAN))
    return jnp.where(code < 0.0, -size, size)


def scale_of(value):
    peak = jnp.max(jnp.abs(value), axis=0, keepdims=True)
    return jnp.maximum(peak * 1.0001, 1e-34)


def loop(count, body, carry, unrolled):
    if unrolled:
        for index in range(count):
            carry = body(index, carry)
        return carry
    return lax.fori_loop(0, count, body, carry)


def piece(refs, index, place):
    return refs[index] if len(refs) > 1 else refs[0].at[index ^ place]


def exchange(pieces):
    if len(pieces) == 1:
        return [lax.all_to_all(pieces[0], "seq", 0, 0, tiled=True)]
    others = [
        lax.ppermute(value, "seq", [(one, one ^ index) for one in range(len(pieces))])
        for index, value in enumerate(pieces[1:], 1)
    ]
    return [pieces[0], *others]


def in_order(pieces, order):
    return [pieces[index] for index in order] if len(pieces) > 1 else pieces


def by_index(refs, order):
    if len(refs) == 1:
        return refs
    return [refs[order.index(index)] for index in range(len(refs))]


def piece_shapes(devices, rows):
    if devices == LISTED:
        return [jax.ShapeDtypeStruct((rows, LANES), jnp.bfloat16)] * devices
    return [jax.ShapeDtypeStruct((devices, rows, LANES), jnp.bfloat16)]


def join(mask, one, two, side):
    return jnp.where(mask, pltpu.roll(one, side * HALF, 1), pltpu.roll(two, HALF - side * HALF, 1))


def pack_kernel(steps, *refs):
    low_refs, filter_ref, refs = refs[:4], refs[4], refs[5:]
    low, high, staged, in_sems, out_sems = refs[-5:]
    out_refs = refs[:-5]
    rows, channels = filter_ref.shape
    devices = channels // HALF
    half = rows // 2
    place = lax.axis_index("seq")
    left = left_lanes((rows, LANES))
    left_half = left_lanes((half, LANES))
    copies = {}
    for step in steps:
        tile = step ^ (place // 2)
        at = pl.ds(pl.multiple_of(tile * LANES, LANES), LANES)
        pairs = [(ref.at[:, at], low.at[step, stream]) for stream, ref in enumerate(low_refs)]
        pairs.append((filter_ref.at[:, at], high.at[step]))
        copies[step] = [
            pltpu.make_async_copy(source, target, in_sems.at[step, stream])
            for stream, (source, target) in enumerate(pairs)
        ]
        for copy in copies[step]:
            copy.start()
    leaving = []
    for step in steps:
        for copy in copies[step]:
            copy.wait()
        for index in (2 * step + 1, 2 * step):
            side = lax.rem(index ^ place, 2)
            for first, second, start in ((0, 1, 0), (3, 2, rows)):
                one = low[step, first].astype(jnp.float32)
                two = low[step, second].astype(jnp.float32)
                joined = join(left, one, two, side).astype(jnp.bfloat16)
                staged[index, pl.ds(start, rows), :] = joined
            pair = join(left_half, high[step, :half], high[step, half:], side)
            scale = scale_of(pair)
            staged[index, pl.ds(2 * rows, half), :] = encode(pair, scale).astype(jnp.bfloat16)
            head, tail = head_tail(jnp.broadcast_to(scale, (8, LANES)))
            both = jnp.concatenate([head.astype(jnp.float32), tail.astype(jnp.float32)], axis=0)
            staged[index, pl.ds(2 * rows + half, 16), :] = both.astype(jnp.bfloat16)
            if len(out_refs) == 1:
                target = out_refs[0].at[index ^ place]
            else:
                target = out_refs[2 * steps.index(step) + index % 2]
            leaving.append(pltpu.make_async_copy(staged.at[index], target, out_sems.at[index]))
            leaving[-1].start()
    for copy in leaving:
        copy.wait()


def pack_steps(arrays, devices, steps):
    rows = arrays[-1].shape[0]
    sent_rows = 2 * rows + rows // 2 + 16
    shapes = piece_shapes(devices, sent_rows)
    if len(shapes) > 1:
        shapes = shapes[: 2 * len(steps)]
    anywhere = pl.BlockSpec(memory_space=pl.ANY)
    return pl.pallas_call(
        functools.partial(pack_kernel, steps),
        in_specs=[anywhere] * 5,
        out_specs=[anywhere] * len(shapes),
        out_shape=shapes,
        scratch_shapes=[
            pltpu.VMEM((devices // 2, 4, rows, LANES), jnp.bfloat16),
            pltpu.VMEM((devices // 2, rows, LANES), jnp.float32),
            pltpu.VMEM((devices, sent_rows, LANES), jnp.bfloat16),
            pltpu.SemaphoreType.DMA((devices // 2, 5)),
            pltpu.SemaphoreType.DMA((devices,)),
        ],
        compiler_params=pltpu.CompilerParams(vmem_limit_bytes=VMEM_BYTES),
    )(*arrays)


def pack(streams, cotangent, long_filter, devices):
    arrays = (*streams, cotangent, long_filter)
    if devices != LISTED:
        return pack_steps(arrays, devices, tuple(range(devices // 2)))
    pieces = [None] * devices
    for steps in PACK_STEPS:
        made = pack_steps(arrays, devices, steps)
        for at, step in enumerate(steps):
            pieces[2 * step], pieces[2 * step + 1] = made[2 * at], made[2 * at + 1]
    return pieces


def finish_kernel(
    pieces, query_ref, key_ref, value_ref, cot_ref, gated_out, query_out, key_out, value_out,
    filter_out, taps_out, skip_out, before, after,
):
    in_refs = by_index(pieces, BACK_ORDER)
    rows, channels = query_ref.shape
    half = rows // 2
    place = lax.axis_index("seq")
    odd = lax.rem(place, 2) == 1
    left = left_lanes((rows, LANES))
    left_half = left_lanes((half, LANES))

    def one_tile(step, _):
        refs = piece(in_refs, 2 * step, place), piece(in_refs, 2 * step + 1, place)
        at = pl.ds(pl.multiple_of((step ^ (place // 2)) * LANES, LANES), LANES)

        def both(start, count):
            one, two = (ref[pl.ds(start, count), :].astype(jnp.float32) for ref in refs)
            return jnp.where(odd, two, one), jnp.where(odd, one, two)

        def sides(mask, values):
            one, two = values
            return jnp.where(mask, one, swap(two)), jnp.where(mask, swap(one), two)

        miscs = both(rows + half, MISC)
        scales = [misc[0:5] + misc[5:10] for misc in miscs]

        def small(start, stop, scale):
            return [
                decode(misc[start:stop], row[scale : scale + 1])
                for misc, row in zip(miscs, scales)
            ]

        codes = both(0, rows)
        back, mixed = sides(left, [decode(code, row[0:1]) for code, row in zip(codes, scales)])
        codes = both(rows, half)
        upper, lower = sides(
            left_half, [decode(code, row[1:2]) for code, row in zip(codes, scales)]
        )
        filter_out[pl.ds(0, half), at] = upper
        filter_out[pl.ds(half, half), at] = lower
        ends = sides(left_lanes((8, LANES)), [misc[24:32] for misc in miscs])
        lefts, rights = sides(left_lanes((6, LANES)), small(12, 18, 3))
        taps = (lefts[0:3], rights[0:3], rights[3:6])
        lefts, rights = sides(left_lanes((6, LANES)), small(18, 24, 4))
        for offset in range(3):
            taps_out[0, offset : offset + 1, at] = lefts[offset : offset + 1]
            taps_out[1, offset : offset + 1, at] = rights[offset : offset + 1]
            taps_out[2, offset : offset + 1, at] = rights[3 + offset : 4 + offset]
        skip_out[0:1, at] = lefts[3:4]
        back_edge, mixed_edge = sides(left_lanes((2, LANES)), small(10, 12, 2))
        convs, edges = [], []
        for stream, (source, end, row) in enumerate(
            ((query_ref, ends[0], 0), (key_ref, ends[1], 0), (value_ref, ends[1], 2))
        ):
            now = source[:, at].astype(jnp.float32)
            before[stream, 6:8, :] = end[row : row + 2]
            before[stream, pl.ds(8, rows), :] = now
            before[stream, pl.ds(8 + rows, 2), :] = end[row + 4 : row + 6]
            conv = taps[stream][0:1] * now
            edge = taps[stream][0:1] * end[row + 4 : row + 6]
            for offset in (1, 2):
                weight = taps[stream][offset : offset + 1]
                conv = conv + weight * before[stream, pl.ds(8 - offset, rows), :]
                edge = edge + weight * before[stream, pl.ds(8 + rows - offset, 2), :]
            convs.append(conv)
            edges.append(edge)
        cotangent = cot_ref[:, at].astype(jnp.float32)
        cot_edge = ends[0][6:8]
        gated_out[:, at] = (convs[0] * mixed).astype(jnp.bfloat16)
        for stream, (out, grad, edge) in enumerate(
            (
                (query_out, cotangent * mixed, cot_edge * mixed_edge),
                (key_out, back * convs[2], back_edge * edges[2]),
                (value_out, back * convs[1], back_edge * edges[1]),
            )
        ):
            after[stream, pl.ds(0, rows), :] = grad
            after[stream, pl.ds(rows, 2), :] = edge
            total = taps[stream][0:1] * grad
            for offset in (1, 2):
                weight = taps[stream][offset : offset + 1]
                total = total + weight * after[stream, pl.ds(offset, rows), :]
            out[:, at] = total.astype(jnp.bfloat16)
        return 0

    loop(channels // LANES, one_tile, 0, len(in_refs) > 1)


def finish(received, streams, cotangent):
    rows, channels = cotangent.shape
    count = len(received)
    low = jax.ShapeDtypeStruct((rows, channels), jnp.bfloat16)

    def kernel(*refs):
        finish_kernel(refs[:count], *refs[count:])

    return pl.pallas_call(
        kernel,
        out_shape=(
            low,
            low,
            low,
            low,
            jax.ShapeDtypeStruct((rows, channels), jnp.float32),
            jax.ShapeDtypeStruct((3, 3, channels), jnp.float32),
            jax.ShapeDtypeStruct((1, channels), jnp.float32),
        ),
        scratch_shapes=[
            pltpu.VMEM((3, rows + 16, LANES), jnp.float32),
            pltpu.VMEM((3, rows + 8, LANES), jnp.float32),
        ],
        compiler_params=pltpu.CompilerParams(
            vmem_limit_bytes=3 * (channels // HALF) * MEBIBYTE // 2
        ),
    )(*in_order(received, BACK_ORDER), *streams, cotangent)


def operator_kernel(
    pieces, out_refs, forward_ref, inverse_ref, taps_ref,
    ends, starts, edged, first_ref, second_ref, fields, spectra, filters, rhs, rhs_back,
    shared, misc,
):
    in_refs = by_index(pieces, OUT_ORDER)
    blocks = fields.shape[0]
    place = lax.axis_index("seq")
    rows = forward_ref.shape[0] // 2
    half = blocks // 2
    half_rows = rows // 2
    unrolled = len(in_refs) > 1
    grad_scale = 1.0 / math.sqrt(blocks * rows)
    left = left_lanes((rows, LANES))
    left_half = left_lanes((half_rows, LANES))
    taps = taps_ref[...]
    query_taps = [taps[i : i + 1] for i in range(3)]
    value_taps = [taps[3 + i : 4 + i] for i in range(3)]
    gain = taps[6:7]
    nothing = jnp.zeros((8, LANES), jnp.float32)

    def lay(buffer, side, place, value):
        head, tail = head_tail(value)
        count = value.shape[0]
        at = pl.ds(side * LANES, LANES)
        rhs[buffer, pl.ds(place, count), at] = head
        rhs[buffer, pl.ds(rows + place, count), at] = tail
        rhs[buffer, pl.ds(2 * rows + place, count), at] = head

    def transformed(buffer):
        return jnp.dot(forward_ref[...], rhs[buffer], preferred_element_type=jnp.float32)

    def keep_ends(index, _):
        ref = piece(in_refs, index, place)
        block = index ^ place
        for stream in (0, 1):
            start = stream * rows
            last = ref[pl.ds(start + rows - 16, 16), :].astype(jnp.float32)
            first = ref[pl.ds(start, 16), :].astype(jnp.float32)
            ends[block + 1, 2 * stream : 2 * stream + 2, :] = last[14:16]
            ends[block + 1, 2 * stream + 4 : 2 * stream + 6, :] = first[0:2]
        return 0

    ends[0] = nothing
    ends[blocks + 1] = nothing
    loop(blocks, keep_ends, 0, unrolled)

    def transform(pair, _):
        spot = 2 * pair if unrolled else 0
        for side in range(2):
            ref = piece(in_refs, 2 * pair + side, place)
            scale = ref[pl.ds(2 * rows + half_rows, 16), :].astype(jnp.float32)
            code = ref[pl.ds(2 * rows, half_rows), :].astype(jnp.float32)
            taken = decode(code, scale[0:1] + scale[8:9])
            turned = swap(taken)
            lay(spot, side, 0, jnp.where(left_half, taken, turned))
            lay(spot, side, half_rows, jnp.where(left_half, turned, taken))
        result = transformed(spot)
        for side in range(2):
            filters[(2 * pair + side) ^ place] = result[:, side * LANES : (side + 1) * LANES]
        for side in range(2):
            index = 2 * pair + side
            ref = piece(in_refs, index, place)
            outs = []
            for stream, weights in ((0, query_taps), (1, value_taps)):
                now = ref[pl.ds(stream * rows, rows), :].astype(jnp.float32)
                last = ends[index ^ place, 2 * stream : 2 * stream + 2, :]
                edged[index, stream, 6:8, :] = last
                edged[index, stream, pl.ds(8, rows), :] = now
                total = weights[0] * now
                for offset in (1, 2):
                    shifted = edged[index, stream, pl.ds(8 - offset, rows), :]
                    total = total + weights[offset] * shifted
                outs.append(total)
            first_ref[index] = outs[0]
            second_ref[index] = outs[1]
            field = outs[0] * outs[1]
            fields[index] = field
            lay(spot + 1, side, 0, field)
        result = transformed(spot + 1)
        for side in range(2):
            spectra[(2 * pair + side) ^ place] = result[:, side * LANES : (side + 1) * LANES]
        return 0

    loop(half, transform, 0, unrolled)

    chunk = 8
    left_chunk = left_lanes((chunk, LANES))
    conjugate = jnp.where(left_chunk, -1.0, 1.0)

    def products(pairs):
        one = two = three = None
        for (re, im, both), (join_re, join_less, join_more) in pairs:
            terms = join_re * both, re * join_less, im * join_more
            if one is None:
                one, two, three = terms
            else:
                one, two, three = one + terms[0], two + terms[1], three + terms[2]
        return one - three, one + two

    def spectral(step, sign):
        real_at = pl.ds(pl.multiple_of(step * chunk, chunk), chunk)
        imag_at = pl.ds(pl.multiple_of(rows + step * chunk, chunk), chunk)
        field_re = [spectra[block, real_at, :] for block in range(blocks)]
        field_im = [spectra[block, imag_at, :] for block in range(blocks)]

        def joined(re, im, block):
            if block == 0:
                return re[0], im[0]
            if sign > 0:
                return re[block] - im[block - 1], im[block] + re[block - 1]
            return re[block] + im[block - 1], im[block] - re[block - 1]

        turned = []
        for block in range(blocks):
            re = jnp.where(left_chunk, field_re[blocks - 1 - block], field_re[block])
            im = jnp.where(left_chunk, field_im[blocks - 1 - block], field_im[block])
            turned.append((re, im, re + im))
        filt_re = [filters[block, real_at, :] for block in range(blocks)]
        filt_im = [filters[block, imag_at, :] for block in range(blocks)]
        joins = []
        for block in range(blocks):
            re, im = joined(filt_re, filt_im, block)
            im = im * conjugate
            joins.append((re, im - re, re + im))
        outs = [
            products([(turned[block - lag], joins[lag]) for lag in range(block + 1)])
            for block in range(blocks)
        ]
        grads = []
        for block in range(blocks):
            re = jnp.where(left_chunk, field_re[block], swap(field_re[block]))
            im = jnp.where(left_chunk, field_im[block], swap(field_im[block]))
            grads.append((re, im, re + im))
        sums = [joined(field_re, field_im, block) for block in range(blocks)]
        joins = []
        for block in range(blocks):
            parts = []
            for part in range(2):
                far = sums[block - half][part] if block >= half else 0.0
                parts.append(jnp.where(left_chunk, swap(sums[block][part]), far))
            re, im = parts
            joins.append((re, -im - re, re - im))
        for block in range(blocks):
            for part, at in ((0, real_at), (1, imag_at)):
                spectra[block, at, :] = jnp.where(
                    left_chunk, outs[blocks - 1 - block][part], outs[block][part]
                )
        for lag in range(half):
            out = products([(grads[block], joins[block - lag]) for block in range(lag, blocks)])
            filters[lag, real_at, :] = out[0]
            filters[lag, imag_at, :] = out[1]

    trips = rows // chunk // 4

    def even(trip, _):
        for part in range(2):
            spectral(2 * trip + part, 1)
        return 0

    def odd(trip, _):
        for part in range(2):
            spectral(2 * trip + part, -1)
        return 0

    lax.fori_loop(0, trips, even, 0)
    lax.fori_loop(trips, 2 * trips, odd, 0)

    def back(values, buffer):
        for side, value in enumerate(values):
            head, tail = head_tail(value)
            at = pl.ds(side * LANES, LANES)
            rhs_back[buffer, pl.ds(0, 2 * rows), at] = head
            rhs_back[buffer, pl.ds(2 * rows, 2 * rows), at] = tail
            rhs_back[buffer, pl.ds(4 * rows, 2 * rows), at] = head
        result = jnp.dot(inverse_ref[...], rhs_back[buffer], preferred_element_type=jnp.float32)
        return result[:, :LANES], result[:, LANES:]

    def filter_grads(pair, _):
        values = filters[2 * pair], filters[2 * pair + 1]
        for side, value in enumerate(back(values, pair if unrolled else 0)):
            filters[2 * pair + side, pl.ds(0, rows), :] = value * grad_scale
        return 0

    loop(half // 2, filter_grads, 0, unrolled)

    def fold(value):
        return jnp.sum(value.reshape(rows // 8, 8, LANES), axis=0)

    def outputs(pair, totals):
        values = [spectra[(2 * pair + side) ^ place] for side in range(2)]
        results = back(values, (half // 2 + pair) if unrolled else 0)
        for side, result in enumerate(results):
            index = 2 * pair + side
            block = index ^ place
            out_ref = piece(out_refs, index, place)
            field = fields[index]
            result = result + gain * field
            scale = scale_of(result)
            out_ref[pl.ds(0, rows), :] = encode(result, scale).astype(jnp.bfloat16)
            misc[index, 0:1, :] = scale
            starts[block] = result[:8]
            turned = swap(result)
            grads = (second_ref[index] * turned, first_ref[index] * turned)
            new_totals = []
            for stream in (0, 1):
                for offset in range(3):
                    earlier = edged[index, stream, pl.ds(8 - offset, rows), :]
                    total = totals[3 * stream + offset]
                    new_totals.append(total + fold(grads[stream] * earlier))
            totals = tuple(new_totals)

            upper_half = block // half
            value = filters[lax.rem(block, half), pl.ds(0, rows), :]
            halves = join(left_half, value[:half_rows], value[half_rows:], upper_half)
            scale = scale_of(halves)
            code = encode(halves, scale).astype(jnp.bfloat16)
            out_ref[pl.ds(rows, half_rows), :] = code
            misc[index, 1:2, :] = scale
        return totals

    starts[blocks] = nothing
    totals = loop(half, outputs, (nothing,) * 6, unrolled)
    sums = [grad_scale * jnp.sum(total, axis=0, keepdims=True) for total in totals]
    shared[0:6, :] = taps[0:6]
    for row in range(6):
        value = sums[row]
        if row == 3:
            value = jnp.where(left_lanes((1, LANES)), filters[0, 0:1, :], value)
        shared[6 + row : 7 + row, :] = value
    tap_rows, sum_rows = shared[0:6, :], shared[6:12, :]
    tap_scale, sum_scale = scale_of(tap_rows), scale_of(sum_rows)
    tap_codes, sum_codes = encode(tap_rows, tap_scale), encode(sum_rows, sum_scale)

    def close(index, _):
        out_ref = piece(out_refs, index, place)
        block = index ^ place
        edge = starts[block + 1, 0:2, :]
        scale = scale_of(edge)
        misc[index, 2:3, :] = scale
        misc[index, 3:4, :] = tap_scale
        misc[index, 4:5, :] = sum_scale
        scales = misc[index, 0:5, :]
        misc[index, 5:10, :] = scales - scales.astype(jnp.bfloat16).astype(jnp.float32)
        misc[index, 10:12, :] = encode(edge, scale)
        misc[index, 12:18, :] = tap_codes
        misc[index, 18:24, :] = sum_codes
        misc[index, 24:28, :] = ends[block, 0:4, :]
        misc[index, 28:32, :] = ends[block + 2, 4:8, :]
        out_ref[pl.ds(rows + half_rows, MISC), :] = misc[index].astype(jnp.bfloat16)
        return 0

    loop(blocks, close, 0, unrolled)


def operator(taps, received, devices):
    count = len(received)
    blocks = devices
    rows = (received[0].shape[-2] - 16) * 2 // 5
    forward, inverse = transform_matrices(rows)
    wide = (blocks, rows, LANES)
    listed = count > 1

    def kernel(*refs):
        ins, (forward_ref, inverse_ref, taps_ref) = refs[:count], refs[count : count + 3]
        outs, scratch = refs[count + 3 : 2 * count + 3], refs[2 * count + 3 :]
        operator_kernel(ins, outs, forward_ref, inverse_ref, taps_ref, *scratch)

    return pl.pallas_call(
        kernel,
        out_shape=piece_shapes(devices, rows + rows // 2 + MISC),
        scratch_shapes=[
            pltpu.VMEM((blocks + 2, 8, LANES), jnp.float32),
            pltpu.VMEM((blocks + 1, 8, LANES), jnp.float32),
            pltpu.VMEM((blocks, 2, rows + 8, LANES), jnp.float32),
            pltpu.VMEM(wide, jnp.float32),
            pltpu.VMEM(wide, jnp.float32),
            pltpu.VMEM(wide, jnp.float32),
            pltpu.VMEM((blocks, 2 * rows, LANES), jnp.float32),
            pltpu.VMEM((blocks, 2 * rows, LANES), jnp.float32),
            pltpu.VMEM((blocks if listed else 2, 3 * rows, 2 * LANES), jnp.bfloat16),
            pltpu.VMEM((3 * blocks // 4 if listed else 1, 6 * rows, 2 * LANES), jnp.bfloat16),
            pltpu.VMEM((16, LANES), jnp.float32),
            pltpu.VMEM((blocks, MISC, LANES), jnp.float32),
        ],
        compiler_params=pltpu.CompilerParams(
            vmem_limit_bytes=min(4 * blocks * MEBIBYTE, VMEM_BYTES)
        ),
    )(*in_order(received, OUT_ORDER), jnp.asarray(forward), jnp.asarray(inverse), taps)


def own_taps(short_taps, skip_gain, received):
    places = lax.axis_size("seq")
    columns = lax.axis_size("chan")
    share = skip_gain.shape[0]

    def pair(one, two):
        fill = ((0, 0), (0, HALF - share))
        return jnp.concatenate([jnp.pad(one, fill), jnp.pad(two, fill)], axis=1)

    straight = jnp.concatenate([jnp.ones((1, share)), jnp.zeros((2, share))]).astype(jnp.float32)
    rows = jnp.concatenate(
        [
            pair(short_taps[0], short_taps[1]),
            pair(straight, short_taps[2]),
            pair(skip_gain[None], skip_gain[None]),
            jnp.zeros((1, LANES), jnp.float32),
        ]
    )
    route = [
        (flat, (flat % places) * columns + flat // places) for flat in range(places * columns)
    ]
    if len(received) > 1:
        unit = jnp.ones((1, 1), jnp.bfloat16)
        rows, unit, received[-1] = lax.optimization_barrier((rows, unit, received[-1]))
        received[0] = received[0] * unit
    return lax.ppermute(rows, ("seq", "chan"), route), received


def spread(value, devices):
    rows, channels = value.shape
    share = channels // devices
    if share == HALF:
        return value
    wide = jnp.pad(value.reshape(rows, devices, share), ((0, 0), (0, 0), (0, HALF - share)))
    return wide.reshape(rows, devices * HALF)


def gathered(value, share):
    if share == HALF:
        return value
    groups = value.reshape(*value.shape[:-1], value.shape[-1] // HALF, HALF)[..., :share]
    return groups.reshape(*value.shape[:-1], -1)


def per_device(query_rows, key_rows, value_rows, long_filter, short_taps, skip_gain, cotangent):
    devices = lax.axis_size("seq")
    share = query_rows.shape[1] // devices
    streams = [spread(value, devices) for value in (query_rows, key_rows, value_rows)]
    upstream = spread(cotangent, devices)
    received = exchange(pack(streams, upstream, spread(long_filter, devices), devices))
    taps, received = own_taps(short_taps, skip_gain, received)
    results = exchange(operator(taps, received, devices))
    outs = finish(results, streams, upstream)
    *outs, skip_grad = (gathered(value, share) for value in outs)
    return (*outs, skip_grad[0])


def solution(mesh):
    in_specs = (
        P("seq", "chan"),
        P("seq", "chan"),
        P("seq", "chan"),
        P("seq", "chan"),
        P(None, None, ("seq", "chan")),
        P(("seq", "chan")),
        P("seq", "chan"),
    )
    out_specs = (
        P("seq", "chan"),
        P("seq", "chan"),
        P("seq", "chan"),
        P("seq", "chan"),
        P("seq", "chan"),
        P(None, None, "chan"),
        P("chan"),
    )
    return jax.shard_map(
        per_device, mesh=mesh, in_specs=in_specs, out_specs=out_specs, check_vma=False
    )
```

```python
import functools
import math

import jax
import jax.numpy as jnp
import numpy as np
from jax import lax
from jax.experimental import pallas as pl
from jax.experimental.pallas import tpu as pltpu
from jax.sharding import PartitionSpec as P

HALF = 64
LANES = 2 * HALF
MISC = 32
SPAN = 252.0
FLOOR = 125.0
MEBIBYTE = 1024 * 1024
VMEM_BYTES = 62 * MEBIBYTE
LISTED = 8
OUT_ORDER = (0, 7, 6, 3, 2, 5, 4, 1)
PACK_STEPS = ((3,), (1, 2, 0))
BACK_ORDER = (0, 7, 2, 5, 4, 3, 6, 1)


def swap(value):
    return pltpu.roll(value, HALF, 1)


def left_lanes(shape):
    return lax.broadcasted_iota(jnp.int32, shape, 1) < HALF


def head_tail(value):
    head = value.astype(jnp.bfloat16)
    tail = (value - head.astype(jnp.float32)).astype(jnp.bfloat16)
    return head, tail


def transform_matrices(rows):
    freq = np.concatenate([np.arange(0, rows, 2), np.arange(1, rows, 2)])
    turn = (2 * freq[:, None] + 1) * np.arange(rows)[None, :] % (4 * rows)
    theta = turn * (math.pi / (2 * rows))
    forward = np.concatenate([np.cos(theta), -np.sin(theta)])
    inverse = forward.T / rows

    def split(matrix):
        single = matrix.astype(np.float32)
        head = single.astype(jnp.bfloat16)
        tail = (single - head.astype(np.float32)).astype(jnp.bfloat16)
        return np.concatenate([head, head, tail], axis=1)

    return split(forward), split(inverse)


def encode(value, scale):
    code = jnp.exp2(jnp.abs(value) * (SPAN / scale) - FLOOR)
    return jnp.where(value < 0.0, -code, code)


def decode(code, scale):
    size = (jnp.log2(jnp.abs(code)) + FLOOR) * (scale * (1.0 / SPAN))
    return jnp.where(code < 0.0, -size, size)


def scale_of(value):
    peak = jnp.max(jnp.abs(value), axis=0, keepdims=True)
    return jnp.maximum(peak * 1.0001, 1e-34)


def loop(count, body, carry, unrolled):
    if unrolled:
        for index in range(count):
            carry = body(index, carry)
        return carry
    return lax.fori_loop(0, count, body, carry)


def piece(refs, index, place):
    return refs[index] if len(refs) > 1 else refs[0].at[index ^ place]


def exchange(pieces):
    if len(pieces) == 1:
        return [lax.all_to_all(pieces[0], "seq", 0, 0, tiled=True)]
    others = [
        lax.ppermute(value, "seq", [(one, one ^ index) for one in range(len(pieces))])
        for index, value in enumerate(pieces[1:], 1)
    ]
    return [pieces[0], *others]


def in_order(pieces, order):
    return [pieces[index] for index in order] if len(pieces) > 1 else pieces


def by_index(refs, order):
    if len(refs) == 1:
        return refs
    return [refs[order.index(index)] for index in range(len(refs))]


def piece_shapes(devices, rows):
    if devices == LISTED:
        return [jax.ShapeDtypeStruct((rows, LANES), jnp.bfloat16)] * devices
    return [jax.ShapeDtypeStruct((devices, rows, LANES), jnp.bfloat16)]


def join(mask, one, two, side):
    return jnp.where(mask, pltpu.roll(one, side * HALF, 1), pltpu.roll(two, HALF - side * HALF, 1))


def pack_kernel(steps, *refs):
    low_refs, filter_ref, refs = refs[:4], refs[4], refs[5:]
    low, high, staged, in_sems, out_sems = refs[-5:]
    out_refs = refs[:-5]
    rows, channels = filter_ref.shape
    devices = channels // HALF
    half = rows // 2
    place = lax.axis_index("seq")
    left = left_lanes((rows, LANES))
    left_half = left_lanes((half, LANES))
    copies = {}
    for step in steps:
        tile = step ^ (place // 2)
        at = pl.ds(pl.multiple_of(tile * LANES, LANES), LANES)
        pairs = [(ref.at[:, at], low.at[step, stream]) for stream, ref in enumerate(low_refs)]
        pairs.append((filter_ref.at[:, at], high.at[step]))
        copies[step] = [
            pltpu.make_async_copy(source, target, in_sems.at[step, stream])
            for stream, (source, target) in enumerate(pairs)
        ]
        for copy in copies[step]:
            copy.start()
    leaving = []
    for step in steps:
        for copy in copies[step]:
            copy.wait()
        for index in (2 * step + 1, 2 * step):
            side = lax.rem(index ^ place, 2)
            for first, second, start in ((0, 1, 0), (3, 2, rows)):
                one = low[step, first].astype(jnp.float32)
                two = low[step, second].astype(jnp.float32)
                joined = join(left, one, two, side).astype(jnp.bfloat16)
                staged[index, pl.ds(start, rows), :] = joined
            pair = join(left_half, high[step, :half], high[step, half:], side)
            scale = scale_of(pair)
            staged[index, pl.ds(2 * rows, half), :] = encode(pair, scale).astype(jnp.bfloat16)
            head, tail = head_tail(jnp.broadcast_to(scale, (8, LANES)))
            both = jnp.concatenate([head.astype(jnp.float32), tail.astype(jnp.float32)], axis=0)
            staged[index, pl.ds(2 * rows + half, 16), :] = both.astype(jnp.bfloat16)
            if len(out_refs) == 1:
                target = out_refs[0].at[index ^ place]
            else:
                target = out_refs[2 * steps.index(step) + index % 2]
            leaving.append(pltpu.make_async_copy(staged.at[index], target, out_sems.at[index]))
            leaving[-1].start()
    for copy in leaving:
        copy.wait()


def pack_steps(arrays, devices, steps):
    rows = arrays[-1].shape[0]
    sent_rows = 2 * rows + rows // 2 + 16
    shapes = piece_shapes(devices, sent_rows)
    if len(shapes) > 1:
        shapes = shapes[: 2 * len(steps)]
    anywhere = pl.BlockSpec(memory_space=pl.ANY)
    return pl.pallas_call(
        functools.partial(pack_kernel, steps),
        in_specs=[anywhere] * 5,
        out_specs=[anywhere] * len(shapes),
        out_shape=shapes,
        scratch_shapes=[
            pltpu.VMEM((devices // 2, 4, rows, LANES), jnp.bfloat16),
            pltpu.VMEM((devices // 2, rows, LANES), jnp.float32),
            pltpu.VMEM((devices, sent_rows, LANES), jnp.bfloat16),
            pltpu.SemaphoreType.DMA((devices // 2, 5)),
            pltpu.SemaphoreType.DMA((devices,)),
        ],
        compiler_params=pltpu.CompilerParams(vmem_limit_bytes=VMEM_BYTES),
    )(*arrays)


def pack(streams, cotangent, long_filter, devices):
    arrays = (*streams, cotangent, long_filter)
    if devices != LISTED:
        return pack_steps(arrays, devices, tuple(range(devices // 2)))
    pieces = [None] * devices
    for steps in PACK_STEPS:
        made = pack_steps(arrays, devices, steps)
        for at, step in enumerate(steps):
            pieces[2 * step], pieces[2 * step + 1] = made[2 * at], made[2 * at + 1]
    return pieces


def finish_kernel(
    pieces, query_ref, key_ref, value_ref, cot_ref, gated_out, query_out, key_out, value_out,
    filter_out, taps_out, skip_out, before, after,
):
    in_refs = by_index(pieces, BACK_ORDER)
    rows, channels = query_ref.shape
    half = rows // 2
    place = lax.axis_index("seq")
    odd = lax.rem(place, 2) == 1
    left = left_lanes((rows, LANES))
    left_half = left_lanes((half, LANES))

    def one_tile(step, _):
        refs = piece(in_refs, 2 * step, place), piece(in_refs, 2 * step + 1, place)
        at = pl.ds(pl.multiple_of((step ^ (place // 2)) * LANES, LANES), LANES)

        def both(start, count):
            one, two = (ref[pl.ds(start, count), :].astype(jnp.float32) for ref in refs)
            return jnp.where(odd, two, one), jnp.where(odd, one, two)

        def sides(mask, values):
            one, two = values
            return jnp.where(mask, one, swap(two)), jnp.where(mask, swap(one), two)

        miscs = both(rows + half, MISC)
        scales = [misc[0:5] + misc[5:10] for misc in miscs]

        def small(start, stop, scale):
            return [
                decode(misc[start:stop], row[scale : scale + 1])
                for misc, row in zip(miscs, scales)
            ]

        codes = both(0, rows)
        back, mixed = sides(left, [decode(code, row[0:1]) for code, row in zip(codes, scales)])
        codes = both(rows, half)
        upper, lower = sides(
            left_half, [decode(code, row[1:2]) for code, row in zip(codes, scales)]
        )
        filter_out[pl.ds(0, half), at] = upper
        filter_out[pl.ds(half, half), at] = lower
        ends = sides(left_lanes((8, LANES)), [misc[24:32] for misc in miscs])
        lefts, rights = sides(left_lanes((6, LANES)), small(12, 18, 3))
        taps = (lefts[0:3], rights[0:3], rights[3:6])
        lefts, rights = sides(left_lanes((6, LANES)), small(18, 24, 4))
        for offset in range(3):
            taps_out[0, offset : offset + 1, at] = lefts[offset : offset + 1]
            taps_out[1, offset : offset + 1, at] = rights[offset : offset + 1]
            taps_out[2, offset : offset + 1, at] = rights[3 + offset : 4 + offset]
        skip_out[0:1, at] = lefts[3:4]
        back_edge, mixed_edge = sides(left_lanes((2, LANES)), small(10, 12, 2))
        convs, edges = [], []
        for stream, (source, end, row) in enumerate(
            ((query_ref, ends[0], 0), (key_ref, ends[1], 0), (value_ref, ends[1], 2))
        ):
            now = source[:, at].astype(jnp.float32)
            before[stream, 6:8, :] = end[row : row + 2]
            before[stream, pl.ds(8, rows), :] = now
            before[stream, pl.ds(8 + rows, 2), :] = end[row + 4 : row + 6]
            conv = taps[stream][0:1] * now
            edge = taps[stream][0:1] * end[row + 4 : row + 6]
            for offset in (1, 2):
                weight = taps[stream][offset : offset + 1]
                conv = conv + weight * before[stream, pl.ds(8 - offset, rows), :]
                edge = edge + weight * before[stream, pl.ds(8 + rows - offset, 2), :]
            convs.append(conv)
            edges.append(edge)
        cotangent = cot_ref[:, at].astype(jnp.float32)
        cot_edge = ends[0][6:8]
        gated_out[:, at] = (convs[0] * mixed).astype(jnp.bfloat16)
        for stream, (out, grad, edge) in enumerate(
            (
                (query_out, cotangent * mixed, cot_edge * mixed_edge),
                (key_out, back * convs[2], back_edge * edges[2]),
                (value_out, back * convs[1], back_edge * edges[1]),
            )
        ):
            after[stream, pl.ds(0, rows), :] = grad
            after[stream, pl.ds(rows, 2), :] = edge
            total = taps[stream][0:1] * grad
            for offset in (1, 2):
                weight = taps[stream][offset : offset + 1]
                total = total + weight * after[stream, pl.ds(offset, rows), :]
            out[:, at] = total.astype(jnp.bfloat16)
        return 0

    loop(channels // LANES, one_tile, 0, len(in_refs) > 1)


def finish(received, streams, cotangent):
    rows, channels = cotangent.shape
    count = len(received)
    low = jax.ShapeDtypeStruct((rows, channels), jnp.bfloat16)

    def kernel(*refs):
        finish_kernel(refs[:count], *refs[count:])

    return pl.pallas_call(
        kernel,
        out_shape=(
            low,
            low,
            low,
            low,
            jax.ShapeDtypeStruct((rows, channels), jnp.float32),
            jax.ShapeDtypeStruct((3, 3, channels), jnp.float32),
            jax.ShapeDtypeStruct((1, channels), jnp.float32),
        ),
        scratch_shapes=[
            pltpu.VMEM((3, rows + 16, LANES), jnp.float32),
            pltpu.VMEM((3, rows + 8, LANES), jnp.float32),
        ],
        compiler_params=pltpu.CompilerParams(
            vmem_limit_bytes=3 * (channels // HALF) * MEBIBYTE // 2
        ),
    )(*in_order(received, BACK_ORDER), *streams, cotangent)


def operator_kernel(
    pieces, out_refs, forward_ref, inverse_ref, taps_ref,
    ends, starts, edged, first_ref, second_ref, fields, spectra, filters, rhs, rhs_back,
    shared, misc,
):
    in_refs = by_index(pieces, OUT_ORDER)
    blocks = fields.shape[0]
    place = lax.axis_index("seq")
    rows = forward_ref.shape[0] // 2
    half = blocks // 2
    half_rows = rows // 2
    unrolled = len(in_refs) > 1
    grad_scale = 1.0 / math.sqrt(blocks * rows)
    left = left_lanes((rows, LANES))
    left_half = left_lanes((half_rows, LANES))
    taps = taps_ref[...]
    query_taps = [taps[i : i + 1] for i in range(3)]
    value_taps = [taps[3 + i : 4 + i] for i in range(3)]
    gain = taps[6:7]
    nothing = jnp.zeros((8, LANES), jnp.float32)

    def lay(buffer, side, place, value):
        head, tail = head_tail(value)
        count = value.shape[0]
        at = pl.ds(side * LANES, LANES)
        rhs[buffer, pl.ds(place, count), at] = head
        rhs[buffer, pl.ds(rows + place, count), at] = tail
        rhs[buffer, pl.ds(2 * rows + place, count), at] = head

    def transformed(buffer):
        return jnp.dot(forward_ref[...], rhs[buffer], preferred_element_type=jnp.float32)

    def keep_ends(index, _):
        ref = piece(in_refs, index, place)
        block = index ^ place
        for stream in (0, 1):
            start = stream * rows
            last = ref[pl.ds(start + rows - 16, 16), :].astype(jnp.float32)
            first = ref[pl.ds(start, 16), :].astype(jnp.float32)
            ends[block + 1, 2 * stream : 2 * stream + 2, :] = last[14:16]
            ends[block + 1, 2 * stream + 4 : 2 * stream + 6, :] = first[0:2]
        return 0

    ends[0] = nothing
    ends[blocks + 1] = nothing
    loop(blocks, keep_ends, 0, unrolled)

    def transform(pair, _):
        spot = 2 * pair if unrolled else 0
        for side in range(2):
            ref = piece(in_refs, 2 * pair + side, place)
            scale = ref[pl.ds(2 * rows + half_rows, 16), :].astype(jnp.float32)
            code = ref[pl.ds(2 * rows, half_rows), :].astype(jnp.float32)
            taken = decode(code, scale[0:1] + scale[8:9])
            turned = swap(taken)
            lay(spot, side, 0, jnp.where(left_half, taken, turned))
            lay(spot, side, half_rows, jnp.where(left_half, turned, taken))
        result = transformed(spot)
        for side in range(2):
            filters[(2 * pair + side) ^ place] = result[:, side * LANES : (side + 1) * LANES]
        for side in range(2):
            index = 2 * pair + side
            ref = piece(in_refs, index, place)
            outs = []
            for stream, weights in ((0, query_taps), (1, value_taps)):
                now = ref[pl.ds(stream * rows, rows), :].astype(jnp.float32)
                last = ends[index ^ place, 2 * stream : 2 * stream + 2, :]
                edged[index, stream, 6:8, :] = last
                edged[index, stream, pl.ds(8, rows), :] = now
                total = weights[0] * now
                for offset in (1, 2):
                    shifted = edged[index, stream, pl.ds(8 - offset, rows), :]
                    total = total + weights[offset] * shifted
                outs.append(total)
            first_ref[index] = outs[0]
            second_ref[index] = outs[1]
            field = outs[0] * outs[1]
            fields[index] = field
            lay(spot + 1, side, 0, field)
        result = transformed(spot + 1)
        for side in range(2):
            spectra[(2 * pair + side) ^ place] = result[:, side * LANES : (side + 1) * LANES]
        return 0

    loop(half, transform, 0, unrolled)

    chunk = 8
    left_chunk = left_lanes((chunk, LANES))
    conjugate = jnp.where(left_chunk, -1.0, 1.0)

    def products(pairs):
        one = two = three = None
        for (re, im, both), (join_re, join_less, join_more) in pairs:
            terms = join_re * both, re * join_less, im * join_more
            if one is None:
                one, two, three = terms
            else:
                one, two, three = one + terms[0], two + terms[1], three + terms[2]
        return one - three, one + two

    def spectral(step, sign):
        real_at = pl.ds(pl.multiple_of(step * chunk, chunk), chunk)
        imag_at = pl.ds(pl.multiple_of(rows + step * chunk, chunk), chunk)
        field_re = [spectra[block, real_at, :] for block in range(blocks)]
        field_im = [spectra[block, imag_at, :] for block in range(blocks)]

        def joined(re, im, block):
            if block == 0:
                return re[0], im[0]
            if sign > 0:
                return re[block] - im[block - 1], im[block] + re[block - 1]
            return re[block] + im[block - 1], im[block] - re[block - 1]

        turned = []
        for block in range(blocks):
            re = jnp.where(left_chunk, field_re[blocks - 1 - block], field_re[block])
            im = jnp.where(left_chunk, field_im[blocks - 1 - block], field_im[block])
            turned.append((re, im, re + im))
        filt_re = [filters[block, real_at, :] for block in range(blocks)]
        filt_im = [filters[block, imag_at, :] for block in range(blocks)]
        joins = []
        for block in range(blocks):
            re, im = joined(filt_re, filt_im, block)
            im = im * conjugate
            joins.append((re, im - re, re + im))
        outs = [
            products([(turned[block - lag], joins[lag]) for lag in range(block + 1)])
            for block in range(blocks)
        ]
        grads = []
        for block in range(blocks):
            re = jnp.where(left_chunk, field_re[block], swap(field_re[block]))
            im = jnp.where(left_chunk, field_im[block], swap(field_im[block]))
            grads.append((re, im, re + im))
        sums = [joined(field_re, field_im, block) for block in range(blocks)]
        joins = []
        for block in range(blocks):
            parts = []
            for part in range(2):
                far = sums[block - half][part] if block >= half else 0.0
                parts.append(jnp.where(left_chunk, swap(sums[block][part]), far))
            re, im = parts
            joins.append((re, -im - re, re - im))
        for block in range(blocks):
            for part, at in ((0, real_at), (1, imag_at)):
                spectra[block, at, :] = jnp.where(
                    left_chunk, outs[blocks - 1 - block][part], outs[block][part]
                )
        for lag in range(half):
            out = products([(grads[block], joins[block - lag]) for block in range(lag, blocks)])
            filters[lag, real_at, :] = out[0]
            filters[lag, imag_at, :] = out[1]

    trips = rows // chunk // 4

    def even(trip, _):
        for part in range(2):
            spectral(2 * trip + part, 1)
        return 0

    def odd(trip, _):
        for part in range(2):
            spectral(2 * trip + part, -1)
        return 0

    lax.fori_loop(0, trips, even, 0)
    lax.fori_loop(trips, 2 * trips, odd, 0)

    def back(values, buffer):
        for side, value in enumerate(values):
            head, tail = head_tail(value)
            at = pl.ds(side * LANES, LANES)
            rhs_back[buffer, pl.ds(0, 2 * rows), at] = head
            rhs_back[buffer, pl.ds(2 * rows, 2 * rows), at] = tail
            rhs_back[buffer, pl.ds(4 * rows, 2 * rows), at] = head
        result = jnp.dot(inverse_ref[...], rhs_back[buffer], preferred_element_type=jnp.float32)
        return result[:, :LANES], result[:, LANES:]

    def filter_grads(pair, _):
        values = filters[2 * pair], filters[2 * pair + 1]
        for side, value in enumerate(back(values, pair if unrolled else 0)):
            filters[2 * pair + side, pl.ds(0, rows), :] = value * grad_scale
        return 0

    loop(half // 2, filter_grads, 0, unrolled)

    def fold(value):
        return jnp.sum(value.reshape(rows // 8, 8, LANES), axis=0)

    def outputs(pair, totals):
        values = [spectra[(2 * pair + side) ^ place] for side in range(2)]
        results = back(values, (half // 2 + pair) if unrolled else 0)
        for side, result in enumerate(results):
            index = 2 * pair + side
            block = index ^ place
            out_ref = piece(out_refs, index, place)
            field = fields[index]
            result = result + gain * field
            scale = scale_of(result)
            out_ref[pl.ds(0, rows), :] = encode(result, scale).astype(jnp.bfloat16)
            misc[index, 0:1, :] = scale
            starts[block] = result[:8]
            turned = swap(result)
            grads = (second_ref[index] * turned, first_ref[index] * turned)
            new_totals = []
            for stream in (0, 1):
                for offset in range(3):
                    earlier = edged[index, stream, pl.ds(8 - offset, rows), :]
                    total = totals[3 * stream + offset]
                    new_totals.append(total + fold(grads[stream] * earlier))
            totals = tuple(new_totals)

            upper_half = block // half
            value = filters[lax.rem(block, half), pl.ds(0, rows), :]
            halves = join(left_half, value[:half_rows], value[half_rows:], upper_half)
            scale = scale_of(halves)
            code = encode(halves, scale).astype(jnp.bfloat16)
            out_ref[pl.ds(rows, half_rows), :] = code
            misc[index, 1:2, :] = scale
        return totals

    starts[blocks] = nothing
    totals = loop(half, outputs, (nothing,) * 6, unrolled)
    sums = [grad_scale * jnp.sum(total, axis=0, keepdims=True) for total in totals]
    shared[0:6, :] = taps[0:6]
    for row in range(6):
        value = sums[row]
        if row == 3:
            value = jnp.where(left_lanes((1, LANES)), filters[0, 0:1, :], value)
        shared[6 + row : 7 + row, :] = value
    tap_rows, sum_rows = shared[0:6, :], shared[6:12, :]
    tap_scale, sum_scale = scale_of(tap_rows), scale_of(sum_rows)
    tap_codes, sum_codes = encode(tap_rows, tap_scale), encode(sum_rows, sum_scale)

    def close(index, _):
        out_ref = piece(out_refs, index, place)
        block = index ^ place
        edge = starts[block + 1, 0:2, :]
        scale = scale_of(edge)
        misc[index, 2:3, :] = scale
        misc[index, 3:4, :] = tap_scale
        misc[index, 4:5, :] = sum_scale
        scales = misc[index, 0:5, :]
        misc[index, 5:10, :] = scales - scales.astype(jnp.bfloat16).astype(jnp.float32)
        misc[index, 10:12, :] = encode(edge, scale)
        misc[index, 12:18, :] = tap_codes
        misc[index, 18:24, :] = sum_codes
        misc[index, 24:28, :] = ends[block, 0:4, :]
        misc[index, 28:32, :] = ends[block + 2, 4:8, :]
        out_ref[pl.ds(rows + half_rows, MISC), :] = misc[index].astype(jnp.bfloat16)
        return 0

    loop(blocks, close, 0, unrolled)


def operator(taps, received, devices):
    count = len(received)
    blocks = devices
    rows = (received[0].shape[-2] - 16) * 2 // 5
    forward, inverse = transform_matrices(rows)
    wide = (blocks, rows, LANES)
    listed = count > 1

    def kernel(*refs):
        ins, (forward_ref, inverse_ref, taps_ref) = refs[:count], refs[count : count + 3]
        outs, scratch = refs[count + 3 : 2 * count + 3], refs[2 * count + 3 :]
        operator_kernel(ins, outs, forward_ref, inverse_ref, taps_ref, *scratch)

    return pl.pallas_call(
        kernel,
        out_shape=piece_shapes(devices, rows + rows // 2 + MISC),
        scratch_shapes=[
            pltpu.VMEM((blocks + 2, 8, LANES), jnp.float32),
            pltpu.VMEM((blocks + 1, 8, LANES), jnp.float32),
            pltpu.VMEM((blocks, 2, rows + 8, LANES), jnp.float32),
            pltpu.VMEM(wide, jnp.float32),
            pltpu.VMEM(wide, jnp.float32),
            pltpu.VMEM(wide, jnp.float32),
            pltpu.VMEM((blocks, 2 * rows, LANES), jnp.float32),
            pltpu.VMEM((blocks, 2 * rows, LANES), jnp.float32),
            pltpu.VMEM((blocks if listed else 2, 3 * rows, 2 * LANES), jnp.bfloat16),
            pltpu.VMEM((3 * blocks // 4 if listed else 1, 6 * rows, 2 * LANES), jnp.bfloat16),
            pltpu.VMEM((16, LANES), jnp.float32),
            pltpu.VMEM((blocks, MISC, LANES), jnp.float32),
        ],
        compiler_params=pltpu.CompilerParams(
            vmem_limit_bytes=min(4 * blocks * MEBIBYTE, VMEM_BYTES)
        ),
    )(*in_order(received, OUT_ORDER), jnp.asarray(forward), jnp.asarray(inverse), taps)


def own_taps(short_taps, skip_gain, received):
    places = lax.axis_size("seq")
    columns = lax.axis_size("chan")
    share = skip_gain.shape[0]

    def pair(one, two):
        fill = ((0, 0), (0, HALF - share))
        return jnp.concatenate([jnp.pad(one, fill), jnp.pad(two, fill)], axis=1)

    straight = jnp.concatenate([jnp.ones((1, share)), jnp.zeros((2, share))]).astype(jnp.float32)
    rows = jnp.concatenate(
        [
            pair(short_taps[0], short_taps[1]),
            pair(straight, short_taps[2]),
            pair(skip_gain[None], skip_gain[None]),
            jnp.zeros((1, LANES), jnp.float32),
        ]
    )
    route = [
        (flat, (flat % places) * columns + flat // places) for flat in range(places * columns)
    ]
    if len(received) > 1:
        unit = jnp.ones((1, 1), jnp.bfloat16)
        rows, unit, received[-1] = lax.optimization_barrier((rows, unit, received[-1]))
        received[0] = received[0] * unit
    return lax.ppermute(rows, ("seq", "chan"), route), received


def spread(value, devices):
    rows, channels = value.shape
    share = channels // devices
    if share == HALF:
        return value
    wide = jnp.pad(value.reshape(rows, devices, share), ((0, 0), (0, 0), (0, HALF - share)))
    return wide.reshape(rows, devices * HALF)


def gathered(value, share):
    if share == HALF:
        return value
    groups = value.reshape(*value.shape[:-1], value.shape[-1] // HALF, HALF)[..., :share]
    return groups.reshape(*value.shape[:-1], -1)


def per_device(query_rows, key_rows, value_rows, long_filter, short_taps, skip_gain, cotangent):
    devices = lax.axis_size("seq")
    share = query_rows.shape[1] // devices
    streams = [spread(value, devices) for value in (query_rows, key_rows, value_rows)]
    upstream = spread(cotangent, devices)
    received = exchange(pack(streams, upstream, spread(long_filter, devices), devices))
    taps, received = own_taps(short_taps, skip_gain, received)
    results = exchange(operator(taps, received, devices))
    outs = finish(results, streams, upstream)
    *outs, skip_grad = (gathered(value, share) for value in outs)
    return (*outs, skip_grad[0])


def solution(mesh):
    in_specs = (
        P("seq", "chan"),
        P("seq", "chan"),
        P("seq", "chan"),
        P("seq", "chan"),
        P(None, None, ("seq", "chan")),
        P(("seq", "chan")),
        P("seq", "chan"),
    )
    out_specs = (
        P("seq", "chan"),
        P("seq", "chan"),
        P("seq", "chan"),
        P("seq", "chan"),
        P("seq", "chan"),
        P(None, None, "chan"),
        P("chan"),
    )
    return jax.shard_map(
        per_device, mesh=mesh, in_specs=in_specs, out_specs=out_specs, check_vma=False
    )
```
